32 devices in a mesh: dp: 2 (over x), head: 16 (over z, y, core).
Axes of the slice: x: 2, y: 2, z: 4, core: 2. Of those that a mesh axis runs over, the one named last changes fastest.
Arguments:
- tokens: bfloat16 [8192, 1024], P(('dp', 'head')), may hold values from -6 to 6
- lengths: int32 [2, 4], P('dp'), may hold values from 1 to 4, 8 in all within a row
- w_query: bfloat16 [1024, 1024], P(None, 'head'), may hold values from -0.1875 to 0.1875
- w_key: bfloat16 [1024, 1024], P(None, 'head'), may hold values from -0.1875 to 0.1875
- w_value: bfloat16 [1024, 1024], P(None, 'head'), may hold values from -0.1875 to 0.1875
- s_qk: float32 [1024], P('head'), may hold values from 0.8 to 1.6
- w_out: bfloat16 [1024, 1024], P('head'), may hold values from -0.1875 to 0.1875
- up_weight: bfloat16 [4096, 1024], P(('dp', 'head')), may hold values from -0.1875 to 0.1875
- gate_weight: bfloat16 [4096, 1024], P(('dp', 'head')), may hold values from -0.1875 to 0.1875
- down_weight: bfloat16 [4096, 1024], P(('dp', 'head')), may hold values from -0.09375 to 0.09375
- s_up: bfloat16 [4096], P(('dp', 'head')), may hold values from 0.5 to 1.5
- s_gate: bfloat16 [4096], P(('dp', 'head')), may hold values from 0.5 to 1.5
- alpha_attn: float32 [1024], replicated, may hold values from 0.1 to 0.9
- alpha_mlp: float32 [1024], replicated, may hold values from 0.1 to 0.9
- cotangent: bfloat16 [8192, 1024], P(('dp', 'head')), may hold values from -6 to 6
Outputs:
- mixed: bfloat16 [8192, 1024], P(('dp', 'head'))
- tokens_grad: bfloat16 [8192, 1024], P(('dp', 'head'))
- w_query_grad: float32 [1024, 1024], P(None, 'head')
- w_key_grad: float32 [1024, 1024], P(None, 'head')
- w_value_grad: float32 [1024, 1024], P(None, 'head')
- s_qk_grad: float32 [1024], P('head')
- w_out_grad: float32 [1024, 1024], P('head')
- up_grad: float32 [4096, 1024], P(('dp', 'head'))
- gate_grad: float32 [4096, 1024], P(('dp', 'head'))
- down_grad: float32 [4096, 1024], P(('dp', 'head'))
- s_up_grad: float32 [4096], P(('dp', 'head'))
- s_gate_grad: float32 [4096], P(('dp', 'head'))
- alpha_attn_grad: float32 [1024], replicated
- alpha_mlp_grad: float32 [1024], replicated
The draws below stay inside these ranges and needn't reach their ends.
Inputs may be any that keep to these rules, and one draw needn't show every extreme that they name: Row g gives, in blocks of 512 tokens, the lengths of the 4 sequences that fill the g-th group of 4096 tokens in order; each row sums to 8 and its largest entry is 4.
All inputs are finite; a program needn't handle non-finite values.
Results may differ from the reference program's by a relative error of at most 0.02.
Values may be sent and summed in bfloat16 or wider, within the bound.
A program may use at most 192 MiB of HBM per device.

```python
import math
import jax
import jax.numpy as jnp
import numpy as np
from jax import lax

D = 1024
HEADS = 16
HEAD_DIM = 64
FF = 4096
BLOCK = 512
TOK_GROUP = 4096
TOKENS = 8192
MAXLEN = 2048
UNITS = 8
DOCS = 4
N_DP = 2


def block_levels(key, shape, pieces, smallest, high):
    loudness = 1.0
    for position, shards_of in pieces:
        heights = jax.random.uniform(jax.random.fold_in(jax.random.fold_in(key, 6), position), (shards_of,), jnp.float32, smallest / len(pieces), high / len(pieces))
        loudness = loudness * jnp.repeat(jnp.exp(heights), shape[position] // shards_of).reshape((-1,) + (1,) * (len(shape) - 1 - position))
    return loudness


def split_up(amount, total, bound, slope):
    portions = [(1 << 20) // math.isqrt(standing ** slope) + 1 for standing in range(2, amount + 1)]
    spare, holding = total - bound - (amount - 1), [1] * (amount - 1)
    while spare > 0:
        movable = [i for i in range(amount - 1) if holding[i] < bound]
        pool, budget = sum([portions[i] for i in movable]), spare
        for i in movable:
            addition = min(bound - holding[i], max(1, budget * portions[i] // pool), spare)
            holding[i] = holding[i] + addition
            spare = spare - addition
    return np.array([bound] + holding)


def ragged_sizes(own_key, count, total, bound, skew):
    if count == 2:
        one = jax.random.randint(own_key, (), max(1, total - bound), min(bound, total - 1) + 1)
        return jnp.stack([one, total - one])
    sizes = jnp.asarray(split_up(count, total, bound, skew), jnp.int32)
    couples = (count - 1) // 2
    giver, receiver = sizes[1:1 + 2 * couples:2], sizes[2:2 + 2 * couples:2]
    slack = jnp.minimum(giver - 1, bound - receiver)
    moved = jax.random.randint(jax.random.fold_in(own_key, 1), (couples,), 0, 1 << 20) % (slack + 1)
    sizes = sizes.at[1:1 + 2 * couples:2].set(giver - moved).at[2:2 + 2 * couples:2].set(receiver + moved)
    return sizes[jax.random.permutation(jax.random.fold_in(own_key, 2), count)]


def normal_values(rng, shape, scale, bound, split=(), held_as=jnp.bfloat16):
    loudness = block_levels(rng, shape, split, -0.22, 0.18) if split else 1.0
    values = jax.random.normal(rng, shape, jnp.float32) * scale * loudness
    return jnp.minimum(jnp.maximum(values, -bound), bound).astype(held_as)


def setup_inputs(seed: int = 0) -> dict:
    arg_keys = jax.random.split(jax.random.key(seed), 16)
    return {
        "tokens": normal_values(arg_keys[0], (TOKENS, D), 1.0, 6.0, ((0, 32),)),
        "lengths": jax.vmap(lambda own: ragged_sizes(own, DOCS, UNITS, MAXLEN // BLOCK, 1))(jax.random.split(arg_keys[1], N_DP)).reshape((N_DP, DOCS)).astype(jnp.int32),
        "w_query": normal_values(arg_keys[2], (D, D), D ** -0.5, 0.1875, ((1, 16),)),
        "w_key": normal_values(arg_keys[3], (D, D), D ** -0.5, 0.1875, ((1, 16),)),
        "w_value": normal_values(arg_keys[4], (D, D), D ** -0.5, 0.1875, ((1, 16),)),
        "s_qk": jnp.clip(0.8 + 0.8 * jax.random.uniform(arg_keys[5], (D,), jnp.float32) ** block_levels(arg_keys[5], (D,), ((0, 16),), -0.2, 0.2), 0.8, 1.6),
        "w_out": normal_values(arg_keys[6], (D, D), D ** -0.5, 0.1875, ((0, 16),)),
        "up_weight": normal_values(arg_keys[7], (FF, D), D ** -0.5, 0.1875, ((0, 32),)),
        "gate_weight": normal_values(arg_keys[8], (FF, D), D ** -0.5, 0.1875, ((0, 32),)),
        "down_weight": normal_values(arg_keys[9], (FF, D), FF ** -0.5, 0.09375, ((0, 32),)),
        "s_up": jnp.clip(0.5 + 1.0 * jax.random.uniform(arg_keys[10], (FF,), jnp.float32) ** block_levels(arg_keys[10], (FF,), ((0, 32),), -0.2, 0.2), 0.5, 1.5).astype(jnp.bfloat16),
        "s_gate": jnp.clip(0.5 + 1.0 * jax.random.uniform(arg_keys[11], (FF,), jnp.float32) ** block_levels(arg_keys[11], (FF,), ((0, 32),), -0.2, 0.2), 0.5, 1.5).astype(jnp.bfloat16),
        "alpha_attn": jnp.clip(jax.random.uniform(arg_keys[12], (D,), jnp.float32, 0.1, 0.9), 0.1, 0.9),
        "alpha_mlp": jnp.clip(jax.random.uniform(arg_keys[13], (D,), jnp.float32, 0.1, 0.9), 0.1, 0.9),
        "cotangent": normal_values(arg_keys[14], (TOKENS, D), 1.0, 6.0, ((0, 32),)),
    }


epsilon = 1e-06
precise = lax.Precision.HIGHEST

@jax.custom_vjp
def low(v):
    return lax.optimization_barrier(v.astype(jnp.bfloat16)).astype(jnp.float32)

@jax.custom_vjp
def low_back(v):
    return v

def low_keep(v):
    return (low(v), None)

def low_pass(kept, grad):
    return (grad,)

def back_keep(v):
    return (v, None)

def back_low(kept, grad):
    return (low(grad),)
low.defvjp(low_keep, low_pass)
low_back.defvjp(back_keep, back_low)

def sphere(values):
    return values * lax.rsqrt(lax.optimization_barrier(jnp.mean(values * values, axis=-1, keepdims=True)) + epsilon)

def matmul(left, right):
    return jnp.dot(left, right, precision=precise, preferred_element_type=jnp.float32)

def layout(lengths_row, group_rows):
    lengths_row = lengths_row.astype(jnp.int32)
    ends = (jnp.cumsum(lengths_row) * BLOCK).astype(jnp.int32)
    starts = (ends - lengths_row * BLOCK).astype(jnp.int32)
    row_index = jnp.arange(group_rows, dtype=jnp.int32)
    seq_index = lax.optimization_barrier(jnp.sum((row_index[:, None] >= ends[None, :]).astype(jnp.int32), axis=1)).astype(jnp.int32)
    member = seq_index[:, None] == jnp.arange(lengths_row.shape[0], dtype=jnp.int32)[None, :]
    first_row = lax.optimization_barrier(jnp.sum(jnp.where(member, starts[None, :], 0), axis=1)).astype(jnp.int32)
    return (seq_index, (row_index - first_row).astype(jnp.int32))

def rotation_angles(places):
    half_dim = HEAD_DIM // 2
    frequency = jnp.exp(jnp.arange(half_dim, dtype=jnp.float32) * (-2.0 * math.log(10000.0) / HEAD_DIM))
    return places.astype(jnp.float32)[:, None] * frequency[None, :]

def rotate(heads, angles):
    half_dim = heads.shape[-1] // 2
    cosine = jnp.cos(angles)[:, None, :]
    sine_part = jnp.sin(angles)[:, None, :]
    first_half = heads[..., :half_dim]
    second_half = heads[..., half_dim:]
    return jnp.concatenate([first_half * cosine - second_half * sine_part, second_half * cosine + first_half * sine_part], axis=-1)

def head_features(projected, head_gain, angles):
    count_rows = projected.shape[0]
    heads = projected.reshape(count_rows, -1, HEAD_DIM)
    heads = sphere(rotate(heads, angles)) * head_gain.reshape(-1, HEAD_DIM)[None, :, :]
    return heads.reshape(count_rows, -1)

def attention(query_unit, key_unit, value_proj, seq_ids):
    root = math.sqrt(HEAD_DIM)
    query_groups = query_unit.reshape(N_DP, TOK_GROUP, HEADS, HEAD_DIM)
    key_groups = key_unit.reshape(N_DP, TOK_GROUP, HEADS, HEAD_DIM)
    value_groups = value_proj.reshape(N_DP, TOK_GROUP, HEADS, HEAD_DIM)

    def one_block(block_id):
        group_id = block_id // UNITS
        block_index = block_id % UNITS
        query_group = lax.dynamic_index_in_dim(query_groups, group_id, 0, keepdims=False)
        key_group = lax.dynamic_index_in_dim(key_groups, group_id, 0, keepdims=False)
        value_group = lax.dynamic_index_in_dim(value_groups, group_id, 0, keepdims=False)
        seq_group = lax.dynamic_index_in_dim(seq_ids, group_id, 0, keepdims=False)
        key_start = jnp.maximum((block_index + 1) * BLOCK - MAXLEN, 0).astype(jnp.int32)
        query_rows = lax.dynamic_slice_in_dim(query_group, (block_index * BLOCK).astype(jnp.int32), BLOCK, 0)
        key_rows = lax.dynamic_slice_in_dim(key_group, key_start, MAXLEN, 0)
        value_rows = lax.dynamic_slice_in_dim(value_group, key_start, MAXLEN, 0)
        query_seq = lax.dynamic_slice_in_dim(seq_group, (block_index * BLOCK).astype(jnp.int32), BLOCK, 0)
        key_seq = lax.dynamic_slice_in_dim(seq_group, key_start, MAXLEN, 0)
        query_row = block_index * BLOCK + jnp.arange(BLOCK, dtype=jnp.int32)
        key_row = key_start + jnp.arange(MAXLEN, dtype=jnp.int32)
        allowed = (query_seq[:, None] == key_seq[None, :]) & (key_row[None, :] <= query_row[:, None])
        scores = jnp.einsum('qhd,khd->hqk', query_rows, key_rows, precision=precise) / root
        scores = low_back(scores)
        scores = jnp.where(allowed[None, :, :], scores, -1e+30)
        highest = lax.optimization_barrier(jnp.max(scores, axis=-1, keepdims=True))
        shifted = jnp.exp(scores - highest)
        weights = shifted / lax.optimization_barrier(jnp.sum(shifted, axis=-1, keepdims=True))
        return jnp.einsum('hqk,khd->qhd', low(weights), value_rows, precision=precise)
    outputs = lax.map(jax.checkpoint(one_block), jnp.arange(N_DP * UNITS, dtype=jnp.int32))
    return outputs.reshape(TOKENS, D)

def forward(tokens, w_query, w_key, w_value, s_qk, w_out, up_weight, gate_weight, down_weight, s_up, s_gate, alpha_attn, alpha_mlp, seq_ids, angles):
    queries = low_back(matmul(tokens, w_query))
    keys = low_back(matmul(tokens, w_key))
    value_proj = low(low_back(matmul(tokens, w_value)))
    query_unit = low(head_features(queries, s_qk, angles))
    key_unit = low(head_features(keys, s_qk, angles))
    attended = low(low_back(attention(query_unit, key_unit, value_proj, seq_ids)))
    branch = low_back(matmul(attended, w_out))
    hidden = sphere(tokens + alpha_attn * (sphere(branch) - tokens))
    hidden_low = low(hidden)
    up_proj = low_back(matmul(hidden_low, up_weight.T))
    gate_proj = low_back(matmul(hidden_low, gate_weight.T))
    gated = gate_proj * s_gate
    inner = low(up_proj * s_up * (gated * jax.nn.sigmoid(gated)))
    mlp_out = low_back(matmul(inner, down_weight))
    return sphere(hidden + alpha_mlp * (sphere(mlp_out) - hidden))

def reference(tokens, lengths, w_query, w_key, w_value, s_qk, w_out, up_weight, gate_weight, down_weight, s_up, s_gate, alpha_attn, alpha_mlp, cotangent):
    seq_ids, places = jax.vmap(lambda row: layout(row, TOK_GROUP))(lengths)
    angles = rotation_angles(places.reshape(-1))
    floats = tuple((array.astype(jnp.float32) for array in (tokens, w_query, w_key, w_value, s_qk, w_out, up_weight, gate_weight, down_weight, s_up, s_gate, alpha_attn, alpha_mlp)))
    mixed, pullback = jax.vjp(lambda *inputs: forward(*inputs, seq_ids, angles), *floats)
    grads = pullback(cotangent.astype(jnp.float32))
    return (mixed.astype(jnp.bfloat16), grads[0].astype(jnp.bfloat16), grads[1], grads[2], grads[3], grads[4], grads[5], grads[6], grads[7], grads[8], grads[9], grads[10], grads[11], grads[12])
```

```python
import math

import jax
import jax.numpy as jnp
from jax import lax
from jax.experimental import pallas as pl
from jax.experimental.pallas import tpu as pltpu
from jax.sharding import Mesh
from jax.sharding import PartitionSpec as P

HEAD_DIM = 64
BLOCK = 512
EPSILON = 1e-06
ROOT = math.sqrt(HEAD_DIM)
SCORE_SCALE = math.log2(math.e) / ROOT
AXES = ("o", "x", "z", "y", "c")
GROUP = ("z", "y", "c")
PLANE = ("x", "y", "c")
OWNERS = ("o", "z")
f32, bf16 = jnp.float32, jnp.bfloat16
VMEM_LIMIT = 56 * 2**20


def dot(left, right, left_dim, right_dim):
    return lax.dot_general(
        left, right, (((left_dim,), (right_dim,)), ((), ())), preferred_element_type=f32
    )


def unit_start(lengths, unit):
    start, end = jnp.int32(0), jnp.int32(0)
    for j in range(lengths.shape[1]):
        end = end + lengths[0, j]
        start = jnp.where(unit >= end, end, start)
    return start


def causal(weights):
    key = lax.broadcasted_iota(jnp.int32, weights.shape, 0)
    query = lax.broadcasted_iota(jnp.int32, weights.shape, 1)
    return jnp.where(key <= query, weights, 0.0)


def block_columns(index):
    return pl.ds(pl.multiple_of(index * BLOCK, BLOCK), BLOCK)


def attention_forward_kernel(lengths, qt, kt, vt, ot, lse):
    def unit(u, _):
        columns = block_columns(u)
        query = qt[:, columns]

        def part(j, carry, diagonal):
            total, attended = carry
            keys = block_columns(j)
            weights = jnp.exp2(dot(kt[:, keys], query, 0, 0) * SCORE_SCALE)
            if diagonal:
                weights = causal(weights)
            total = total + jnp.sum(weights, axis=0, keepdims=True)
            attended = attended + dot(vt[:, keys], weights.astype(bf16), 1, 0)
            return total, attended

        carry = (jnp.zeros((1, BLOCK), f32), jnp.zeros((HEAD_DIM, BLOCK), f32))
        carry = lax.fori_loop(unit_start(lengths, u), u, lambda j, c: part(j, c, False), carry)
        total, attended = part(u, carry, True)
        ot[:, columns] = (attended * (1.0 / total)).astype(bf16)
        lse[:, columns] = jnp.log2(total)
        return 0

    lax.fori_loop(0, qt.shape[1] // BLOCK, unit, 0)


def attention_backward_kernel(lengths, qt, kt, vt, ot, got, lse, gqt, gkt, gvt):
    def unit(u, _):
        columns = block_columns(u)
        query, grad, log_total = qt[:, columns], got[:, columns], lse[:, columns]
        inner = jnp.sum(grad.astype(f32) * ot[:, columns].astype(f32), axis=0, keepdims=True)

        def part(j, query_grad, diagonal):
            keys = block_columns(j)
            key, value = kt[:, keys], vt[:, keys]
            weights = jnp.exp2(dot(key, query, 0, 0) * SCORE_SCALE - log_total)
            if diagonal:
                weights = causal(weights)
            weight_grad = dot(value, grad, 0, 0)
            score_grad = (weights * (weight_grad - inner)).astype(bf16)
            key_part = dot(query, score_grad, 1, 1)
            value_part = dot(grad, weights.astype(bf16), 1, 1)
            if diagonal:
                gkt[:, keys] = key_part
                gvt[:, keys] = value_part
            else:
                gkt[:, keys] += key_part
                gvt[:, keys] += value_part
            return query_grad + dot(key, score_grad, 1, 0)

        query_grad = part(u, jnp.zeros((HEAD_DIM, BLOCK), f32), True)
        gqt[:, columns] = lax.fori_loop(
            unit_start(lengths, u), u, lambda j, c: part(j, c, False), query_grad
        )
        return 0

    lax.fori_loop(0, qt.shape[1] // BLOCK, unit, 0)


def attention_call(kernel, name, outs, lengths, *operands):
    vmem = pl.BlockSpec(memory_space=pltpu.VMEM)
    return pl.pallas_call(
        kernel,
        name=name,
        out_shape=outs,
        in_specs=[pl.BlockSpec(memory_space=pltpu.SMEM)] + [vmem] * len(operands),
        out_specs=tuple(vmem for _ in outs),
        compiler_params=pltpu.CompilerParams(vmem_limit_bytes=VMEM_LIMIT),
    )(lengths, *operands)


def attention_forward(lengths, qt, kt, vt):
    rows = qt.shape[1]
    outs = (jax.ShapeDtypeStruct((HEAD_DIM, rows), bf16), jax.ShapeDtypeStruct((1, rows), f32))
    return attention_call(attention_forward_kernel, "attn_forward", outs, lengths, qt, kt, vt)


def attention_backward(lengths, *operands):
    outs = (jax.ShapeDtypeStruct(operands[0].shape, f32),) * 3
    return attention_call(attention_backward_kernel, "attn_backward", outs, lengths, *operands)


def sphere(values):
    return values * lax.rsqrt(jnp.mean(values * values, axis=-1, keepdims=True) + EPSILON)


def turn_table(lengths_row, rows):
    ends = jnp.sum(jnp.where(jnp.tri(lengths_row.shape[0], dtype=bool), lengths_row[None, :], 0), 1)
    row = jnp.arange(rows, dtype=jnp.int32)
    passed = (row // BLOCK)[None, :] >= ends[:, None]
    place = row - BLOCK * jnp.max(jnp.where(passed, ends[:, None], 0), axis=0)
    half = HEAD_DIM // 2
    frequency = jnp.exp(jnp.arange(half, dtype=f32) * (-2.0 * math.log(10000.0) / HEAD_DIM))
    angle = place.astype(f32)[None, :] * frequency[:, None]
    return jnp.cos(angle), jnp.sin(angle)


def turn(values, cosine, sine):
    half = HEAD_DIM // 2
    a, b = values[:half], values[half:]
    return jnp.concatenate([a * cosine - b * sine, b * cosine + a * sine], axis=0)


def unit_features(turned):
    scale = lax.rsqrt(jnp.mean(turned * turned, axis=0, keepdims=True) + EPSILON)
    return turned * scale, scale


def features_back(turned, gain, grad, cosine, sine):
    normal, scale = unit_features(turned)
    gain_grad = jnp.sum(grad * normal, axis=1)
    grad = grad * gain[:, None]
    grad = scale * (grad - normal * jnp.mean(grad * normal, axis=0, keepdims=True))
    return turn(grad, cosine, -sine), gain_grad


def front(branch, own_tokens, alpha):
    return sphere(own_tokens + alpha * (sphere(branch) - own_tokens))


def core(up_proj, gate_proj, up_scale, gate_scale):
    gated = gate_proj * gate_scale
    return up_proj * up_scale * (gated * jax.nn.sigmoid(gated))


def gather(values, axes):
    return lax.all_gather(values, axes, axis=0, tiled=True)


def scatter_sum(values, axes):
    return lax.psum_scatter(values, axes, scatter_dimension=0, tiled=True)


def shards(
    tokens, lengths, w_query, w_key, w_value, s_qk, w_out, up_weight, gate_weight, down_weight,
    s_up, s_gate, alpha_attn, alpha_mlp, cotangent,
):
    units = up_weight.shape[0]
    mlp_weight = gather(jnp.stack([up_weight, gate_weight, down_weight])[None], OWNERS)
    mlp_scale = gather(jnp.stack([s_up, s_gate])[None], OWNERS).astype(f32)
    owners = mlp_weight.shape[0]
    up_full, gate_full, down_full = (
        mlp_weight[:, i].reshape(owners * units, -1) for i in range(3)
    )
    up_scale, gate_scale = (mlp_scale[:, i].reshape(1, owners * units) for i in range(2))

    group_tokens = gather(tokens, GROUP)
    rows = group_tokens.shape[0]
    cosine, sine = turn_table(lengths[0], rows)
    joint = jnp.concatenate([w_query, w_key, w_value], axis=1)
    projected = dot(joint, group_tokens, 0, 1)
    gain = s_qk[:, None]
    turned_q = turn(projected[:HEAD_DIM], cosine, sine)
    turned_k = turn(projected[HEAD_DIM : 2 * HEAD_DIM], cosine, sine)
    qt = (unit_features(turned_q)[0] * gain).astype(bf16)
    kt = (unit_features(turned_k)[0] * gain).astype(bf16)
    vt = projected[2 * HEAD_DIM :].astype(bf16)
    ot, lse = attention_forward(lengths, qt, kt, vt)
    branch = scatter_sum(dot(ot, w_out, 0, 0).astype(bf16), GROUP).astype(f32)

    hidden, front_pull = jax.vjp(front, branch, tokens.astype(f32), alpha_attn)
    hidden_low = gather(hidden.astype(bf16), PLANE)
    up_proj = dot(hidden_low, up_full, 1, 1)
    gate_proj = dot(hidden_low, gate_full, 1, 1)
    inner, core_pull = jax.vjp(core, up_proj, gate_proj, up_scale, gate_scale)
    inner_low = inner.astype(bf16)
    mlp_out = scatter_sum(dot(inner_low, down_full, 1, 0).astype(bf16), PLANE).astype(f32)
    mixed, finish_pull = jax.vjp(front, mlp_out, hidden, alpha_mlp)
    mlp_out_grad, hidden_grad, alpha_mlp_grad = finish_pull(cotangent.astype(f32))
    mlp_out_low = gather(mlp_out_grad.astype(bf16), PLANE)
    down_grad = dot(inner_low, mlp_out_low, 0, 0)
    up_proj_grad, gate_proj_grad, up_scale_grad, gate_scale_grad = core_pull(
        dot(mlp_out_low, down_full, 1, 1)
    )
    up_low, gate_low = up_proj_grad.astype(bf16), gate_proj_grad.astype(bf16)
    hidden_part = dot(up_low, up_full, 1, 0) + dot(gate_low, gate_full, 1, 0)
    hidden_grad = hidden_grad + scatter_sum(hidden_part.astype(bf16), PLANE).astype(f32)
    up_grad = dot(up_low, hidden_low, 0, 0)
    gate_grad = dot(gate_low, hidden_low, 0, 0)
    mlp_grads = jnp.stack(
        [g.astype(bf16).reshape(owners, units, -1) for g in (up_grad, gate_grad, down_grad)], 1
    )
    mlp_grads = scatter_sum(mlp_grads, OWNERS)[0].astype(f32)
    scale_grads = jnp.stack(
        [g.reshape(owners, units) for g in (up_scale_grad, gate_scale_grad)], axis=1
    )
    scale_grads = scatter_sum(scale_grads, OWNERS)[0]
    branch_grad, token_grad, alpha_attn_grad = front_pull(hidden_grad)

    group_branch = gather(branch_grad.astype(bf16), GROUP)
    got = dot(w_out, group_branch, 1, 1).astype(bf16)
    out_grad = dot(ot, group_branch, 1, 0)
    gqt, gkt, gvt = attention_backward(lengths, qt, kt, vt, ot, got, lse)
    gqt, query_gain_grad = features_back(turned_q, s_qk, gqt * (1.0 / ROOT), cosine, sine)
    gkt, key_gain_grad = features_back(turned_k, s_qk, gkt * (1.0 / ROOT), cosine, sine)
    joint_grad = jnp.concatenate([gqt, gkt, gvt], axis=0).astype(bf16)
    token_part = dot(joint_grad, joint, 0, 1)
    token_attn_grad = scatter_sum(token_part.astype(bf16), GROUP).astype(f32)
    joint_weight_grad = dot(group_tokens, joint_grad, 0, 1)
    dp = ("o", "x")
    joint_weight_grad = lax.psum(joint_weight_grad.astype(bf16), dp).astype(f32)
    out_grad = lax.psum(out_grad.astype(bf16), dp).astype(f32)
    gain_grad = lax.psum(query_gain_grad + key_gain_grad, dp)
    alpha_sums = lax.psum(jnp.stack([alpha_attn_grad, alpha_mlp_grad]), AXES)
    return (
        mixed.astype(bf16),
        (token_grad + token_attn_grad).astype(bf16),
        joint_weight_grad[:, :HEAD_DIM],
        joint_weight_grad[:, HEAD_DIM : 2 * HEAD_DIM],
        joint_weight_grad[:, 2 * HEAD_DIM :],
        gain_grad,
        out_grad,
        mlp_grads[0],
        mlp_grads[1],
        mlp_grads[2],
        scale_grads[0],
        scale_grads[1],
        alpha_sums[0],
        alpha_sums[1],
    )


def solution(mesh):
    dp, head = mesh.shape["dp"], mesh.shape["head"]
    fine = Mesh(mesh.devices.reshape(dp // 2, 2, head // 4, 2, 2), AXES)
    group, rows, heads = P(("o", "x"), None), P(AXES, None), P(None, GROUP)
    in_specs = (
        rows, group, heads, heads, heads, P(GROUP), P(GROUP, None), rows, rows, rows,
        P(AXES), P(AXES), P(), P(), rows,
    )
    out_specs = (
        rows, rows, heads, heads, heads, P(GROUP), P(GROUP, None), rows, rows, rows,
        P(AXES), P(AXES), P(), P(),
    )
    return jax.shard_map(
        shards, mesh=fine, in_specs=in_specs, out_specs=out_specs, check_vma=False
    )
```

```python
import functools
import math

import jax
import jax.numpy as jnp
from jax import lax
from jax.experimental import pallas as pl
from jax.experimental.pallas import tpu as pltpu
from jax.sharding import Mesh
from jax.sharding import PartitionSpec as P

HEAD_DIM = 64
BLOCK = 512
EPSILON = 1e-06
ROOT = math.sqrt(HEAD_DIM)
SCORE_SCALE = math.log2(math.e) / ROOT
AXES = ("o", "x", "z", "y", "c")
GROUP = ("z", "y", "c")
PLANE = ("x", "y", "c")
OWNERS = ("o", "z")
f32, bf16 = jnp.float32, jnp.bfloat16
VMEM_LIMIT = 56 * 2**20


def dot(left, right, left_dim, right_dim):
    return lax.dot_general(
        left, right, (((left_dim,), (right_dim,)), ((), ())), preferred_element_type=f32
    )


def unit_start(lengths, unit):
    start, end = jnp.int32(0), jnp.int32(0)
    for j in range(lengths.shape[1]):
        end = end + lengths[0, j]
        start = jnp.where(unit >= end, end, start)
    return start


def causal(weights):
    key = lax.broadcasted_iota(jnp.int32, weights.shape, 0)
    query = lax.broadcasted_iota(jnp.int32, weights.shape, 1)
    return jnp.where(key <= query, weights, 0.0)


def block_columns(index):
    return pl.ds(pl.multiple_of(index * BLOCK, BLOCK), BLOCK)


def attention_forward_kernel(lengths, qt, kt, vt, ot, lse):
    def unit(u, _):
        columns = block_columns(u)
        query = qt[:, columns]

        def part(j, carry, diagonal):
            total, attended = carry
            keys = block_columns(j)
            weights = jnp.exp2(dot(kt[:, keys], query, 0, 0) * SCORE_SCALE)
            if diagonal:
                weights = causal(weights)
            total = total + jnp.sum(weights, axis=0, keepdims=True)
            attended = attended + dot(vt[:, keys], weights.astype(bf16), 1, 0)
            return total, attended

        carry = (jnp.zeros((1, BLOCK), f32), jnp.zeros((HEAD_DIM, BLOCK), f32))
        carry = lax.fori_loop(unit_start(lengths, u), u, lambda j, c: part(j, c, False), carry)
        total, attended = part(u, carry, True)
        ot[:, columns] = (attended * (1.0 / total)).astype(bf16)
        lse[:, columns] = jnp.log2(total)
        return 0

    lax.fori_loop(0, qt.shape[1] // BLOCK, unit, 0)


def attention_backward_kernel(lengths, qt, kt, vt, ot, got, lse, gqt, gkt, gvt):
    def unit(u, _):
        columns = block_columns(u)
        query, grad, log_total = qt[:, columns], got[:, columns], lse[:, columns]
        inner = jnp.sum(grad.astype(f32) * ot[:, columns].astype(f32), axis=0, keepdims=True)

        def part(j, query_grad, diagonal):
            keys = block_columns(j)
            key, value = kt[:, keys], vt[:, keys]
            weights = jnp.exp2(dot(key, query, 0, 0) * SCORE_SCALE - log_total)
            if diagonal:
                weights = causal(weights)
            weight_grad = dot(value, grad, 0, 0)
            score_grad = (weights * (weight_grad - inner)).astype(bf16)
            key_part = dot(query, score_grad, 1, 1)
            value_part = dot(grad, weights.astype(bf16), 1, 1)
            if diagonal:
                gkt[:, keys] = key_part
                gvt[:, keys] = value_part
            else:
                gkt[:, keys] += key_part
                gvt[:, keys] += value_part
            return query_grad + dot(key, score_grad, 1, 0)

        query_grad = part(u, jnp.zeros((HEAD_DIM, BLOCK), f32), True)
        gqt[:, columns] = lax.fori_loop(
            unit_start(lengths, u), u, lambda j, c: part(j, c, False), query_grad
        )
        return 0

    lax.fori_loop(0, qt.shape[1] // BLOCK, unit, 0)


def attention_call(kernel, name, outs, lengths, *operands):
    vmem = pl.BlockSpec(memory_space=pltpu.VMEM)
    return pl.pallas_call(
        kernel,
        name=name,
        out_shape=outs,
        in_specs=[pl.BlockSpec(memory_space=pltpu.SMEM)] + [vmem] * len(operands),
        out_specs=tuple(vmem for _ in outs),
        compiler_params=pltpu.CompilerParams(vmem_limit_bytes=VMEM_LIMIT),
    )(lengths, *operands)


def attention_forward(lengths, qt, kt, vt):
    rows = qt.shape[1]
    outs = (jax.ShapeDtypeStruct((HEAD_DIM, rows), bf16), jax.ShapeDtypeStruct((1, rows), f32))
    return attention_call(attention_forward_kernel, "attn_forward", outs, lengths, qt, kt, vt)


def attention_backward(lengths, *operands):
    outs = (jax.ShapeDtypeStruct(operands[0].shape, f32),) * 3
    return attention_call(attention_backward_kernel, "attn_backward", outs, lengths, *operands)


def sphere(values):
    return values * lax.rsqrt(jnp.mean(values * values, axis=-1, keepdims=True) + EPSILON)


def turn_table(lengths_row, rows):
    ends = jnp.sum(jnp.where(jnp.tri(lengths_row.shape[0], dtype=bool), lengths_row[None, :], 0), 1)
    row = jnp.arange(rows, dtype=jnp.int32)
    passed = (row // BLOCK)[None, :] >= ends[:, None]
    place = row - BLOCK * jnp.max(jnp.where(passed, ends[:, None], 0), axis=0)
    half = HEAD_DIM // 2
    frequency = jnp.exp(jnp.arange(half, dtype=f32) * (-2.0 * math.log(10000.0) / HEAD_DIM))
    angle = place.astype(f32)[None, :] * frequency[:, None]
    return jnp.cos(angle), jnp.sin(angle)


def turn(values, cosine, sine):
    half = HEAD_DIM // 2
    a, b = values[:half], values[half:]
    return jnp.concatenate([a * cosine - b * sine, b * cosine + a * sine], axis=0)


def unit_features(turned):
    scale = lax.rsqrt(jnp.mean(turned * turned, axis=0, keepdims=True) + EPSILON)
    return turned * scale, scale


def features_back(turned, gain, grad, cosine, sine):
    normal, scale = unit_features(turned)
    gain_grad = jnp.sum(grad * normal, axis=1)
    grad = grad * gain[:, None]
    grad = scale * (grad - normal * jnp.mean(grad * normal, axis=0, keepdims=True))
    return turn(grad, cosine, -sine), gain_grad


def front(branch, own_tokens, alpha):
    return sphere(own_tokens + alpha * (sphere(branch) - own_tokens))


def core(up_proj, gate_proj, up_scale, gate_scale):
    gated = gate_proj * gate_scale
    return up_proj * up_scale * (gated * jax.nn.sigmoid(gated))


def gather(values, axes):
    return lax.all_gather(values, axes, axis=0, tiled=True)


def scatter_sum(values, axes):
    return lax.psum_scatter(values, axes, scatter_dimension=0, tiled=True)


MESH_ID = pl.DeviceIdType.MESH


def here(*names):
    return tuple(lax.axis_index(name) for name in names)


def greet(neighbours):
    barrier = pltpu.get_barrier_semaphore()
    count = jnp.int32(0)
    for condition, device in neighbours:

        @pl.when(condition)
        def _():
            pl.semaphore_signal(barrier, inc=1, device_id=device, device_id_type=MESH_ID)

        count = count + jnp.where(condition, 1, 0)
    pl.semaphore_wait(barrier, count)


def remote(source, target, send, receive, device):
    return pltpu.make_async_remote_copy(
        src_ref=source,
        dst_ref=target,
        send_sem=send,
        recv_sem=receive,
        device_id=device,
        device_id_type=MESH_ID,
    )


def line_order(z, length, step):
    picked = jnp.int32(0)
    for at in range(length):
        order = sorted(range(length), key=lambda p: (abs(p - at), p if at < length // 2 else -p))
        picked = jnp.where(z == at, order[step], picked)
    return picked


def group_neighbours(length):
    z, y, c = here("z", "y", "c")
    return [
        (z > 0, {"z": z - 1}),
        (z < length - 1, {"z": z + 1}),
        (z >= 0, {"y": 1 - y}),
        (z >= 0, {"c": 1 - c}),
    ]


def group_gather(length, own, held, send, receive, on_unit):
    z, y, c = here("z", "y", "c")
    rows = held.shape[1] // 2

    def block(zz, yy, cc):
        return held.at[zz * 2 + yy, pl.ds(pl.multiple_of(cc * rows, rows), rows)]

    def copy(kind, zz, yy, cc, device):
        at = block(zz, yy, cc)
        number = (zz * 2 + yy) * 2 + cc
        return remote(at, at, send.at[kind, number], receive.at[number], device)

    def arrived(zz, yy, cc):
        copy(3, zz, yy, cc, {"c": 1 - c}).wait_recv()

    def passed_on(zz, act):
        @pl.when((zz <= z) & (z < length - 1))
        def _():
            act(copy(0, zz, y, c, {"z": z + 1}))

        @pl.when((zz >= z) & (z > 0))
        def _():
            act(copy(1, zz, y, c, {"z": z - 1}))

        act(copy(2, zz, y, c, {"y": 1 - y}))
        act(copy(3, zz, y, c, {"c": 1 - c}))

    block(z, y, c)[...] = own[...]
    order = [line_order(z, length, step) for step in range(length)]
    for step in range(length + 1):
        if step < length:
            if step > 0:
                arrived(order[step], y, c)
            passed_on(order[step], lambda copy_: copy_.start())
        if step > 0:
            zz = order[step - 1]
            arrived(zz, y, 1 - c)
            on_unit(zz * 2 + y)
            arrived(zz, 1 - y, c)
            copy(3, zz, 1 - y, c, {"c": 1 - c}).start()
            arrived(zz, 1 - y, 1 - c)
            on_unit(zz * 2 + 1 - y)
    for step in range(length):
        passed_on(order[step], lambda copy_: copy_.wait_send())
        copy(3, order[step], 1 - y, c, {"c": 1 - c}).wait_send()


GATHER_SEMAPHORES = 4


def gather_scratch(units, rows, width):
    return [
        pltpu.VMEM((units, 2 * rows, width), bf16),
        pltpu.SemaphoreType.DMA((GATHER_SEMAPHORES, 2 * units)),
        pltpu.SemaphoreType.DMA((2 * units,)),
    ]


def scatter_scratch(length, rows, width):
    return [
        pltpu.VMEM((2 * length, rows, width), f32),
        pltpu.VMEM((2, 2 * length, rows, width), bf16),
        pltpu.VMEM((2, length, rows, width), bf16),
        pltpu.VMEM((3, length, rows, width), bf16),
        pltpu.SemaphoreType.DMA((2, 2 * length)),
        pltpu.SemaphoreType.DMA((2, length)),
        pltpu.SemaphoreType.DMA((3, length)),
    ]


def group_scatter(length, produce, own, cross, across, along, cross_sem, across_sem, along_sem, between=None):
    z, y, c = here("z", "y", "c")

    def to_core(unit):
        return remote(cross.at[0, unit], cross.at[1, unit], cross_sem.at[0, unit], cross_sem.at[1, unit], {"c": 1 - c})

    def to_y(zz):
        return remote(across.at[0, zz], across.at[1, zz], across_sem.at[0, zz], across_sem.at[1, zz], {"y": 1 - y})

    def to_z(zz, slot, device):
        return remote(along.at[0, zz], along.at[slot, zz], along_sem.at[0, zz], along_sem.at[slot, zz], device)

    def from_z(zz, slot):
        to_z(zz, slot, {"c": 1 - c}).wait_recv()
        return along[slot, zz].astype(f32)

    order = [line_order(z, length, length - 1 - step) for step in range(length)]

    def first(zz):
        for yy in (1 - y, y):
            unit = zz * 2 + yy
            cross[0, unit] = produce(unit, 1 - c).astype(bf16)
            to_core(unit).start()
        for yy in (1 - y, y):
            unit = zz * 2 + yy
            own[unit] = produce(unit, c)

    def second(zz):
        unit = zz * 2 + 1 - y
        to_core(unit).wait_recv()
        across[0, zz] = (own[unit] + cross[1, unit].astype(f32)).astype(bf16)
        to_y(zz).start()

    def third(zz, last):
        unit = zz * 2 + y
        to_core(unit).wait_recv()
        own[unit] += cross[1, unit].astype(f32)
        to_y(zz).wait_recv()
        own[unit] += across[1, zz].astype(f32)

        @pl.when((zz >= z) & (z > 0))
        def _():
            own[unit] += from_z(zz, 1)

        @pl.when((zz <= z) & (z < length - 1))
        def _():
            own[unit] += from_z(zz, 2)

        if last:
            return own[unit]
        along[0, zz] = own[unit].astype(bf16)

        @pl.when(zz > z)
        def _():
            to_z(zz, 1, {"z": z + 1}).start()

        @pl.when(zz < z)
        def _():
            to_z(zz, 2, {"z": z - 1}).start()

        return None

    total = None
    for step in range(length + 2):
        if step < length:
            first(order[step])
        if 1 <= step <= length:
            second(order[step - 1])
        if step == length and between is not None:
            between()
        if step >= 2:
            total = third(order[step - 2], step == length + 1)
    for step in range(length):
        zz = order[step]
        for yy in (0, 1):
            to_core(zz * 2 + yy).wait_send()
        to_y(zz).wait_send()
        if step < length - 1:
            to_z(zz, 1, {"c": 1 - c}).wait_send()
    return total


def remote_call(kernel, name, number, outs, out_specs, in_specs, scratch, *operands):
    return pl.pallas_call(
        kernel,
        name=name,
        out_shape=outs,
        in_specs=in_specs,
        out_specs=out_specs,
        scratch_shapes=scratch,
        compiler_params=pltpu.CompilerParams(
            collective_id=number, has_side_effects=True, vmem_limit_bytes=VMEM_LIMIT
        ),
    )(*operands)


IN_VMEM = pl.BlockSpec(memory_space=pltpu.VMEM)
ANYWHERE = pl.BlockSpec(memory_space=pl.ANY)


def like(shape, dtype):
    return jax.ShapeDtypeStruct(shape, dtype)


def project_kernel(
    length, tokens, joint, gain, cosine, sine, gathered, turned_q, turned_k, qt, kt, vt,
    held, send, receive, out_sem,
):
    greet(group_neighbours(length))

    def on_unit(unit):
        copy = pltpu.make_async_copy(held.at[unit], gathered.at[unit], out_sem.at[unit])
        copy.start()
        columns = block_columns(unit)
        projected = dot(joint[...], held[unit], 1, 1)
        for part, turned, features in ((0, turned_q, qt), (1, turned_k, kt)):
            values = turn(
                projected[part * HEAD_DIM : (part + 1) * HEAD_DIM], cosine[:, columns], sine[:, columns]
            )
            turned[:, columns] = values
            features[:, columns] = (unit_features(values)[0] * gain[...]).astype(bf16)
        vt[:, columns] = projected[2 * HEAD_DIM :].astype(bf16)

    group_gather(length, tokens, held, send, receive, on_unit)
    for unit in range(2 * length):
        pltpu.make_async_copy(held.at[unit], gathered.at[unit], out_sem.at[unit]).wait()


def project(length, tokens, joint, gain, cosine, sine):
    rows, width = tokens.shape
    units = 2 * length
    total = units * 2 * rows
    wide, narrow = like((HEAD_DIM, total), f32), like((HEAD_DIM, total), bf16)
    return remote_call(
        functools.partial(project_kernel, length), "project", 1,
        (like((units, 2 * rows, width), bf16), wide, wide, narrow, narrow, narrow),
        (ANYWHERE,) + (IN_VMEM,) * 5, [IN_VMEM] * 5,
        gather_scratch(units, rows, width) + [pltpu.SemaphoreType.DMA((units,))],
        tokens, joint, gain, cosine, sine,
    )


def half_columns(unit, half):
    rows = BLOCK // 2
    return pl.ds(pl.multiple_of(unit * BLOCK + half * rows, rows), rows)


def branch_kernel(length, ot, w_out, branch, *scratch):
    greet(group_neighbours(length))
    branch[...] = group_scatter(
        length, lambda unit, half: dot(ot[:, half_columns(unit, half)], w_out[...], 0, 0), *scratch
    )


def branch_sum(length, ot, w_out, rows):
    width = w_out.shape[1]
    return remote_call(
        functools.partial(branch_kernel, length), "branch_sum", 2,
        like((rows, width), f32), IN_VMEM, [IN_VMEM] * 2, scatter_scratch(length, rows, width), ot, w_out,
    )


def spread_kernel(length, grad, w_out, ot, got, out_grad, held, send, receive):
    greet(group_neighbours(length))
    out_grad[...] = jnp.zeros_like(out_grad)

    def on_unit(unit):
        columns = block_columns(unit)
        got[:, columns] = dot(w_out[...], held[unit], 1, 1).astype(bf16)
        out_grad[...] += dot(ot[:, columns], held[unit], 1, 0)

    group_gather(length, grad, held, send, receive, on_unit)


def spread(length, grad, w_out, ot):
    rows, width = grad.shape
    return remote_call(
        functools.partial(spread_kernel, length), "spread", 3,
        (like(ot.shape, bf16), like(w_out.shape, f32)), (IN_VMEM,) * 2, [IN_VMEM] * 3,
        gather_scratch(2 * length, rows, width), grad, w_out, ot,
    )


def token_kernel(length, grads, joint, token_grad, *scratch):
    greet(group_neighbours(length))
    token_grad[...] = group_scatter(
        length, lambda unit, half: dot(grads[:, half_columns(unit, half)], joint[...], 0, 0), *scratch
    )


def token_sum(length, grads, joint, rows):
    width = joint.shape[1]
    return remote_call(
        functools.partial(token_kernel, length), "token_sum", 4,
        like((rows, width), f32), IN_VMEM, [IN_VMEM] * 2, scatter_scratch(length, rows, width), grads, joint,
    )


def shards(
    tokens, lengths, w_query, w_key, w_value, s_qk, w_out, up_weight, gate_weight, down_weight,
    s_up, s_gate, alpha_attn, alpha_mlp, cotangent,
):
    units = up_weight.shape[0]
    mlp_scale = gather(jnp.stack([s_up, s_gate])[None], OWNERS).astype(f32)
    owners = mlp_scale.shape[0]
    down_full = gather(down_weight, OWNERS)
    up_scale, gate_scale = (mlp_scale[:, i].reshape(1, owners * units) for i in range(2))

    length = lax.axis_size("z")
    own_rows, width = tokens.shape
    rows = 4 * length * own_rows
    cosine, sine = turn_table(lengths[0], rows)
    joint = jnp.concatenate([w_query, w_key, w_value], axis=1).T
    group_tokens, turned_q, turned_k, qt, kt, vt = project(
        length, tokens, joint, s_qk[:, None], cosine, sine
    )
    up_gate = jnp.stack([up_weight, gate_weight])[None]
    qt, up_gate = lax.optimization_barrier((qt, up_gate))
    up_gate = gather(up_gate, OWNERS)
    up_full, gate_full = (up_gate[:, i].reshape(owners * units, -1) for i in range(2))
    ot, lse = attention_forward(lengths, qt, kt, vt)
    branch = branch_sum(length, ot, w_out, own_rows)

    hidden, front_pull = jax.vjp(front, branch, tokens.astype(f32), alpha_attn)
    hidden_low = gather(hidden.astype(bf16), PLANE)
    up_proj = dot(hidden_low, up_full, 1, 1)
    gate_proj = dot(hidden_low, gate_full, 1, 1)
    inner, core_pull = jax.vjp(core, up_proj, gate_proj, up_scale, gate_scale)
    inner_low = inner.astype(bf16)
    mlp_out = scatter_sum(dot(inner_low, down_full, 1, 0).astype(bf16), PLANE).astype(f32)
    mixed, finish_pull = jax.vjp(front, mlp_out, hidden, alpha_mlp)
    mlp_out_grad, hidden_grad, alpha_mlp_grad = finish_pull(cotangent.astype(f32))
    mlp_out_low = gather(mlp_out_grad.astype(bf16), PLANE)
    down_grad = dot(inner_low, mlp_out_low, 0, 0)
    up_proj_grad, gate_proj_grad, up_scale_grad, gate_scale_grad = core_pull(
        dot(mlp_out_low, down_full, 1, 1)
    )
    up_low, gate_low = up_proj_grad.astype(bf16), gate_proj_grad.astype(bf16)
    hidden_part = dot(up_low, up_full, 1, 0) + dot(gate_low, gate_full, 1, 0)
    hidden_grad = hidden_grad + scatter_sum(hidden_part.astype(bf16), PLANE).astype(f32)
    up_grad = dot(up_low, hidden_low, 0, 0)
    gate_grad = dot(gate_low, hidden_low, 0, 0)
    mlp_grads = jnp.stack(
        [g.astype(bf16).reshape(owners, units, -1) for g in (up_grad, gate_grad, down_grad)], 1
    )
    mlp_grads = scatter_sum(mlp_grads, OWNERS)[0].astype(f32)
    scale_grads = jnp.stack(
        [g.reshape(owners, units) for g in (up_scale_grad, gate_scale_grad)], axis=1
    )
    scale_grads = scatter_sum(scale_grads, OWNERS)[0]
    branch_grad, token_grad, alpha_attn_grad = front_pull(hidden_grad)

    got, out_grad = spread(length, branch_grad.astype(bf16), w_out, ot)
    gqt, gkt, gvt = attention_backward(lengths, qt, kt, vt, ot, got, lse)
    gqt, query_gain_grad = features_back(turned_q, s_qk, gqt * (1.0 / ROOT), cosine, sine)
    gkt, key_gain_grad = features_back(turned_k, s_qk, gkt * (1.0 / ROOT), cosine, sine)
    joint_grad = jnp.concatenate([gqt, gkt, gvt], axis=0).astype(bf16)
    token_attn_grad = token_sum(length, joint_grad, joint, own_rows)
    joint_weight_grad = dot(group_tokens.reshape(rows, width), joint_grad, 0, 1)
    dp = ("o", "x")
    joint_weight_grad = lax.psum(joint_weight_grad.astype(bf16), dp).astype(f32)
    out_grad = lax.psum(out_grad.astype(bf16), dp).astype(f32)
    gain_grad = lax.psum(query_gain_grad + key_gain_grad, dp)
    alpha_sums = lax.psum(jnp.stack([alpha_attn_grad, alpha_mlp_grad]), AXES)
    return (
        mixed.astype(bf16),
        (token_grad + token_attn_grad).astype(bf16),
        joint_weight_grad[:, :HEAD_DIM],
        joint_weight_grad[:, HEAD_DIM : 2 * HEAD_DIM],
        joint_weight_grad[:, 2 * HEAD_DIM :],
        gain_grad,
        out_grad,
        mlp_grads[0],
        mlp_grads[1],
        mlp_grads[2],
        scale_grads[0],
        scale_grads[1],
        alpha_sums[0],
        alpha_sums[1],
    )


def solution(mesh):
    dp, head = mesh.shape["dp"], mesh.shape["head"]
    fine = Mesh(mesh.devices.reshape(dp // 2, 2, head // 4, 2, 2), AXES)
    group, rows, heads = P(("o", "x"), None), P(AXES, None), P(None, GROUP)
    in_specs = (
        rows, group, heads, heads, heads, P(GROUP), P(GROUP, None), rows, rows, rows,
        P(AXES), P(AXES), P(), P(), rows,
    )
    out_specs = (
        rows, rows, heads, heads, heads, P(GROUP), P(GROUP, None), rows, rows, rows,
        P(AXES), P(AXES), P(), P(),
    )
    return jax.shard_map(
        shards, mesh=fine, in_specs=in_specs, out_specs=out_specs, check_vma=False
    )
```

```python
import functools
import math

import jax
import jax.numpy as jnp
from jax import lax
from jax.experimental import pallas as pl
from jax.experimental.pallas import tpu as pltpu
from jax.sharding import Mesh
from jax.sharding import PartitionSpec as P

HEAD_DIM = 64
BLOCK = 512
EPSILON = 1e-06
ROOT = math.sqrt(HEAD_DIM)
SCORE_SCALE = math.log2(math.e) / ROOT
AXES = ("o", "x", "z", "y", "c")
GROUP = ("z", "y", "c")
f32, bf16 = jnp.float32, jnp.bfloat16
VMEM_LIMIT = 56 * 2**20


def dot(left, right, left_dim, right_dim):
    return lax.dot_general(
        left, right, (((left_dim,), (right_dim,)), ((), ())), preferred_element_type=f32
    )


def unit_start(lengths, unit):
    start, end = jnp.int32(0), jnp.int32(0)
    for j in range(lengths.shape[1]):
        end = end + lengths[0, j]
        start = jnp.where(unit >= end, end, start)
    return start


def causal(weights):
    key = lax.broadcasted_iota(jnp.int32, weights.shape, 0)
    query = lax.broadcasted_iota(jnp.int32, weights.shape, 1)
    return jnp.where(key <= query, weights, 0.0)


def block_columns(index):
    return pl.ds(pl.multiple_of(index * BLOCK, BLOCK), BLOCK)


def attention_forward_kernel(lengths, qt, kt, vt, ot, lse):
    def unit(u, _):
        columns = block_columns(u)
        query = qt[:, columns]

        def part(j, carry, diagonal):
            total, attended = carry
            keys = block_columns(j)
            weights = jnp.exp2(dot(kt[:, keys], query, 0, 0) * SCORE_SCALE)
            if diagonal:
                weights = causal(weights)
            total = total + jnp.sum(weights, axis=0, keepdims=True)
            attended = attended + dot(vt[:, keys], weights.astype(bf16), 1, 0)
            return total, attended

        carry = (jnp.zeros((1, BLOCK), f32), jnp.zeros((HEAD_DIM, BLOCK), f32))
        carry = lax.fori_loop(unit_start(lengths, u), u, lambda j, c: part(j, c, False), carry)
        total, attended = part(u, carry, True)
        ot[:, columns] = (attended * (1.0 / total)).astype(bf16)
        lse[:, columns] = jnp.log2(total)
        return 0

    lax.fori_loop(0, qt.shape[1] // BLOCK, unit, 0)


def attention_backward_kernel(lengths, qt, kt, vt, ot, got, lse, gqt, gkt, gvt):
    def unit(u, _):
        columns = block_columns(u)
        query, grad, log_total = qt[:, columns], got[:, columns], lse[:, columns]
        inner = jnp.sum(grad.astype(f32) * ot[:, columns].astype(f32), axis=0, keepdims=True)

        def part(j, query_grad, diagonal):
            keys = block_columns(j)
            key, value = kt[:, keys], vt[:, keys]
            weights = jnp.exp2(dot(key, query, 0, 0) * SCORE_SCALE - log_total)
            if diagonal:
                weights = causal(weights)
            weight_grad = dot(value, grad, 0, 0)
            score_grad = (weights * (weight_grad - inner)).astype(bf16)
            key_part = dot(query, score_grad, 1, 1)
            value_part = dot(grad, weights.astype(bf16), 1, 1)
            if diagonal:
                gkt[:, keys] = key_part
                gvt[:, keys] = value_part
            else:
                gkt[:, keys] += key_part
                gvt[:, keys] += value_part
            return query_grad + dot(key, score_grad, 1, 0)

        query_grad = part(u, jnp.zeros((HEAD_DIM, BLOCK), f32), True)
        gqt[:, columns] = lax.fori_loop(
            unit_start(lengths, u), u, lambda j, c: part(j, c, False), query_grad
        )
        return 0

    lax.fori_loop(0, qt.shape[1] // BLOCK, unit, 0)


def attention_call(kernel, name, outs, lengths, *operands):
    vmem = pl.BlockSpec(memory_space=pltpu.VMEM)
    return pl.pallas_call(
        kernel,
        name=name,
        out_shape=outs,
        in_specs=[pl.BlockSpec(memory_space=pltpu.SMEM)] + [vmem] * len(operands),
        out_specs=tuple(vmem for _ in outs),
        compiler_params=pltpu.CompilerParams(vmem_limit_bytes=VMEM_LIMIT),
    )(lengths, *operands)


def attention_forward(lengths, qt, kt, vt):
    rows = qt.shape[1]
    outs = (jax.ShapeDtypeStruct((HEAD_DIM, rows), bf16), jax.ShapeDtypeStruct((1, rows), f32))
    return attention_call(attention_forward_kernel, "attn_forward", outs, lengths, qt, kt, vt)


def attention_backward(lengths, *operands):
    outs = (jax.ShapeDtypeStruct(operands[0].shape, f32),) * 3
    return attention_call(attention_backward_kernel, "attn_backward", outs, lengths, *operands)


def turn_table(lengths_row, rows):
    ends = jnp.sum(jnp.where(jnp.tri(lengths_row.shape[0], dtype=bool), lengths_row[None, :], 0), 1)
    row = jnp.arange(rows, dtype=jnp.int32)
    passed = (row // BLOCK)[None, :] >= ends[:, None]
    place = row - BLOCK * jnp.max(jnp.where(passed, ends[:, None], 0), axis=0)
    half = HEAD_DIM // 2
    frequency = jnp.exp(jnp.arange(half, dtype=f32) * (-2.0 * math.log(10000.0) / HEAD_DIM))
    angle = place.astype(f32)[None, :] * frequency[:, None]
    return jnp.cos(angle), jnp.sin(angle)


def turn(values, cosine, sine):
    half = HEAD_DIM // 2
    a, b = values[:half], values[half:]
    return jnp.concatenate([a * cosine - b * sine, b * cosine + a * sine], axis=0)


def unit_features(turned):
    scale = lax.rsqrt(jnp.mean(turned * turned, axis=0, keepdims=True) + EPSILON)
    return turned * scale, scale


def gather(values, axes):
    return lax.all_gather(values, axes, axis=0, tiled=True)


MESH_ID = pl.DeviceIdType.MESH


def here(*names):
    return tuple(lax.axis_index(name) for name in names)


def greet(neighbours):
    barrier = pltpu.get_barrier_semaphore()
    count = jnp.int32(0)
    for condition, device in neighbours:

        @pl.when(condition)
        def _():
            pl.semaphore_signal(barrier, inc=1, device_id=device, device_id_type=MESH_ID)

        count = count + jnp.where(condition, 1, 0)
    pl.semaphore_wait(barrier, count)


def remote(source, target, send, receive, device):
    return pltpu.make_async_remote_copy(
        src_ref=source,
        dst_ref=target,
        send_sem=send,
        recv_sem=receive,
        device_id=device,
        device_id_type=MESH_ID,
    )


def line_order(z, length, step):
    picked = jnp.int32(0)
    for at in range(length):
        order = sorted(range(length), key=lambda p: (abs(p - at), p if at < length // 2 else -p))
        picked = jnp.where(z == at, order[step], picked)
    return picked


def group_neighbours(length):
    z, y, c = here("z", "y", "c")
    return [
        (z > 0, {"z": z - 1}),
        (z < length - 1, {"z": z + 1}),
        (z >= 0, {"y": 1 - y}),
        (z >= 0, {"c": 1 - c}),
    ]


def group_gather(length, own, held, send, receive, on_unit, at_step=None):
    z, y, c = here("z", "y", "c")
    rows = held.shape[1] // 2

    def block(zz, yy, cc):
        return held.at[zz * 2 + yy, pl.ds(pl.multiple_of(cc * rows, rows), rows)]

    def copy(kind, zz, yy, cc, device):
        at = block(zz, yy, cc)
        number = (zz * 2 + yy) * 2 + cc
        return remote(at, at, send.at[kind, number], receive.at[number], device)

    def arrived(zz, yy, cc):
        copy(3, zz, yy, cc, {"c": 1 - c}).wait_recv()

    def passed_on(zz, act):
        @pl.when((zz <= z) & (z < length - 1))
        def _():
            act(copy(0, zz, y, c, {"z": z + 1}))

        @pl.when((zz >= z) & (z > 0))
        def _():
            act(copy(1, zz, y, c, {"z": z - 1}))

        act(copy(2, zz, y, c, {"y": 1 - y}))
        act(copy(3, zz, y, c, {"c": 1 - c}))

    block(z, y, c)[...] = own[...]
    order = [line_order(z, length, step) for step in range(length)]
    for step in range(length + 1):
        if step < length:
            if step > 0:
                arrived(order[step], y, c)
            passed_on(order[step], lambda copy_: copy_.start())
        if at_step is not None:
            at_step(step)
        if step > 0:
            zz = order[step - 1]
            arrived(zz, y, 1 - c)
            on_unit(zz * 2 + y)
            arrived(zz, 1 - y, c)
            copy(3, zz, 1 - y, c, {"c": 1 - c}).start()
            arrived(zz, 1 - y, 1 - c)
            on_unit(zz * 2 + 1 - y)
    for step in range(length):
        passed_on(order[step], lambda copy_: copy_.wait_send())
        copy(3, order[step], 1 - y, c, {"c": 1 - c}).wait_send()


GATHER_SEMAPHORES = 4


def gather_scratch(units, rows, width):
    return [
        pltpu.VMEM((units, 2 * rows, width), bf16),
        pltpu.SemaphoreType.DMA((GATHER_SEMAPHORES, 2 * units)),
        pltpu.SemaphoreType.DMA((2 * units,)),
    ]


def scatter_scratch(length, rows, width):
    return [
        pltpu.VMEM((2 * length, rows, width), f32),
        pltpu.VMEM((2, 2 * length, rows, width), bf16),
        pltpu.VMEM((2, length, rows, width), bf16),
        pltpu.VMEM((3, length, rows, width), bf16),
        pltpu.SemaphoreType.DMA((2, 2 * length)),
        pltpu.SemaphoreType.DMA((2, length)),
        pltpu.SemaphoreType.DMA((3, length)),
    ]


def group_scatter(length, produce, own, cross, across, along, cross_sem, across_sem, along_sem, prepare=None, between=None, at_step=None):
    z, y, c = here("z", "y", "c")

    def to_core(unit):
        return remote(cross.at[0, unit], cross.at[1, unit], cross_sem.at[0, unit], cross_sem.at[1, unit], {"c": 1 - c})

    def to_y(zz):
        return remote(across.at[0, zz], across.at[1, zz], across_sem.at[0, zz], across_sem.at[1, zz], {"y": 1 - y})

    def to_z(zz, slot, device):
        return remote(along.at[0, zz], along.at[slot, zz], along_sem.at[0, zz], along_sem.at[slot, zz], device)

    def from_z(zz, slot):
        to_z(zz, slot, {"c": 1 - c}).wait_recv()
        return along[slot, zz].astype(f32)

    order = [line_order(z, length, length - 1 - step) for step in range(length)]

    def first(zz):
        for yy in (1 - y, y):
            unit = zz * 2 + yy
            if prepare is not None:
                prepare(unit)
            cross[0, unit] = produce(unit, 1 - c).astype(bf16)
            to_core(unit).start()
        for yy in (1 - y, y):
            unit = zz * 2 + yy
            own[unit] = produce(unit, c)

    def second(zz):
        unit = zz * 2 + 1 - y
        to_core(unit).wait_recv()
        across[0, zz] = (own[unit] + cross[1, unit].astype(f32)).astype(bf16)
        to_y(zz).start()

    def third(zz, last):
        unit = zz * 2 + y
        to_core(unit).wait_recv()
        own[unit] += cross[1, unit].astype(f32)
        to_y(zz).wait_recv()
        own[unit] += across[1, zz].astype(f32)

        @pl.when((zz >= z) & (z > 0))
        def _():
            own[unit] += from_z(zz, 1)

        @pl.when((zz <= z) & (z < length - 1))
        def _():
            own[unit] += from_z(zz, 2)

        if last:
            return own[unit]
        along[0, zz] = own[unit].astype(bf16)

        @pl.when(zz > z)
        def _():
            to_z(zz, 1, {"z": z + 1}).start()

        @pl.when(zz < z)
        def _():
            to_z(zz, 2, {"z": z - 1}).start()

        return None

    total = None
    for step in range(length + 2):
        if step < length:
            first(order[step])
        if at_step is not None:
            at_step(step)
        if 1 <= step <= length:
            second(order[step - 1])
        if step == length and between is not None:
            between()
        if step >= 2:
            total = third(order[step - 2], step == length + 1)
    for step in range(length):
        zz = order[step]
        for yy in (0, 1):
            to_core(zz * 2 + yy).wait_send()
        to_y(zz).wait_send()
        if step < length - 1:
            to_z(zz, 1, {"c": 1 - c}).wait_send()
    return total


def remote_call(kernel, name, number, outs, out_specs, in_specs, scratch, *operands):
    return pl.pallas_call(
        kernel,
        name=name,
        out_shape=outs,
        in_specs=in_specs,
        out_specs=out_specs,
        scratch_shapes=scratch,
        compiler_params=pltpu.CompilerParams(
            collective_id=number, has_side_effects=True, vmem_limit_bytes=VMEM_LIMIT
        ),
    )(*operands)


IN_VMEM = pl.BlockSpec(memory_space=pltpu.VMEM)
ANYWHERE = pl.BlockSpec(memory_space=pl.ANY)


def like(shape, dtype):
    return jax.ShapeDtypeStruct(shape, dtype)


class LineGather:
    def __init__(self, length, own, held, send, receive, local_sem):
        self.length, self.own, self.held = length, own, held
        self.sems, self.local_sem = (send, receive), local_sem
        self.z = lax.axis_index("z")

    def copy(self, way, zz, source=None):
        send, receive = self.sems
        at = self.held.at[zz]
        device = {"z": self.z + 1} if way == 0 else {"z": self.z - 1}
        return remote(at if source is None else source, at, send.at[way, zz], receive.at[zz], device)

    def ways(self, d, act):
        z, length = self.z, self.length
        for way, zz, there, more in (
            (0, z - d, z - d >= 0, z < length - 1),
            (1, z + d, z + d < length, z > 0),
        ):
            act(way, zz, there, there & more)

    def stage(self, d):
        z = self.z
        if d == 0:
            pltpu.make_async_copy(self.own, self.held.at[z], self.local_sem).start()

        def begin(way, zz, there, more):
            if d > 0:

                @pl.when(there)
                def _():
                    self.arrival(way, zz).wait_recv()

            if d < self.length - 1:

                @pl.when(more)
                def _():
                    self.copy(way, zz, self.own if d == 0 else None).start()

        if d < self.length:
            self.ways(d, begin)
            return
        for e in range(self.length - 1):

            def finish(way, zz, there, more):
                @pl.when(more)
                def _():
                    self.copy(way, zz, self.own if e == 0 else None).wait_send()

            self.ways(e, finish)
        pltpu.make_async_copy(self.own, self.held.at[z], self.local_sem).wait()

    def arrival(self, way, zz):
        send, receive = self.sems
        at = self.held.at[zz]
        return remote(at, at, send.at[way, zz], receive.at[zz], {"c": 1 - lax.axis_index("c")})


def line_gather_semaphores(length):
    return [
        pltpu.SemaphoreType.DMA((2, length)),
        pltpu.SemaphoreType.DMA((length,)),
        pltpu.SemaphoreType.DMA,
    ]


class LineScatter:
    def __init__(self, length, parts, sums, moving, sems):
        self.length, self.parts, self.sums, self.moving, self.sems = length, parts, sums, moving, sems
        self.z = lax.axis_index("z")
        self.count = parts.shape[1]
        self.order = [line_order(self.z, length, length - 1 - step) for step in range(length)]
        self.items = [(i, step) for step in range(length - 1) for i in range(self.count)]

    def copy(self, i, zz, slot, device):
        return remote(
            self.moving.at[0, zz, i], self.moving.at[slot, zz, i],
            self.sems.at[0, zz, i], self.sems.at[slot, zz, i], device,
        )

    def summed(self, i, zz, store):
        z, length = self.z, self.length
        aside = {"c": 1 - lax.axis_index("c")}
        below, above = (zz >= z) & (z > 0), (zz <= z) & (z < length - 1)

        def value(slots):
            total = self.parts[zz, i].astype(f32)
            for slot in slots:
                total = total + self.moving[slot, zz, i].astype(f32)
            return total

        for slot, condition in ((1, below), (2, above)):

            @pl.when(condition)
            def _():
                self.copy(i, zz, slot, aside).wait_recv()

        @pl.when(below & above)
        def _():
            store(value((1, 2)))

        @pl.when(below & jnp.logical_not(above))
        def _():
            store(value((1,)))

        @pl.when(above & jnp.logical_not(below))
        def _():
            store(value((2,)))

        @pl.when(jnp.logical_not(above | below))
        def _():
            store(value(()))

    def item(self, i, step):
        zz = self.order[step]

        def store(total):
            self.moving[0, zz, i] = total.astype(bf16)

        self.summed(i, zz, store)

        @pl.when(zz > self.z)
        def _():
            self.copy(i, zz, 1, {"z": self.z + 1}).start()

        @pl.when(zz < self.z)
        def _():
            self.copy(i, zz, 2, {"z": self.z - 1}).start()

    def hook(self, h, pace=2):
        at_end = (self.z == 0) | (self.z == self.length - 1)
        for late, condition in ((0, at_end), (1, jnp.logical_not(at_end))):
            share = self.items[max(0, (h - late) * pace) : max(0, (h - late + 1) * pace)]
            if share:

                @pl.when(condition)
                def _():
                    for i, step in share:
                        self.item(i, step)

    def finish(self, hooks, pace=2):
        while (hooks - 1) * pace < len(self.items):
            self.hook(hooks, pace)
            hooks += 1
        for i in range(self.count):

            def store(total):
                self.sums[i] = total

            self.summed(i, self.order[self.length - 1], store)
        for i, step in self.items:
            self.copy(i, self.order[step], 1, {"c": 1 - lax.axis_index("c")}).wait_send()


def project_kernel(
    length, tokens, joint, gain, cosine, sine, gathered, turned_q, turned_k, qt, kt, vt,
    held, send, receive, out_sem,
):
    greet(group_neighbours(length))

    def on_unit(unit):
        copy = pltpu.make_async_copy(held.at[unit], gathered.at[unit], out_sem.at[unit])
        copy.start()
        columns = block_columns(unit)
        projected = dot(joint[...], held[unit], 1, 1)
        for part, turned, features in ((0, turned_q, qt), (1, turned_k, kt)):
            values = turn(
                projected[part * HEAD_DIM : (part + 1) * HEAD_DIM], cosine[:, columns], sine[:, columns]
            )
            turned[:, columns] = values
            features[:, columns] = (unit_features(values)[0] * gain[...]).astype(bf16)
        vt[:, columns] = projected[2 * HEAD_DIM :].astype(bf16)

    group_gather(length, tokens, held, send, receive, on_unit)
    for unit in range(2 * length):
        pltpu.make_async_copy(held.at[unit], gathered.at[unit], out_sem.at[unit]).wait()


def project(length, tokens, joint, gain, cosine, sine):
    rows, width = tokens.shape
    units = 2 * length
    total = units * 2 * rows
    wide, narrow = like((HEAD_DIM, total), f32), like((HEAD_DIM, total), bf16)
    return remote_call(
        functools.partial(project_kernel, length), "project", 1,
        (like((units, 2 * rows, width), bf16), wide, wide, narrow, narrow, narrow),
        (ANYWHERE,) + (IN_VMEM,) * 5, [IN_VMEM] * 5,
        gather_scratch(units, rows, width) + [pltpu.SemaphoreType.DMA((units,))],
        tokens, joint, gain, cosine, sine,
    )


def half_columns(unit, half):
    rows = BLOCK // 2
    return pl.ds(pl.multiple_of(unit * BLOCK + half * rows, rows), rows)


def branch_kernel(length, ot, w_out, weight, branch, weights, send, receive, local_sem, *scratch):
    greet(group_neighbours(length))
    line = LineGather(length, weight, weights, send, receive, local_sem)
    stages = {0: 0, 3: 1, 5: 2}

    def at_step(step):
        if step in stages:
            line.stage(stages[step])

    branch[...] = group_scatter(
        length, lambda unit, half: dot(ot[:, half_columns(unit, half)], w_out[...], 0, 0), *scratch,
        at_step=at_step,
    )
    for stage in range(1, length + 1):
        if stage not in stages.values():
            line.stage(stage)


def branch_sum(length, ot, w_out, weight, rows):
    width = w_out.shape[1]
    return remote_call(
        functools.partial(branch_kernel, length), "branch_sum", 2,
        (like((rows, width), f32), like((length, *weight.shape), bf16)), (IN_VMEM, ANYWHERE),
        [IN_VMEM] * 2 + [ANYWHERE], line_gather_semaphores(length) + scatter_scratch(length, rows, width),
        ot, w_out, weight,
    )


def spread_kernel(
    length, grad, w_out, ot, parts, got, out_grad, sums, held, send, receive, moving, moving_sem
):
    greet(group_neighbours(length))
    out_grad[...] = jnp.zeros_like(out_grad)
    line = LineScatter(length, parts, sums, moving, moving_sem)

    def on_unit(unit):
        columns = block_columns(unit)
        got[:, columns] = dot(w_out[...], held[unit], 1, 1).astype(bf16)
        out_grad[...] += dot(ot[:, columns], held[unit], 1, 0)

    group_gather(length, grad, held, send, receive, on_unit, line.hook)
    line.finish(length + 1)


def spread(length, grad, w_out, ot, parts):
    rows, width = grad.shape
    _, count, units, _ = parts.shape
    return remote_call(
        functools.partial(spread_kernel, length), "spread", 3,
        (like(ot.shape, bf16), like(w_out.shape, f32), like((count, units, width), f32)), (IN_VMEM,) * 3,
        [IN_VMEM] * 4,
        gather_scratch(2 * length, rows, width)
        + [pltpu.VMEM((3, *parts.shape), bf16), pltpu.SemaphoreType.DMA((3, length, count))],
        grad, w_out, ot, parts,
    )


def flip(position, bit):
    return position + bit - 2 * bit * ((position // bit) % 2)


def inward_kernel(
    length, gqt, gkt, gvt, turned_q, turned_k, gain, cosine, sine, joint, gathered, out_grad, alpha_grads,
    scale_grads, direct, token_grad, weight_grads, alpha_sums, scale_sums, gain_grad,
    grads, held, held_sem, gains, gain_sem, sent, taken, weight_sem, small_out, small_in, small_sem,
    *scratch,
):
    x, z, y, c = here("x", "z", "y", "c")
    to_x = {"x": 1 - x}
    bits = [1 << i for i in range(length.bit_length() - 1)]
    greet(group_neighbours(length) + [(x >= 0, to_x)] + [(x >= 0, {"z": flip(z, bit)}) for bit in bits])
    partners = [{"c": 1 - c}, {"y": 1 - y}, to_x] + [{"z": flip(z, bit)} for bit in bits]
    load = pltpu.make_async_copy(gathered, held, held_sem)
    load.start()
    gains[0] = jnp.zeros_like(gains[0])
    small_out[0] = jnp.zeros_like(small_out[0])
    small_out[0, 0:2] = alpha_grads[...]
    small_out[0, 2:4, : scale_grads.shape[1]] = scale_grads[...]

    def exchange(i):
        return remote(small_out.at[i], small_in.at[i], small_sem.at[0, i], small_sem.at[1, i], partners[i])

    def at_step(step):
        if 0 < step <= len(partners):
            exchange(step - 1).wait_recv()
            small_out[step] = small_out[step - 1]
            summed = 2 if step <= 3 else 4
            small_out[step, :summed] += small_in[step - 1, :summed]
        if step < len(partners):
            exchange(step).start()

    def prepare(unit):
        columns = block_columns(unit)
        for part, turned, outer in ((0, turned_q, gqt), (1, turned_k, gkt)):
            normal, scale = unit_features(turned[:, columns])
            grad = outer[:, columns] * (1.0 / ROOT)
            product = grad * normal
            width = gains.shape[2]
            for i in range(BLOCK // width):
                gains[0] += product[:, i * width : (i + 1) * width]
            grad = grad * gain[...]
            grad = scale * (grad - normal * jnp.mean(grad * normal, axis=0, keepdims=True))
            grad = turn(grad, cosine[:, columns], -sine[:, columns])
            grads[part * HEAD_DIM : (part + 1) * HEAD_DIM, columns] = grad.astype(bf16)
        grads[2 * HEAD_DIM :, columns] = gvt[:, columns].astype(bf16)

    gain_copy = remote(gains.at[0], gains.at[1], gain_sem.at[0], gain_sem.at[1], to_x)
    weight_copy = remote(sent, taken, weight_sem.at[0], weight_sem.at[1], to_x)

    def between():
        gain_copy.start()
        load.wait()
        rows = grads.shape[1]
        product = dot(grads[...], held[...].reshape(rows, held.shape[2]), 1, 0)
        sent[: 3 * HEAD_DIM] = product.astype(bf16)
        sent[3 * HEAD_DIM :] = out_grad[...].astype(bf16)
        weight_copy.start()

    total = group_scatter(
        length, lambda unit, half: dot(grads[:, half_columns(unit, half)], joint[...], 0, 0), *scratch,
        prepare=prepare, between=between, at_step=at_step,
    )
    token_grad[...] = (direct[...] + total).astype(bf16)
    for step in range(length + 2, len(partners) + 1):
        at_step(step)
    alpha_sums[...] = small_out[len(partners), 0:2]
    scale_sums[...] = small_out[len(partners), 2:4, : scale_sums.shape[1]]
    gain_copy.wait()
    gain_grad[...] = jnp.sum(gains[0] + gains[1], axis=1, keepdims=True)
    weight_copy.wait()
    weight_grads[...] = sent[...].astype(f32) + taken[...].astype(f32)
    for i in range(len(partners)):
        exchange(i).wait_send()


def inward(length, gathered, direct, out_grad, alpha_grads, scale_grads, *operands):
    rows, width = direct.shape
    units, block, _ = gathered.shape
    exchanges = 3 + length.bit_length() - 1
    small = (exchanges + 1, 4, width)
    weights = (4 * HEAD_DIM, width)
    scratch = [
        pltpu.VMEM((3 * HEAD_DIM, units * block), bf16),
        pltpu.VMEM(gathered.shape, bf16),
        pltpu.SemaphoreType.DMA,
        pltpu.VMEM((2, HEAD_DIM, 128), f32),
        pltpu.SemaphoreType.DMA((2,)),
        pltpu.VMEM(weights, bf16),
        pltpu.VMEM(weights, bf16),
        pltpu.SemaphoreType.DMA((2,)),
        pltpu.VMEM(small, f32),
        pltpu.VMEM(small, f32),
        pltpu.SemaphoreType.DMA((2, exchanges)),
    ]
    return remote_call(
        functools.partial(inward_kernel, length), "inward", 4,
        (
            like((rows, width), bf16), like(weights, f32), like(alpha_grads.shape, f32),
            like(scale_grads.shape, f32), like((HEAD_DIM, 1), f32),
        ),
        (IN_VMEM,) * 5, [IN_VMEM] * 9 + [ANYWHERE] + [IN_VMEM] * 4,
        scratch + scatter_scratch(length, rows, width),
        *operands, gathered, out_grad, alpha_grads, scale_grads, direct,
    )


def plane_neighbours():
    x, y, c = here("x", "y", "c")
    return [(x >= 0, {"x": 1 - x}), (x >= 0, {"y": 1 - y}), (x >= 0, {"c": 1 - c})]


def plane_gather(held, send, receive, on_pair):
    x, y, c = here("x", "y", "c")
    rows = held.shape[1] // 2
    half = rows // 2
    q0, qx, qy, qd = x * 2 + y, (1 - x) * 2 + y, x * 2 + 1 - y, (1 - x) * 2 + 1 - y
    to_x, to_y, to_c = (0, {"x": 1 - x}), (1, {"y": 1 - y}), (2, {"c": 1 - c})

    def copy(way, q, cc, h):
        at = held.at[q, pl.ds(pl.multiple_of(cc * rows + h * half, half), half)]
        return remote(at, at, send.at[way[0], q * 2 + h], receive.at[(q * 2 + cc) * 2 + h], way[1])

    def arrived(q, cc, h):
        copy(to_c, q, cc, h).wait_recv()

    sent = []

    def start(way, q, h):
        sent.append((way, q, h))
        copy(way, q, c, h).start()

    start(to_x, q0, 0)
    start(to_y, q0, 1)
    start(to_c, q0, 0)
    start(to_c, q0, 1)
    start(to_x, q0, 1)
    start(to_y, q0, 0)
    for h in (0, 1):
        arrived(q0, 1 - c, h)
    on_pair(q0)
    arrived(qx, c, 0)
    start(to_y, qx, 0)
    start(to_c, qx, 0)
    arrived(qy, c, 1)
    start(to_x, qy, 1)
    start(to_c, qy, 1)
    arrived(qx, c, 1)
    start(to_c, qx, 1)
    arrived(qy, c, 0)
    start(to_c, qy, 0)
    for q in (qx, qy):
        for h in (0, 1):
            arrived(q, 1 - c, h)
        on_pair(q)
    for h in (0, 1):
        arrived(qd, c, h)
        start(to_c, qd, h)
    for h in (0, 1):
        arrived(qd, 1 - c, h)
    on_pair(qd)
    for way, q, h in sent:
        copy(way, q, c, h).wait_send()


def plane_scatter(produce, own, cross, side, cross_sem, side_sem, between=None):
    x, y, c = here("x", "y", "c")
    rows = own.shape[1]
    half = rows // 2
    q0, qx, qy, qd = x * 2 + y, (1 - x) * 2 + y, x * 2 + 1 - y, (1 - x) * 2 + 1 - y
    to_x, to_y = {"x": 1 - x}, {"y": 1 - y}

    def to_core(q):
        return remote(cross.at[0, q], cross.at[1, q], cross_sem.at[0, q], cross_sem.at[1, q], {"c": 1 - c})

    def beside(kind, h, device):
        part = pl.ds(h * half, half)
        return remote(
            side.at[0, kind, part], side.at[1, kind, part], side_sem.at[0, kind, h], side_sem.at[1, kind, h], device
        )

    def first(q):
        cross[0, q] = produce(q, 1 - c).astype(bf16)
        to_core(q).start()
        own[q] = produce(q, c)

    def joined(q):
        to_core(q).wait_recv()
        own[q] += cross[1, q].astype(f32)

    def send(kind, q, h, device):
        part = pl.ds(h * half, half)
        side[0, kind, part] = own[q, part].astype(bf16)
        beside(kind, h, device).start()

    def add(q, kind, h, device):
        part = pl.ds(h * half, half)
        beside(kind, h, device).wait_recv()
        own[q, part] += side[1, kind, part].astype(f32)

    first(qd)
    first(qx)
    joined(qd)
    send(0, qd, 0, to_x)
    send(0, qd, 1, to_y)
    first(qy)
    joined(qx)
    send(1, qx, 0, to_x)
    joined(qy)
    send(2, qy, 1, to_y)
    first(q0)
    add(qx, 0, 1, to_y)
    send(1, qx, 1, to_x)
    add(qy, 0, 0, to_x)
    send(2, qy, 0, to_y)
    joined(q0)
    if between is not None:
        between()
    for h in (0, 1):
        add(q0, 1, h, to_x)
        add(q0, 2, 1 - h, to_y)
    for q in (q0, qx, qy, qd):
        to_core(q).wait_send()
    beside(0, 0, to_x).wait_send()
    beside(0, 1, to_y).wait_send()
    for h in (0, 1):
        beside(1, h, to_x).wait_send()
        beside(2, h, to_y).wait_send()


def mean_of(values):
    return jnp.mean(values, axis=-1, keepdims=True)


def scale_of(values):
    return lax.rsqrt(mean_of(values * values) + EPSILON)


def step_forward(target, start, alpha):
    target_scale = scale_of(target)
    unit = target * target_scale
    moved = start + alpha * (unit - start)
    moved_scale = scale_of(moved)
    return moved * moved_scale, unit, target_scale, moved_scale


def step_back(grad, result, unit, target_scale, moved_scale, start, alpha):
    moved_grad = moved_scale * (grad - result * mean_of(grad * result))
    unit_grad = alpha * moved_grad
    target_grad = target_scale * (unit_grad - unit * mean_of(unit_grad * unit))
    return target_grad, moved_grad - unit_grad, moved_grad * (unit - start)


CHUNK = 32
SCALE_ROWS = 16


def mlp_kernel(
    length, branch, tokens, alpha_attn, alpha_mlp, cotangent, up_gate, own_down, up_scale, gate_scale,
    mixed, branch_low, token_grad, alpha_grads, weight_grads, scale_grads,
    hidden, hidden_grad, held, grads, ups, gates, inner, up_low, gate_low, own, cross, side,
    gather_send, gather_receive, cross_sem, side_sem, down, down_send, down_receive, down_local,
):
    x, z, y, c = here("x", "z", "y", "c")
    rows, width = branch.shape
    owners, units = length, own_down.shape[0]
    full = owners * units
    q0 = x * 2 + y
    greet(plane_neighbours() + [(z > 0, {"z": z - 1}), (z < length - 1, {"z": z + 1})])
    line = LineGather(length, own_down, down, down_send, down_receive, down_local)
    line.stage(0)
    done = []

    def each_chunk(body):
        def step(i, carry):
            start = pl.multiple_of(i * CHUNK, CHUNK)
            body(pl.ds(start, CHUNK), pl.ds(pl.multiple_of(c * rows + start, CHUNK), CHUNK))
            return carry

        lax.fori_loop(0, rows // CHUNK, step, 0)

    def each_half(body):
        def step(i, carry):
            body(pl.ds(pl.multiple_of(i * rows, rows), rows))
            return carry

        lax.fori_loop(0, 2, step, 0)

    def weight(i):
        return up_gate[:, i, :units].reshape(full, width)

    def down_weight():
        return down[...].reshape(full, width)

    def half_rows(half):
        return pl.ds(pl.multiple_of(half * rows, rows), rows)

    alpha_grads[...] = jnp.zeros_like(alpha_grads)
    scale_grads[...] = jnp.zeros_like(scale_grads)

    def enter(part, place):
        result = step_forward(branch[part], tokens[part].astype(f32), alpha_attn[...])[0]
        hidden[part] = result
        held[q0, place] = result.astype(bf16)

    each_chunk(enter)

    def forward(q):
        def half(part):
            block = held[q, part]
            up = dot(block, weight(0), 1, 1)
            gate = dot(block, weight(1), 1, 1)
            ups[q, part] = up
            gates[q, part] = gate
            gated = gate * gate_scale[...]
            inner[q, part] = (up * up_scale[...] * (gated * jax.nn.sigmoid(gated))).astype(bf16)

        each_half(half)
        done.append(q)
        if len(done) in stages:
            line.stage(stages[len(done)])

    stages = {1: 1, 3: 2}
    plane_gather(held, gather_send.at[0], gather_receive.at[0], forward)
    for stage in range(3, length + 1):
        line.stage(stage)
    plane_scatter(
        lambda q, half: dot(inner[q, half_rows(half)], down_weight(), 1, 0),
        own, cross, side, cross_sem.at[0], side_sem.at[0],
    )

    def turn_back(part, place):
        start, alpha = hidden[part], alpha_mlp[...]
        result, unit, target_scale, moved_scale = step_forward(own[q0, part], start, alpha)
        mixed[part] = result.astype(bf16)
        target_grad, start_grad, alpha_part = step_back(
            cotangent[part].astype(f32), result, unit, target_scale, moved_scale, start, alpha
        )
        alpha_grads[1:2] += jnp.sum(alpha_part, axis=0, keepdims=True)
        hidden_grad[part] = start_grad
        grads[q0, place] = target_grad.astype(bf16)

    each_chunk(turn_back)

    def backward(q):
        def half(part):
            inner_grad = dot(grads[q, part], down_weight(), 1, 1)
            up, gate = ups[q, part], gates[q, part]
            gated = gate * gate_scale[...]
            share = jax.nn.sigmoid(gated)
            silu = gated * share
            lifted = inner_grad * up
            gated_grad = lifted * up_scale[...] * (share * (1.0 + gated * (1.0 - share)))
            up_low[q, part] = (inner_grad * up_scale[...] * silu).astype(bf16)
            gate_low[q, part] = (gated_grad * gate_scale[...]).astype(bf16)
            scale_grads[0:1] += jnp.sum(lifted * silu, axis=0, keepdims=True)
            scale_grads[1:2] += jnp.sum(gated_grad * gate, axis=0, keepdims=True)

        each_half(half)

    plane_gather(grads, gather_send.at[1], gather_receive.at[1], backward)

    def weights_back():
        tall = 4 * 2 * rows
        for i, (left, right) in enumerate(((up_low, held), (gate_low, held), (inner, grads))):

            def step(n, carry):
                columns = pl.ds(pl.multiple_of(n * BLOCK, BLOCK), BLOCK)
                product = dot(
                    left[...].reshape(tall, full), right[:, :, columns].reshape(tall, BLOCK), 0, 0
                )
                weight_grads[:, i, :, columns] = product.astype(bf16).reshape(owners, units, BLOCK)
                return carry

            lax.fori_loop(0, width // BLOCK, step, 0)

    plane_scatter(
        lambda q, half: dot(up_low[q, half_rows(half)], weight(0), 1, 0)
        + dot(gate_low[q, half_rows(half)], weight(1), 1, 0),
        own, cross, side, cross_sem.at[1], side_sem.at[1], weights_back,
    )

    def leave(part, place):
        start, alpha = tokens[part].astype(f32), alpha_attn[...]
        result, unit, target_scale, moved_scale = step_forward(branch[part], start, alpha)
        target_grad, start_grad, alpha_part = step_back(
            hidden_grad[part] + own[q0, part], result, unit, target_scale, moved_scale, start, alpha
        )
        alpha_grads[0:1] += jnp.sum(alpha_part, axis=0, keepdims=True)
        branch_low[part] = target_grad.astype(bf16)
        token_grad[part] = start_grad

    each_chunk(leave)


def mlp(length, branch, tokens, alpha_attn, alpha_mlp, cotangent, up_gate, down, up_scale, gate_scale):
    rows, width = branch.shape
    owners, units = length, down.shape[0]
    full = owners * units
    low, wide = like((rows, width), bf16), like((rows, width), f32)
    scratch = [
        pltpu.VMEM((rows, width), f32),
        pltpu.VMEM((rows, width), f32),
        pltpu.VMEM((4, 2 * rows, width), bf16),
        pltpu.VMEM((4, 2 * rows, width), bf16),
        pltpu.VMEM((4, 2 * rows, full), f32),
        pltpu.VMEM((4, 2 * rows, full), f32),
        pltpu.VMEM((4, 2 * rows, full), bf16),
        pltpu.VMEM((4, 2 * rows, full), bf16),
        pltpu.VMEM((4, 2 * rows, full), bf16),
        pltpu.VMEM((4, rows, width), f32),
        pltpu.VMEM((2, 4, rows, width), bf16),
        pltpu.VMEM((2, 3, rows, width), bf16),
        pltpu.SemaphoreType.DMA((2, 3, 8)),
        pltpu.SemaphoreType.DMA((2, 16)),
        pltpu.SemaphoreType.DMA((2, 2, 4)),
        pltpu.SemaphoreType.DMA((2, 2, 3, 2)),
        pltpu.VMEM((length, *down.shape), bf16),
    ] + line_gather_semaphores(length)
    return remote_call(
        functools.partial(mlp_kernel, length), "mlp", 5,
        (low, low, wide, like((2, width), f32), like((owners, 3, units, width), bf16), like((2, full), f32)),
        (IN_VMEM,) * 6, [IN_VMEM] * 9, scratch,
        branch, tokens, alpha_attn, alpha_mlp, cotangent, up_gate, down, up_scale, gate_scale,
    )


def shards(
    tokens, lengths, w_query, w_key, w_value, s_qk, w_out, up_weight, gate_weight, down_weight,
    s_up, s_gate, alpha_attn, alpha_mlp, cotangent,
):
    outer = lax.axis_size("o")
    own_units = up_weight.shape[0]
    if outer > 1:
        up_weight, gate_weight, down_weight, s_up, s_gate = (
            gather(a, "o") for a in (up_weight, gate_weight, down_weight, s_up, s_gate)
        )
    units = up_weight.shape[0]
    scales = jnp.zeros((2, SCALE_ROWS, up_weight.shape[1]), bf16)
    scales = scales.at[:, 0, :units].set(jnp.stack([s_up, s_gate]))
    up_gate = jnp.concatenate([jnp.stack([up_weight, gate_weight]), scales], axis=1)

    length = lax.axis_size("z")
    own_rows, width = tokens.shape
    rows = 4 * length * own_rows
    cosine, sine = turn_table(lengths[0], rows)
    joint = jnp.concatenate([w_query, w_key, w_value], axis=1).T
    group_tokens, turned_q, turned_k, qt, kt, vt = project(
        length, tokens, joint, s_qk[:, None], cosine, sine
    )
    ot, lse = attention_forward(lengths, qt, kt, vt)
    branch, up_gate = branch_sum(length, ot, w_out, up_gate, own_rows)
    up_scale, gate_scale = (up_gate[:, i, units, :units].reshape(1, -1).astype(f32) for i in range(2))
    mixed, branch_low, token_grad, alpha_grads, mlp_grads, scale_grads = mlp(
        length, branch, tokens, alpha_attn[None], alpha_mlp[None], cotangent, up_gate, down_weight,
        up_scale, gate_scale,
    )
    got, out_grad, mlp_grads = spread(length, branch_low, w_out, ot, mlp_grads)
    gqt, gkt, gvt = attention_backward(lengths, qt, kt, vt, ot, got, lse)
    tokens_grad, attn_grads, alpha_sums, scale_sums, gain_grad = inward(
        length, group_tokens, token_grad, out_grad, alpha_grads, scale_grads,
        gqt, gkt, gvt, turned_q, turned_k, s_qk[:, None], cosine, sine, joint,
    )
    if outer > 1:
        mlp_grads = lax.psum_scatter(mlp_grads, "o", scatter_dimension=1, tiled=True)
        attn_grads, alpha_sums, scale_sums, gain_grad = lax.psum(
            (attn_grads, alpha_sums, scale_sums, gain_grad), "o"
        )
    place = lax.axis_index("z") * units + lax.axis_index("o") * own_units
    scale_sums = lax.dynamic_slice_in_dim(scale_sums, place, own_units, 1)
    return (
        mixed,
        tokens_grad,
        attn_grads[:HEAD_DIM].T,
        attn_grads[HEAD_DIM : 2 * HEAD_DIM].T,
        attn_grads[2 * HEAD_DIM : 3 * HEAD_DIM].T,
        gain_grad[:, 0],
        attn_grads[3 * HEAD_DIM :],
        mlp_grads[0],
        mlp_grads[1],
        mlp_grads[2],
        scale_sums[0],
        scale_sums[1],
        alpha_sums[0],
        alpha_sums[1],
    )


def solution(mesh):
    dp, head = mesh.shape["dp"], mesh.shape["head"]
    fine = Mesh(mesh.devices.reshape(dp // 2, 2, head // 4, 2, 2), AXES)
    group, rows, heads = P(("o", "x"), None), P(AXES, None), P(None, GROUP)
    in_specs = (
        rows, group, heads, heads, heads, P(GROUP), P(GROUP, None), rows, rows, rows,
        P(AXES), P(AXES), P(), P(), rows,
    )
    out_specs = (
        rows, rows, heads, heads, heads, P(GROUP), P(GROUP, None), rows, rows, rows,
        P(AXES), P(AXES), P(), P(),
    )
    return jax.shard_map(
        shards, mesh=fine, in_specs=in_specs, out_specs=out_specs, check_vma=False
    )
```

```python
import functools
import math

import jax
import jax.numpy as jnp
from jax import lax
from jax.experimental import pallas as pl
from jax.experimental.pallas import tpu as pltpu
from jax.sharding import Mesh
from jax.sharding import PartitionSpec as P

HEAD_DIM = 64
BLOCK = 512
REACH = 4
EPSILON = 1e-06
ROOT = math.sqrt(HEAD_DIM)
SCORE_SCALE = math.log2(math.e) / ROOT
AXES = ("o", "x", "z", "y", "c")
GROUP = ("z", "y", "c")
f32, bf16 = jnp.float32, jnp.bfloat16
VMEM_LIMIT = 56 * 2**20


def dot(left, right, left_dim, right_dim):
    return lax.dot_general(
        left, right, (((left_dim,), (right_dim,)), ((), ())), preferred_element_type=f32
    )


def unit_start(lengths, unit):
    start, end = jnp.int32(0), jnp.int32(0)
    for j in range(lengths.shape[1]):
        end = end + lengths[0, j]
        start = jnp.where(unit >= end, end, start)
    return start


def causal(weights):
    key = lax.broadcasted_iota(jnp.int32, weights.shape, 0)
    query = lax.broadcasted_iota(jnp.int32, weights.shape, 1)
    return jnp.where(key <= query, weights, 0.0)


def block_columns(index):
    return pl.ds(pl.multiple_of(index * BLOCK, BLOCK), BLOCK)


def barred(lengths, unit, back):
    return jnp.where(unit - back >= unit_start(lengths, unit), 0.0, 1e30).astype(f32)


def attend(lengths, unit, qt, kt, vt, ot, lse, total, attended):
    columns = block_columns(unit)

    def part(back):
        keys = block_columns(unit - back)
        scores = dot(kt[:, keys], qt[:, columns], 0, 0) * SCORE_SCALE
        if back == 0:
            weights = causal(jnp.exp2(scores))
        else:
            weights = jnp.exp2(scores - barred(lengths, unit, back))
        sums = jnp.sum(weights, axis=0, keepdims=True)
        values = dot(vt[:, keys], weights.astype(bf16), 1, 0)
        if back == 0:
            total[...] = sums
            attended[...] = values
        else:
            total[...] += sums
            attended[...] += values

    part(0)
    for back in range(1, REACH):
        pl.when(unit >= back)(functools.partial(part, back))
    ot[:, columns] = (attended[...] * (1.0 / total[...])).astype(bf16)
    lse[:, columns] = jnp.log2(total[...])


def attend_back(lengths, unit, qt, kt, vt, ot, got, lse, gqt, gkt, gvt):
    columns = block_columns(unit)
    query, grad = qt[:, columns], got[:, columns]
    inner = jnp.sum(grad.astype(f32) * ot[:, columns].astype(f32), axis=0, keepdims=True)

    def part(back):
        keys = block_columns(unit - back)
        key, value = kt[:, keys], vt[:, keys]
        log_total = lse[:, columns]
        if back > 0:
            log_total = log_total + barred(lengths, unit, back)
        weights = jnp.exp2(dot(key, query, 0, 0) * SCORE_SCALE - log_total)
        if back == 0:
            weights = causal(weights)
        score_grad = (weights * (dot(value, grad, 0, 0) - inner)).astype(bf16)
        gkt[:, keys] += dot(query, score_grad, 1, 1)
        gvt[:, keys] += dot(grad, weights.astype(bf16), 1, 1)
        gqt[:, columns] += dot(key, score_grad, 1, 0)

    part(0)
    for back in range(1, REACH):
        pl.when(unit >= back)(functools.partial(part, back))


def turn_table(lengths_row, rows):
    ends = jnp.sum(jnp.where(jnp.tri(lengths_row.shape[0], dtype=bool), lengths_row[None, :], 0), 1)
    row = jnp.arange(rows, dtype=jnp.int32)
    passed = (row // BLOCK)[None, :] >= ends[:, None]
    place = row - BLOCK * jnp.max(jnp.where(passed, ends[:, None], 0), axis=0)
    half = HEAD_DIM // 2
    frequency = jnp.exp(jnp.arange(half, dtype=f32) * (-2.0 * math.log(10000.0) / HEAD_DIM))
    angle = place.astype(f32)[None, :] * frequency[:, None]
    return jnp.cos(angle), jnp.sin(angle)


def turn(values, cosine, sine):
    half = HEAD_DIM // 2
    a, b = values[:half], values[half:]
    return jnp.concatenate([a * cosine - b * sine, b * cosine + a * sine], axis=0)


def unit_features(turned):
    scale = lax.rsqrt(jnp.mean(turned * turned, axis=0, keepdims=True) + EPSILON)
    return turned * scale, scale


def gather(values, axes):
    return lax.all_gather(values, axes, axis=0, tiled=True)


MESH_ID = pl.DeviceIdType.MESH


def here(*names):
    return tuple(lax.axis_index(name) for name in names)


def greet(neighbours):
    barrier = pltpu.get_barrier_semaphore()
    count = jnp.int32(0)
    for condition, device in neighbours:

        @pl.when(condition)
        def _():
            pl.semaphore_signal(barrier, inc=1, device_id=device, device_id_type=MESH_ID)

        count = count + jnp.where(condition, 1, 0)
    pl.semaphore_wait(barrier, count)


def remote(source, target, send, receive, device):
    return pltpu.make_async_remote_copy(
        src_ref=source,
        dst_ref=target,
        send_sem=send,
        recv_sem=receive,
        device_id=device,
        device_id_type=MESH_ID,
    )


def line_order(z, length, step):
    picked = jnp.int32(0)
    for at in range(length):
        order = sorted(range(length), key=lambda p: (abs(p - at), p))
        picked = jnp.where(z == at, order[step], picked)
    return picked


def group_neighbours(length):
    z, y, c = here("z", "y", "c")
    return [
        (z > 0, {"z": z - 1}),
        (z < length - 1, {"z": z + 1}),
        (z >= 0, {"y": 1 - y}),
        (z >= 0, {"c": 1 - c}),
    ]


def group_gather(length, own, held, send, receive, on_unit, at_step=None):
    z, y, c = here("z", "y", "c")
    rows = held.shape[1] // 2
    half = rows // 2

    def copy(kind, zz, yy, cc, h, device):
        at = held.at[zz * 2 + yy, pl.ds(pl.multiple_of(cc * rows + h * half, half), half)]
        number = ((zz * 2 + yy) * 2 + cc) * 2 + h
        return remote(at, at, send.at[kind, number], receive.at[number], device)

    def arrived(zz, yy, cc, h):
        copy(3, zz, yy, cc, h, {"c": 1 - c}).wait_recv()

    def come(distance):
        if distance == 0:
            return [(z, z >= 0, [(0, z < length - 1, {"z": z + 1}), (1, z > 0, {"z": z - 1})])]
        return [
            (z - distance, z >= distance, [(0, z < length - 1, {"z": z + 1})]),
            (z + distance, z + distance < length, [(1, z > 0, {"z": z - 1})]),
        ]

    def passed_on(zz, h, along, act):
        for kind, goes, device in along:

            @pl.when(goes)
            def _():
                act(copy(kind, zz, y, c, h, device))

        act(copy(2, zz, y, c, h, {"y": 1 - y}))
        act(copy(3, zz, y, c, h, {"c": 1 - c}))

    held[z * 2 + y, pl.ds(pl.multiple_of(c * rows, rows), rows)] = own[...]
    order = [line_order(z, length, step) for step in range(length)]
    for tick in range(2 * length + 1):
        step, h = divmod(tick, 2)
        before, last_h = divmod(tick - 1, 2)
        if step < length:
            for zz, there, along in come(step):

                @pl.when(there)
                def _():
                    if step > 0:
                        arrived(zz, y, c, h)
                    passed_on(zz, h, along, lambda copy_: copy_.start())

        if before >= 0:
            arrived(order[before], 1 - y, c, last_h)
            copy(3, order[before], 1 - y, c, last_h, {"c": 1 - c}).start()
        if at_step is not None and h == 0:
            at_step(step)
        if h == 1:
            for i in (0, 1):
                arrived(order[step], y, 1 - c, i)
            on_unit(order[step] * 2 + y)
        if last_h == 1 and before >= 0:
            for i in (0, 1):
                arrived(order[before], 1 - y, 1 - c, i)
            on_unit(order[before] * 2 + 1 - y)
    for h in (0, 1):
        for step in range(length):
            for zz, there, along in come(step):

                @pl.when(there)
                def _():
                    passed_on(zz, h, along, lambda copy_: copy_.wait_send())

            copy(3, order[step], 1 - y, c, h, {"c": 1 - c}).wait_send()


GATHER_SEMAPHORES = 4


def gather_scratch(units, rows, width):
    return [
        pltpu.VMEM((units, 2 * rows, width), bf16),
        pltpu.SemaphoreType.DMA((GATHER_SEMAPHORES, 4 * units)),
        pltpu.SemaphoreType.DMA((4 * units,)),
    ]


def scatter_scratch(length, rows, width):
    return [
        pltpu.VMEM((2 * length, rows, width), f32),
        pltpu.VMEM((2, 2 * length, rows, width), bf16),
        pltpu.VMEM((2, length, rows, width), bf16),
        pltpu.VMEM((3, length, rows, width), bf16),
        pltpu.SemaphoreType.DMA((2, 2 * length)),
        pltpu.SemaphoreType.DMA((2, length, 2)),
        pltpu.SemaphoreType.DMA((3, length, 2)),
    ]


def group_scatter(length, produce, finish, own, cross, across, along, cross_sem, across_sem, along_sem, prepare=None, between=None, at_step=None):
    z, y, c = here("z", "y", "c")

    def to_core(unit):
        return remote(cross.at[0, unit], cross.at[1, unit], cross_sem.at[0, unit], cross_sem.at[1, unit], {"c": 1 - c})

    half = own.shape[1] // 2

    def part(h):
        return pl.ds(h * half, half)

    def to_y(zz, h):
        return remote(
            across.at[0, zz, part(h)], across.at[1, zz, part(h)], across_sem.at[0, zz, h],
            across_sem.at[1, zz, h], {"y": 1 - y},
        )

    def to_z(zz, slot, h, device):
        return remote(
            along.at[0, zz, part(h)], along.at[slot, zz, part(h)], along_sem.at[0, zz, h],
            along_sem.at[slot, zz, h], device,
        )

    def from_z(zz, slot, h):
        to_z(zz, slot, h, {"c": 1 - c}).wait_recv()
        return along[slot, zz, part(h)].astype(f32)

    order = [line_order(z, length, length - 1 - step) for step in range(length)]

    def give(unit):
        cross[0, unit] = produce(unit, 1 - c).astype(bf16)
        to_core(unit).start()

    def first(zz):
        there, here_ = zz * 2 + 1 - y, zz * 2 + y
        if prepare is not None:
            prepare(there)
        give(there)
        own[there] = produce(there, c)
        if prepare is not None:
            prepare(here_)
        to_core(there).wait_recv()
        across[0, zz] = (own[there] + cross[1, there].astype(f32)).astype(bf16)
        for h in (0, 1):
            to_y(zz, h).start()
        give(here_)
        own[here_] = produce(here_, c)

    def third(zz, h, last):
        unit = zz * 2 + y
        if h == 0:
            to_core(unit).wait_recv()
        own[unit, part(h)] += cross[1, unit, part(h)].astype(f32)
        to_y(zz, h).wait_recv()
        own[unit, part(h)] += across[1, zz, part(h)].astype(f32)

        @pl.when((zz >= z) & (z > 0))
        def _():
            own[unit, part(h)] += from_z(zz, 1, h)

        @pl.when((zz <= z) & (z < length - 1))
        def _():
            own[unit, part(h)] += from_z(zz, 2, h)

        if last:
            finish(h, own[unit, part(h)])
            return
        along[0, zz, part(h)] = own[unit, part(h)].astype(bf16)

        @pl.when(zz > z)
        def _():
            to_z(zz, 1, h, {"z": z + 1}).start()

        @pl.when(zz < z)
        def _():
            to_z(zz, 2, h, {"z": z - 1}).start()

    for step in range(length + 1):
        if step < length:
            first(order[step])
        if at_step is not None:
            at_step(step)
        if step == length - 1 and between is not None:
            between()
        if step >= 1:
            for h in (0, 1):
                third(order[step - 1], h, step == length)
    for step in range(length):
        zz = order[step]
        for yy in (0, 1):
            to_core(zz * 2 + yy).wait_send()
        for h in (0, 1):
            to_y(zz, h).wait_send()
            if step < length - 1:
                to_z(zz, 1, h, {"c": 1 - c}).wait_send()


def remote_call(kernel, name, number, outs, out_specs, in_specs, scratch, *operands, aliases={}):
    return pl.pallas_call(
        kernel,
        name=name,
        out_shape=outs,
        in_specs=in_specs,
        out_specs=out_specs,
        scratch_shapes=scratch,
        input_output_aliases=aliases,
        compiler_params=pltpu.CompilerParams(
            collective_id=number, has_side_effects=True, vmem_limit_bytes=VMEM_LIMIT
        ),
    )(*operands)


IN_VMEM = pl.BlockSpec(memory_space=pltpu.VMEM)
IN_SMEM = pl.BlockSpec(memory_space=pltpu.SMEM)
ANYWHERE = pl.BlockSpec(memory_space=pl.ANY)


def like(shape, dtype):
    return jax.ShapeDtypeStruct(shape, dtype)


class LineGather:
    def __init__(self, length, own, held, send, receive, local_sem):
        self.length, self.own, self.held = length, own, held
        self.sems, self.local_sem = (send, receive), local_sem
        self.z = lax.axis_index("z")

    def copy(self, way, zz, source=None):
        send, receive = self.sems
        at = self.held.at[zz]
        device = {"z": self.z + 1} if way == 0 else {"z": self.z - 1}
        return remote(at if source is None else source, at, send.at[way, zz], receive.at[zz], device)

    def ways(self, d, act):
        z, length = self.z, self.length
        for way, zz, there, more in (
            (0, z - d, z - d >= 0, z < length - 1),
            (1, z + d, z + d < length, z > 0),
        ):
            act(way, zz, there, there & more)

    def start(self):
        pltpu.make_async_copy(self.own, self.held.at[self.z], self.local_sem).start()
        self.hand_on(0)

    def hand_on(self, d):
        def begin(way, zz, there, more):
            @pl.when(more)
            def _():
                self.copy(way, zz, self.own if d == 0 else None).start()

        self.ways(d, begin)

    def wait(self, d):
        def arrive(way, zz, there, more):
            @pl.when(there)
            def _():
                self.arrival(way, zz).wait_recv()

        self.ways(d, arrive)

    def sent(self, d):
        def leave(way, zz, there, more):
            @pl.when(more)
            def _():
                self.copy(way, zz, self.own if d == 0 else None).wait_send()

        self.ways(d, leave)
        if d == 0:
            pltpu.make_async_copy(self.own, self.held.at[self.z], self.local_sem).wait()

    def arrival(self, way, zz):
        send, receive = self.sems
        at = self.held.at[zz]
        return remote(at, at, send.at[way, zz], receive.at[zz], {"c": 1 - lax.axis_index("c")})


def line_gather_semaphores(length):
    return [
        pltpu.SemaphoreType.DMA((2, length)),
        pltpu.SemaphoreType.DMA((length,)),
        pltpu.SemaphoreType.DMA,
    ]


class LineScatter:
    def __init__(self, length, parts, rest, out, into, send_sem, receive_sem):
        self.length, self.parts, self.rest = length, parts, rest
        self.out, self.into, self.sems = out, into, (send_sem, receive_sem)
        self.z = lax.axis_index("z")

    def copy(self, way, d, source):
        send, receive = self.sems
        device = {"z": self.z + 1} if way == 0 else {"z": self.z - 1}
        return remote(source, self.into.at[way, d - 2], send.at[way, d - 2], receive.at[way, d - 2], device)

    def arrived(self, way, d):
        send, receive = self.sems
        at = self.into.at[way, d - 2]
        device = {"c": 1 - lax.axis_index("c")}
        remote(at, at, send.at[way, d - 2], receive.at[way, d - 2], device).wait_recv()

    def cases(self, d, alone, joined):
        z, length = self.z, self.length
        for way, dest, valid, behind in (
            (0, z + d, z + d < length, z > 0),
            (1, z - d, z - d >= 0, z < length - 1),
        ):
            behind = behind if d < length - 1 else z < 0
            pl.when(valid & jnp.logical_not(behind))(functools.partial(alone, way, dest))
            pl.when(valid & behind)(functools.partial(joined, way, dest))

    def joint(self, way, dest, d):
        self.arrived(way, d + 1)
        return (self.parts[dest].astype(f32) + self.into[way, d - 1].astype(f32)).astype(bf16)

    def send(self, d):
        def alone(way, dest):
            self.copy(way, d, self.parts.at[dest]).start()

        def joined(way, dest):
            self.out[way, d - 2] = self.joint(way, dest, d)
            self.copy(way, d, self.out.at[way, d - 2]).start()

        self.cases(d, alone, joined)

    def finish(self):
        def alone(way, dest):
            self.rest[way] = self.parts[dest]

        def joined(way, dest):
            self.rest[way] = self.joint(way, dest, 1)

        self.cases(1, alone, joined)
        self.rest[2] = self.parts[self.z]
        for d in range(2, self.length):

            def left(way, dest):
                self.copy(way, d, self.out.at[way, d - 2]).wait_send()

            self.cases(d, left, left)


def line_scatter_scratch(parts):
    length = parts.shape[0]
    hops = (2, length - 2, *parts.shape[1:])
    return [pltpu.VMEM(hops, bf16), pltpu.VMEM(hops, bf16)] + [pltpu.SemaphoreType.DMA(hops[:2])] * 2


def project_kernel(
    length, tokens, joint, gain, cosine, sine, weight, gathered, turned_q, turned_k, qt, kt, vt, weights,
    held, send, receive, out_sem, line_send, line_receive, line_local,
):
    greet(group_neighbours(length))
    line = LineGather(length, weight, weights, line_send, line_receive, line_local)

    def at_step(step):
        if step == length - 1:
            line.start()

    def on_unit(unit):
        copy = pltpu.make_async_copy(held.at[unit], gathered.at[unit], out_sem.at[unit])
        copy.start()
        columns = block_columns(unit)
        projected = dot(joint[...], held[unit], 1, 1)
        for part, turned, features in ((0, turned_q, qt), (1, turned_k, kt)):
            values = turn(
                projected[part * HEAD_DIM : (part + 1) * HEAD_DIM], cosine[:, columns], sine[:, columns]
            )
            turned[:, columns] = values
            features[:, columns] = (unit_features(values)[0] * gain[...]).astype(bf16)
        vt[:, columns] = projected[2 * HEAD_DIM :].astype(bf16)

    group_gather(length, tokens, held, send, receive, on_unit, at_step)
    line.wait(1)
    line.sent(0)
    for unit in range(2 * length):
        pltpu.make_async_copy(held.at[unit], gathered.at[unit], out_sem.at[unit]).wait()


def project(length, tokens, joint, gain, cosine, sine, weight):
    rows, width = tokens.shape
    units = 2 * length
    total = units * 2 * rows
    wide, narrow = like((HEAD_DIM, total), f32), like((HEAD_DIM, total), bf16)
    return remote_call(
        functools.partial(project_kernel, length), "project", 1,
        (
            like((units, 2 * rows, width), bf16), wide, wide, narrow, narrow, narrow,
            like((length, *weight.shape), bf16),
        ),
        (ANYWHERE,) + (IN_VMEM,) * 5 + (ANYWHERE,), [IN_VMEM] * 5 + [ANYWHERE],
        gather_scratch(units, rows, width) + [pltpu.SemaphoreType.DMA((units,))]
        + line_gather_semaphores(length),
        tokens, joint, gain, cosine, sine, weight,
    )


def half_columns(unit, half):
    rows = BLOCK // 2
    return pl.ds(pl.multiple_of(unit * BLOCK + half * rows, rows), rows)


def branch_kernel(
    length, lengths, qt, kt, vt, w_out, weight, before, branch, weights, ot, lse, total, attended,
    send, receive, local_sem, *scratch,
):
    greet(group_neighbours(length))
    line = LineGather(length, weight, weights, send, receive, local_sem)
    line.hand_on(1)

    def at_step(step):
        if 2 <= step < length - 1:
            line.wait(step)
            line.hand_on(step)

    def finish(h, total):
        branch[pl.ds(h * total.shape[0], total.shape[0])] = total

    group_scatter(
        length, lambda unit, half: dot(ot[:, half_columns(unit, half)], w_out[...], 0, 0), finish, *scratch,
        prepare=lambda unit: attend(lengths, unit, qt, kt, vt, ot, lse, total, attended), at_step=at_step,
    )
    line.wait(length - 1)
    for d in range(1, length - 1):
        line.sent(d)


def branch_sum(length, lengths, qt, kt, vt, w_out, weight, weights, rows):
    width = w_out.shape[1]
    return remote_call(
        functools.partial(branch_kernel, length), "branch_sum", 2,
        (
            like((rows, width), f32), like(weights.shape, bf16), like(qt.shape, bf16),
            like((1, qt.shape[1]), f32),
        ),
        (IN_VMEM, ANYWHERE, IN_VMEM, IN_VMEM), [IN_SMEM] + [IN_VMEM] * 4 + [ANYWHERE] * 2,
        [pltpu.VMEM((1, BLOCK), f32), pltpu.VMEM((HEAD_DIM, BLOCK), f32)]
        + line_gather_semaphores(length) + scatter_scratch(length, rows, width),
        lengths, qt, kt, vt, w_out, weight, weights, aliases={6: 1},
    )


def spread_kernel(
    length, lengths, grad, w_out, qt, kt, vt, ot, lse, parts, out_grad, rest, gqt, gkt, gvt,
    got, held, send, receive, *scratch,
):
    greet(group_neighbours(length))
    line = LineScatter(length, parts, rest, *scratch)

    def at_step(step):
        if step == 0:
            for array in (out_grad, gqt, gkt, gvt):
                array[...] = jnp.zeros_like(array)
        if step % 2 == 0 and step < 2 * (length - 2):
            line.send(length - 1 - step // 2)

    def on_unit(unit):
        columns = block_columns(unit)
        got[:, columns] = dot(w_out[...], held[unit], 1, 1).astype(bf16)
        out_grad[...] += dot(ot[:, columns], held[unit], 1, 0)
        attend_back(lengths, unit, qt, kt, vt, ot, got, lse, gqt, gkt, gvt)

    group_gather(length, grad, held, send, receive, on_unit, at_step)
    line.finish()


def spread(length, lengths, grad, w_out, qt, kt, vt, ot, lse, parts):
    rows, width = grad.shape
    _, count, units, _ = parts.shape
    wide = like(ot.shape, f32)
    return remote_call(
        functools.partial(spread_kernel, length), "spread", 3,
        (like(w_out.shape, f32), like((3, count, units, width), bf16), wide, wide, wide), (IN_VMEM,) * 5,
        [IN_SMEM] + [IN_VMEM] * 8,
        [pltpu.VMEM(ot.shape, bf16)] + gather_scratch(2 * length, rows, width)
        + line_scatter_scratch(parts),
        lengths, grad, w_out, qt, kt, vt, ot, lse, parts,
    )


def flip(position, bit):
    return position + bit - 2 * bit * ((position // bit) % 2)


def inward_kernel(
    length, gqt, gkt, gvt, turned_q, turned_k, gain, cosine, sine, joint, gathered, out_grad, alpha_grads,
    scale_grads, direct, rest, token_grad, weight_grads, alpha_sums, scale_sums, gain_grad, sums,
    arrivals, line_sem, grads, held, held_sem, gains, gain_sem, sent, taken, weight_sem, small_out, small_in, small_sem,
    *scratch,
):
    x, z, y, c = here("x", "z", "y", "c")
    to_x = {"x": 1 - x}
    bits = [1 << i for i in range(length.bit_length() - 1)]
    greet(group_neighbours(length) + [(x >= 0, to_x)] + [(x >= 0, {"z": flip(z, bit)}) for bit in bits])
    partners = [{"c": 1 - c}, {"y": 1 - y}, to_x] + [{"z": flip(z, bit)} for bit in bits]
    load = pltpu.make_async_copy(gathered, held, held_sem)
    load.start()
    gains[0] = jnp.zeros_like(gains[0])
    small_out[0] = jnp.zeros_like(small_out[0])
    small_out[0, 0:2] = alpha_grads[...]
    small_out[0, 2:4, : scale_grads.shape[1]] = scale_grads[...]

    def exchange(i):
        return remote(small_out.at[i], small_in.at[i], small_sem.at[0, i], small_sem.at[1, i], partners[i])

    lines = [
        (remote(rest.at[way], arrivals.at[way], line_sem.at[0, way], line_sem.at[1, way], {"z": to}), goes, comes)
        for way, to, goes, comes in (
            (0, z + 1, z < length - 1, z > 0), (1, z - 1, z > 0, z < length - 1)
        )
    ]
    for line, goes, _ in lines:
        pl.when(goes)(line.start)

    def at_step(step):
        if 0 < step <= len(partners):
            exchange(step - 1).wait_recv()
            small_out[step] = small_out[step - 1]
            summed = 2 if step <= 3 else 4
            small_out[step, :summed] += small_in[step - 1, :summed]
        if step < len(partners):
            exchange(step).start()

    def prepare(unit):
        columns = block_columns(unit)
        for part, turned, outer in ((0, turned_q, gqt), (1, turned_k, gkt)):
            normal, scale = unit_features(turned[:, columns])
            grad = outer[:, columns] * (1.0 / ROOT)
            product = grad * normal
            width = gains.shape[2]
            for i in range(BLOCK // width):
                gains[0] += product[:, i * width : (i + 1) * width]
            grad = grad * gain[...]
            grad = scale * (grad - normal * jnp.mean(grad * normal, axis=0, keepdims=True))
            grad = turn(grad, cosine[:, columns], -sine[:, columns])
            grads[part * HEAD_DIM : (part + 1) * HEAD_DIM, columns] = grad.astype(bf16)
        grads[2 * HEAD_DIM :, columns] = gvt[:, columns].astype(bf16)

    gain_copy = remote(gains.at[0], gains.at[1], gain_sem.at[0], gain_sem.at[1], to_x)
    weight_copy = remote(sent, taken, weight_sem.at[0], weight_sem.at[1], to_x)

    def between():
        gain_copy.start()
        load.wait()
        rows = grads.shape[1]
        product = dot(grads[...], held[...].reshape(rows, held.shape[2]), 1, 0)
        sent[: 3 * HEAD_DIM] = product.astype(bf16)
        sent[3 * HEAD_DIM :] = out_grad[...].astype(bf16)
        weight_copy.start()

    def finish(h, total):
        part = pl.ds(h * total.shape[0], total.shape[0])
        token_grad[part] = (direct[part] + total).astype(bf16)

    group_scatter(
        length, lambda unit, half: dot(grads[:, half_columns(unit, half)], joint[...], 0, 0), finish, *scratch,
        prepare=prepare, between=between, at_step=at_step,
    )
    for step in range(length + 1, len(partners) + 1):
        at_step(step)
    alpha_sums[...] = small_out[len(partners), 0:2]
    scale_sums[...] = small_out[len(partners), 2:4, : scale_sums.shape[1]]
    sums[...] = rest[2].astype(f32)
    for way, (line, goes, comes) in enumerate(lines):

        @pl.when(comes)
        def _():
            remote(
                arrivals.at[way], arrivals.at[way], line_sem.at[0, way], line_sem.at[1, way], {"c": 1 - c}
            ).wait_recv()
            sums[...] += arrivals[way].astype(f32)

        pl.when(goes)(line.wait_send)
    gain_copy.wait()
    gain_grad[...] = jnp.sum(gains[0] + gains[1], axis=1, keepdims=True)
    weight_copy.wait()
    weight_grads[...] = sent[...].astype(f32) + taken[...].astype(f32)
    for i in range(len(partners)):
        exchange(i).wait_send()


def inward(length, gathered, direct, out_grad, alpha_grads, scale_grads, rest, *operands):
    rows, width = direct.shape
    units, block, _ = gathered.shape
    exchanges = 3 + length.bit_length() - 1
    small = (exchanges + 1, 4, width)
    weights = (4 * HEAD_DIM, width)
    scratch = [
        pltpu.VMEM((3 * HEAD_DIM, units * block), bf16),
        pltpu.VMEM(gathered.shape, bf16),
        pltpu.SemaphoreType.DMA,
        pltpu.VMEM((2, HEAD_DIM, 128), f32),
        pltpu.SemaphoreType.DMA((2,)),
        pltpu.VMEM(weights, bf16),
        pltpu.VMEM(weights, bf16),
        pltpu.SemaphoreType.DMA((2,)),
        pltpu.VMEM(small, f32),
        pltpu.VMEM(small, f32),
        pltpu.SemaphoreType.DMA((2, exchanges)),
    ]
    return remote_call(
        functools.partial(inward_kernel, length), "inward", 4,
        (
            like((rows, width), bf16), like(weights, f32), like(alpha_grads.shape, f32),
            like(scale_grads.shape, f32), like((HEAD_DIM, 1), f32), like(rest.shape[1:], f32),
        ),
        (IN_VMEM,) * 6, [IN_VMEM] * 9 + [ANYWHERE] + [IN_VMEM] * 5,
        [pltpu.VMEM((2, *rest.shape[1:]), bf16), pltpu.SemaphoreType.DMA((2, 2))] + scratch
        + scatter_scratch(length, rows, width),
        *operands, gathered, out_grad, alpha_grads, scale_grads, direct, rest,
    )


def plane_neighbours():
    x, y, c = here("x", "y", "c")
    return [(x >= 0, {"x": 1 - x}), (x >= 0, {"y": 1 - y}), (x >= 0, {"c": 1 - c})]


def plane_gather(held, send, receive, make_half, on_pair, before_corner):
    x, y, c = here("x", "y", "c")
    rows = held.shape[1] // 2
    half = rows // 2
    q0, qx, qy, qd = x * 2 + y, (1 - x) * 2 + y, x * 2 + 1 - y, (1 - x) * 2 + 1 - y
    to_x, to_y, to_c = (0, {"x": 1 - x}), (1, {"y": 1 - y}), (2, {"c": 1 - c})

    def copy(way, q, cc, h):
        at = held.at[q, pl.ds(pl.multiple_of(cc * rows + h * half, half), half)]
        return remote(at, at, send.at[way[0], q * 2 + h], receive.at[(q * 2 + cc) * 2 + h], way[1])

    def arrived(q, cc, h):
        copy(to_c, q, cc, h).wait_recv()

    sent = []

    def start(way, q, h):
        sent.append((way, q, h))
        copy(way, q, c, h).start()

    for h in (0, 1):
        make_half(h)
        for way in (to_x, to_y, to_c):
            start(way, q0, h)
    for h in (0, 1):
        arrived(q0, 1 - c, h)
    on_pair(q0)
    arrived(qx, c, 0)
    start(to_y, qx, 0)
    start(to_c, qx, 0)
    arrived(qy, c, 0)
    start(to_c, qy, 0)
    arrived(qy, c, 1)
    start(to_x, qy, 1)
    start(to_c, qy, 1)
    arrived(qx, c, 1)
    start(to_c, qx, 1)
    for q in (qx, qy):
        for h in (0, 1):
            arrived(q, 1 - c, h)
        on_pair(q)
    before_corner()
    for h in (0, 1):
        arrived(qd, c, h)
        start(to_c, qd, h)
    for h in (0, 1):
        arrived(qd, 1 - c, h)
    on_pair(qd)
    for way, q, h in sent:
        copy(way, q, c, h).wait_send()


class PlaneScatter:
    def __init__(self, produce, own, cross, side, cross_sem, side_sem):
        self.produce, self.own, self.cross, self.side = produce, own, cross, side
        self.cross_sem, self.side_sem = cross_sem, side_sem
        x, y, self.c = here("x", "y", "c")
        self.half = own.shape[1] // 2
        self.chips = x * 2 + y, (1 - x) * 2 + y, x * 2 + 1 - y, (1 - x) * 2 + 1 - y
        self.to_x, self.to_y = {"x": 1 - x}, {"y": 1 - y}

    def to_core(self, q):
        cross, sem = self.cross, self.cross_sem
        return remote(cross.at[0, q], cross.at[1, q], sem.at[0, q], sem.at[1, q], {"c": 1 - self.c})

    def part(self, h):
        return pl.ds(h * self.half, self.half)

    def beside(self, kind, h, device):
        side, sem, part = self.side, self.side_sem, self.part(h)
        return remote(
            side.at[0, kind, part], side.at[1, kind, part], sem.at[0, kind, h], sem.at[1, kind, h], device
        )

    def first(self, q):
        self.cross[0, q] = self.produce(q, 1 - self.c).astype(bf16)
        self.to_core(q).start()
        self.own[q] = self.produce(q, self.c)

    def joined(self, q):
        self.to_core(q).wait_recv()
        self.own[q] += self.cross[1, q].astype(f32)

    def send(self, kind, q, h, device):
        self.side[0, kind, self.part(h)] = self.own[q, self.part(h)].astype(bf16)
        self.beside(kind, h, device).start()

    def add(self, q, kind, h, device):
        self.beside(kind, h, device).wait_recv()
        self.own[q, self.part(h)] += self.side[1, kind, self.part(h)].astype(f32)

    def begin(self):
        q0, qx, qy, qd = self.chips
        self.first(qx)
        self.first(qy)
        self.joined(qx)
        self.send(1, qx, 0, self.to_x)
        self.joined(qy)
        self.send(2, qy, 1, self.to_y)

    def end(self, between=None):
        q0, qx, qy, qd = self.chips
        to_x, to_y = self.to_x, self.to_y
        self.first(qd)
        self.joined(qd)
        self.send(0, qd, 0, to_x)
        self.send(0, qd, 1, to_y)
        self.first(q0)
        self.add(qx, 0, 1, to_y)
        self.send(1, qx, 1, to_x)
        self.add(qy, 0, 0, to_x)
        self.send(2, qy, 0, to_y)
        self.joined(q0)
        if between is not None:
            between()
        self.add(q0, 1, 0, to_x)
        self.add(q0, 2, 1, to_y)
        self.add(q0, 2, 0, to_y)
        self.add(q0, 1, 1, to_x)
        for q in self.chips:
            self.to_core(q).wait_send()
        self.beside(0, 0, to_x).wait_send()
        self.beside(0, 1, to_y).wait_send()
        for h in (0, 1):
            self.beside(1, h, to_x).wait_send()
            self.beside(2, h, to_y).wait_send()


def mean_of(values):
    return jnp.mean(values, axis=-1, keepdims=True)


def scale_of(values):
    return lax.rsqrt(mean_of(values * values) + EPSILON)


def step_forward(target, start, alpha):
    target_scale = scale_of(target)
    unit = target * target_scale
    moved = start + alpha * (unit - start)
    moved_scale = scale_of(moved)
    return moved * moved_scale, unit, target_scale, moved_scale


def step_back(grad, result, unit, target_scale, moved_scale, start, alpha):
    moved_grad = moved_scale * (grad - result * mean_of(grad * result))
    unit_grad = alpha * moved_grad
    target_grad = target_scale * (unit_grad - unit * mean_of(unit_grad * unit))
    return target_grad, moved_grad - unit_grad, moved_grad * (unit - start)


CHUNK = 32
SCALE_ROWS = 16


def mlp_kernel(
    length, branch, tokens, alpha_attn, alpha_mlp, cotangent, up_gate, own_down, up_scale, gate_scale,
    mixed, branch_low, token_grad, alpha_grads, weight_grads, scale_grads,
    hidden, hidden_grad, held, grads, ups, gates, inner, up_low, gate_low, own, cross, side,
    gather_send, gather_receive, cross_sem, side_sem, down, down_send, down_receive, down_local,
):
    x, z, y, c = here("x", "z", "y", "c")
    rows, width = branch.shape
    owners, units = length, own_down.shape[0]
    full = owners * units
    q0 = x * 2 + y
    greet(plane_neighbours() + [(z > 0, {"z": z - 1}), (z < length - 1, {"z": z + 1})])
    line = LineGather(length, own_down, down, down_send, down_receive, down_local)
    line.start()
    done = []

    def each_chunk(body, h):
        def step(i, carry):
            start = pl.multiple_of(i * CHUNK, CHUNK)
            body(pl.ds(start, CHUNK), pl.ds(pl.multiple_of(c * rows + start, CHUNK), CHUNK))
            return carry

        chunks = rows // CHUNK // 2
        lax.fori_loop(h * chunks, (h + 1) * chunks, step, 0)

    def each_half(body):
        def step(i, carry):
            body(pl.ds(pl.multiple_of(i * rows, rows), rows))
            return carry

        lax.fori_loop(0, 2, step, 0)

    def weight(i):
        return up_gate[:, i, :units].reshape(full, width)

    def down_weight():
        return down[...].reshape(full, width)

    def half_rows(half):
        return pl.ds(pl.multiple_of(half * rows, rows), rows)

    alpha_grads[...] = jnp.zeros_like(alpha_grads)
    scale_grads[...] = jnp.zeros_like(scale_grads)

    def enter(part, place):
        result = step_forward(branch[part], tokens[part].astype(f32), alpha_attn[...])[0]
        hidden[part] = result
        held[q0, place] = result.astype(bf16)

    def forward(q):
        def half(part):
            block = held[q, part]
            up = dot(block, weight(0), 1, 1)
            gate = dot(block, weight(1), 1, 1)
            ups[q, part] = up
            gates[q, part] = gate
            gated = gate * gate_scale[...]
            inner[q, part] = (up * up_scale[...] * (gated * jax.nn.sigmoid(gated))).astype(bf16)

        each_half(half)
        done.append(q)
        if len(done) in (1, 3):
            line.wait(len(done) // 2 + 1)
            line.hand_on(len(done) // 2 + 1)

    def forward_end():
        for d in range(3, length):
            line.wait(d)
            line.hand_on(d)
        for d in range(length - 1):
            line.sent(d)

    out = PlaneScatter(
        lambda q, half: dot(inner[q, half_rows(half)], down_weight(), 1, 0),
        own, cross, side, cross_sem.at[0], side_sem.at[0],
    )

    def forward_corner():
        forward_end()
        out.begin()

    plane_gather(
        held, gather_send.at[0], gather_receive.at[0], lambda h: each_chunk(enter, h), forward, forward_corner
    )
    out.end()

    def turn_back(part, place):
        start, alpha = hidden[part], alpha_mlp[...]
        result, unit, target_scale, moved_scale = step_forward(own[q0, part], start, alpha)
        mixed[part] = result.astype(bf16)
        target_grad, start_grad, alpha_part = step_back(
            cotangent[part].astype(f32), result, unit, target_scale, moved_scale, start, alpha
        )
        alpha_grads[1:2] += jnp.sum(alpha_part, axis=0, keepdims=True)
        hidden_grad[part] = start_grad
        grads[q0, place] = target_grad.astype(bf16)

    def backward(q):
        def half(part):
            inner_grad = dot(grads[q, part], down_weight(), 1, 1)
            up, gate = ups[q, part], gates[q, part]
            gated = gate * gate_scale[...]
            share = jax.nn.sigmoid(gated)
            silu = gated * share
            lifted = inner_grad * up
            gated_grad = lifted * up_scale[...] * (share * (1.0 + gated * (1.0 - share)))
            up_low[q, part] = (inner_grad * up_scale[...] * silu).astype(bf16)
            gate_low[q, part] = (gated_grad * gate_scale[...]).astype(bf16)
            scale_grads[0:1] += jnp.sum(lifted * silu, axis=0, keepdims=True)
            scale_grads[1:2] += jnp.sum(gated_grad * gate, axis=0, keepdims=True)

        each_half(half)

    def weights_back():
        tall = 4 * 2 * rows
        for i, (left, right) in enumerate(((up_low, held), (gate_low, held), (inner, grads))):

            def step(n, carry):
                columns = pl.ds(pl.multiple_of(n * BLOCK, BLOCK), BLOCK)
                product = dot(
                    left[...].reshape(tall, full), right[:, :, columns].reshape(tall, BLOCK), 0, 0
                )
                weight_grads[:, i, :, columns] = product.astype(bf16).reshape(owners, units, BLOCK)
                return carry

            lax.fori_loop(0, width // BLOCK, step, 0)

    back = PlaneScatter(
        lambda q, half: dot(up_low[q, half_rows(half)], weight(0), 1, 0)
        + dot(gate_low[q, half_rows(half)], weight(1), 1, 0),
        own, cross, side, cross_sem.at[1], side_sem.at[1],
    )
    plane_gather(
        grads, gather_send.at[1], gather_receive.at[1], lambda h: each_chunk(turn_back, h), backward, back.begin
    )
    back.end(weights_back)

    def leave(part, place):
        start, alpha = tokens[part].astype(f32), alpha_attn[...]
        result, unit, target_scale, moved_scale = step_forward(branch[part], start, alpha)
        target_grad, start_grad, alpha_part = step_back(
            hidden_grad[part] + own[q0, part], result, unit, target_scale, moved_scale, start, alpha
        )
        alpha_grads[0:1] += jnp.sum(alpha_part, axis=0, keepdims=True)
        branch_low[part] = target_grad.astype(bf16)
        token_grad[part] = start_grad

    for h in (0, 1):
        each_chunk(leave, h)


def mlp(length, branch, tokens, alpha_attn, alpha_mlp, cotangent, up_gate, down, up_scale, gate_scale):
    rows, width = branch.shape
    owners, units = length, down.shape[0]
    full = owners * units
    low, wide = like((rows, width), bf16), like((rows, width), f32)
    scratch = [
        pltpu.VMEM((rows, width), f32),
        pltpu.VMEM((rows, width), f32),
        pltpu.VMEM((4, 2 * rows, width), bf16),
        pltpu.VMEM((4, 2 * rows, width), bf16),
        pltpu.VMEM((4, 2 * rows, full), f32),
        pltpu.VMEM((4, 2 * rows, full), f32),
        pltpu.VMEM((4, 2 * rows, full), bf16),
        pltpu.VMEM((4, 2 * rows, full), bf16),
        pltpu.VMEM((4, 2 * rows, full), bf16),
        pltpu.VMEM((4, rows, width), f32),
        pltpu.VMEM((2, 4, rows, width), bf16),
        pltpu.VMEM((2, 3, rows, width), bf16),
        pltpu.SemaphoreType.DMA((2, 3, 8)),
        pltpu.SemaphoreType.DMA((2, 16)),
        pltpu.SemaphoreType.DMA((2, 2, 4)),
        pltpu.SemaphoreType.DMA((2, 2, 3, 2)),
        pltpu.VMEM((length, *down.shape), bf16),
    ] + line_gather_semaphores(length)
    return remote_call(
        functools.partial(mlp_kernel, length), "mlp", 5,
        (low, low, wide, like((2, width), f32), like((owners, 3, units, width), bf16), like((2, full), f32)),
        (IN_VMEM,) * 6, [IN_VMEM] * 9, scratch,
        branch, tokens, alpha_attn, alpha_mlp, cotangent, up_gate, down, up_scale, gate_scale,
    )


def shards(
    tokens, lengths, w_query, w_key, w_value, s_qk, w_out, up_weight, gate_weight, down_weight,
    s_up, s_gate, alpha_attn, alpha_mlp, cotangent,
):
    outer = lax.axis_size("o")
    own_units = up_weight.shape[0]
    if outer > 1:
        up_weight, gate_weight, down_weight, s_up, s_gate = (
            gather(a, "o") for a in (up_weight, gate_weight, down_weight, s_up, s_gate)
        )
    units = up_weight.shape[0]
    scales = jnp.zeros((2, SCALE_ROWS, up_weight.shape[1]), bf16)
    scales = scales.at[:, 0, :units].set(jnp.stack([s_up, s_gate]))
    up_gate = jnp.concatenate([jnp.stack([up_weight, gate_weight]), scales], axis=1)

    length = lax.axis_size("z")
    own_rows, width = tokens.shape
    rows = 4 * length * own_rows
    cosine, sine = turn_table(lengths[0], rows)
    joint = jnp.concatenate([w_query, w_key, w_value], axis=1).T
    group_tokens, turned_q, turned_k, qt, kt, vt, weights = project(
        length, tokens, joint, s_qk[:, None], cosine, sine, up_gate
    )
    branch, up_gate, ot, lse = branch_sum(
        length, lengths, qt, kt, vt, w_out, up_gate, weights, own_rows
    )
    up_scale, gate_scale = (up_gate[:, i, units, :units].reshape(1, -1).astype(f32) for i in range(2))
    mixed, branch_low, token_grad, alpha_grads, mlp_grads, scale_grads = mlp(
        length, branch, tokens, alpha_attn[None], alpha_mlp[None], cotangent, up_gate, down_weight,
        up_scale, gate_scale,
    )
    out_grad, mlp_grads, gqt, gkt, gvt = spread(
        length, lengths, branch_low, w_out, qt, kt, vt, ot, lse, mlp_grads
    )
    tokens_grad, attn_grads, alpha_sums, scale_sums, gain_grad, mlp_grads = inward(
        length, group_tokens, token_grad, out_grad, alpha_grads, scale_grads, mlp_grads,
        gqt, gkt, gvt, turned_q, turned_k, s_qk[:, None], cosine, sine, joint,
    )
    if outer > 1:
        mlp_grads = lax.psum_scatter(mlp_grads, "o", scatter_dimension=1, tiled=True)
        attn_grads, alpha_sums, scale_sums, gain_grad = lax.psum(
            (attn_grads, alpha_sums, scale_sums, gain_grad), "o"
        )
    place = lax.axis_index("z") * units + lax.axis_index("o") * own_units
    scale_sums = lax.dynamic_slice_in_dim(scale_sums, place, own_units, 1)
    return (
        mixed,
        tokens_grad,
        attn_grads[:HEAD_DIM].T,
        attn_grads[HEAD_DIM : 2 * HEAD_DIM].T,
        attn_grads[2 * HEAD_DIM : 3 * HEAD_DIM].T,
        gain_grad[:, 0],
        attn_grads[3 * HEAD_DIM :],
        mlp_grads[0],
        mlp_grads[1],
        mlp_grads[2],
        scale_sums[0],
        scale_sums[1],
        alpha_sums[0],
        alpha_sums[1],
    )


def solution(mesh):
    dp, head = mesh.shape["dp"], mesh.shape["head"]
    fine = Mesh(mesh.devices.reshape(dp // 2, 2, head // 4, 2, 2), AXES)
    group, rows, heads = P(("o", "x"), None), P(AXES, None), P(None, GROUP)
    in_specs = (
        rows, group, heads, heads, heads, P(GROUP), P(GROUP, None), rows, rows, rows,
        P(AXES), P(AXES), P(), P(), rows,
    )
    out_specs = (
        rows, rows, heads, heads, heads, P(GROUP), P(GROUP, None), rows, rows, rows,
        P(AXES), P(AXES), P(), P(),
    )
    return jax.shard_map(
        shards, mesh=fine, in_specs=in_specs, out_specs=out_specs, check_vma=False
    )
```

```python
import functools
import math

import jax
import jax.numpy as jnp
from jax import lax
from jax.experimental import pallas as pl
from jax.experimental.pallas import tpu as pltpu
from jax.sharding import Mesh
from jax.sharding import PartitionSpec as P

HEAD_DIM = 64
BLOCK = 512
REACH = 4
EPSILON = 1e-06
ROOT = math.sqrt(HEAD_DIM)
SCORE_SCALE = math.log2(math.e) / ROOT
AXES = ("o", "x", "z", "y", "c")
GROUP = ("z", "y", "c")
f32, bf16 = jnp.float32, jnp.bfloat16
VMEM_LIMIT = 60 * 2**20


def dot(left, right, left_dim, right_dim):
    return lax.dot_general(
        left, right, (((left_dim,), (right_dim,)), ((), ())), preferred_element_type=f32
    )


def unit_start(lengths, unit):
    start, end = jnp.int32(0), jnp.int32(0)
    for j in range(lengths.shape[1]):
        end = end + lengths[0, j]
        start = jnp.where(unit >= end, end, start)
    return start


def causal(weights):
    key = lax.broadcasted_iota(jnp.int32, weights.shape, 0)
    query = lax.broadcasted_iota(jnp.int32, weights.shape, 1)
    return jnp.where(key <= query, weights, 0.0)


def block_columns(index):
    return pl.ds(pl.multiple_of(index * BLOCK, BLOCK), BLOCK)


def barred(lengths, unit, back):
    return jnp.where(unit - back >= unit_start(lengths, unit), 0.0, 1e30).astype(f32)


def attend(lengths, unit, qt, kt, vt, ot, lse, total, attended):
    columns = block_columns(unit)

    def part(back):
        keys = block_columns(unit - back)
        scores = dot(kt[:, keys], qt[:, columns], 0, 0) * SCORE_SCALE
        if back == 0:
            weights = causal(jnp.exp2(scores))
        else:
            weights = jnp.exp2(scores - barred(lengths, unit, back))
        sums = jnp.sum(weights, axis=0, keepdims=True)
        values = dot(vt[:, keys], weights.astype(bf16), 1, 0)
        if back == 0:
            total[...] = sums
            attended[...] = values
        else:
            total[...] += sums
            attended[...] += values

    part(0)
    for back in range(1, REACH):
        pl.when(unit >= back)(functools.partial(part, back))
    ot[:, columns] = (attended[...] * (1.0 / total[...])).astype(bf16)
    lse[:, columns] = jnp.log2(total[...])


def attend_back(lengths, unit, qt, kt, vt, ot, got, lse, gqt, gkt, gvt):
    columns = block_columns(unit)
    query, grad = qt[:, columns], got[...]
    inner = jnp.sum(grad.astype(f32) * ot[:, columns].astype(f32), axis=0, keepdims=True)

    def part(back):
        keys = block_columns(unit - back)
        key, value = kt[:, keys], vt[:, keys]
        log_total = lse[:, columns]
        if back > 0:
            log_total = log_total + barred(lengths, unit, back)
        weights = jnp.exp2(dot(key, query, 0, 0) * SCORE_SCALE - log_total)
        if back == 0:
            weights = causal(weights)
        score_grad = (weights * (dot(value, grad, 0, 0) - inner)).astype(bf16)
        gkt[:, keys] += dot(query, score_grad, 1, 1)
        gvt[:, keys] += dot(grad, weights.astype(bf16), 1, 1)
        gqt[:, columns] += dot(key, score_grad, 1, 0)

    part(0)
    for back in range(1, REACH):
        pl.when(unit >= back)(functools.partial(part, back))


def turn_table(lengths, unit):
    shape = (HEAD_DIM // 2, BLOCK)
    first = (unit - unit_start(lengths, unit)) * BLOCK
    place = (first + lax.broadcasted_iota(jnp.int32, shape, 1)).astype(f32)
    turns = lax.broadcasted_iota(jnp.int32, shape, 0).astype(f32)
    angle = place * jnp.exp(turns * (-2.0 * math.log(10000.0) / HEAD_DIM))
    return jnp.cos(angle), jnp.sin(angle)


def as_column(row):
    n = row.shape[1]
    same = lax.broadcasted_iota(jnp.int32, (n, n), 0) == lax.broadcasted_iota(jnp.int32, (n, n), 1)
    return jnp.sum(jnp.where(same, row, 0.0), axis=1, keepdims=True)


def as_row(column):
    n = column.shape[0]
    same = lax.broadcasted_iota(jnp.int32, (n, n), 0) == lax.broadcasted_iota(jnp.int32, (n, n), 1)
    return jnp.sum(jnp.where(same, column, 0.0), axis=0, keepdims=True)


def join(joint, *parts):
    for i, part in enumerate(parts):
        joint[i * HEAD_DIM : (i + 1) * HEAD_DIM] = part[...]


def turn(values, cosine, sine):
    half = HEAD_DIM // 2
    a, b = values[:half], values[half:]
    return jnp.concatenate([a * cosine - b * sine, b * cosine + a * sine], axis=0)


def unit_features(turned):
    scale = lax.rsqrt(jnp.mean(turned * turned, axis=0, keepdims=True) + EPSILON)
    return turned * scale, scale


def gather(values, axes):
    return lax.all_gather(values, axes, axis=0, tiled=True)


MESH_ID = pl.DeviceIdType.MESH


def here(*names):
    return tuple(lax.axis_index(name) for name in names)


def greet(neighbours):
    barrier = pltpu.get_barrier_semaphore()
    count = jnp.int32(0)
    for condition, device in neighbours:

        @pl.when(condition)
        def _():
            pl.semaphore_signal(barrier, inc=1, device_id=device, device_id_type=MESH_ID)

        count = count + jnp.where(condition, 1, 0)
    pl.semaphore_wait(barrier, count)


def remote(source, target, send, receive, device):
    return pltpu.make_async_remote_copy(
        src_ref=source,
        dst_ref=target,
        send_sem=send,
        recv_sem=receive,
        device_id=device,
        device_id_type=MESH_ID,
    )


def line_order(z, length, step):
    picked = jnp.int32(0)
    for at in range(length):
        order = sorted(range(length), key=lambda p: (abs(p - at), p))
        picked = jnp.where(z == at, order[step], picked)
    return picked


def group_neighbours(length):
    z, y, c = here("z", "y", "c")
    return [
        (z > 0, {"z": z - 1}),
        (z < length - 1, {"z": z + 1}),
        (z >= 0, {"y": 1 - y}),
        (z >= 0, {"c": 1 - c}),
    ]


def group_gather(length, own, held, send, receive, on_unit, at_step=None):
    z, y, c = here("z", "y", "c")
    rows = held.shape[1] // 2
    half = rows // 2

    def copy(kind, zz, yy, cc, h, device):
        at = held.at[zz * 2 + yy, pl.ds(pl.multiple_of(cc * rows + h * half, half), half)]
        number = ((zz * 2 + yy) * 2 + cc) * 2 + h
        return remote(at, at, send.at[kind, number], receive.at[number], device)

    def arrived(zz, yy, cc, h):
        copy(3, zz, yy, cc, h, {"c": 1 - c}).wait_recv()

    def come(distance):
        if distance == 0:
            return [(z, z >= 0, [(0, z < length - 1, {"z": z + 1}), (1, z > 0, {"z": z - 1})])]
        return [
            (z - distance, z >= distance, [(0, z < length - 1, {"z": z + 1})]),
            (z + distance, z + distance < length, [(1, z > 0, {"z": z - 1})]),
        ]

    def passed_on(zz, h, along, act):
        for kind, goes, device in along:

            @pl.when(goes)
            def _():
                act(copy(kind, zz, y, c, h, device))

        act(copy(2, zz, y, c, h, {"y": 1 - y}))
        act(copy(3, zz, y, c, h, {"c": 1 - c}))

    held[z * 2 + y, pl.ds(pl.multiple_of(c * rows, rows), rows)] = own[...]
    order = [line_order(z, length, step) for step in range(length)]
    for tick in range(2 * length + 1):
        step, h = divmod(tick, 2)
        before, last_h = divmod(tick - 1, 2)
        if step < length:
            for zz, there, along in come(step):

                @pl.when(there)
                def _():
                    if step > 0:
                        arrived(zz, y, c, h)
                    passed_on(zz, h, along, lambda copy_: copy_.start())

        if before >= 0:
            arrived(order[before], 1 - y, c, last_h)
            copy(3, order[before], 1 - y, c, last_h, {"c": 1 - c}).start()
        if at_step is not None and h == 0:
            at_step(step)
        if h == 1:
            for i in (0, 1):
                arrived(order[step], y, 1 - c, i)
            on_unit(order[step] * 2 + y)
        if last_h == 1 and before >= 0:
            for i in (0, 1):
                arrived(order[before], 1 - y, 1 - c, i)
            on_unit(order[before] * 2 + 1 - y)
    for h in (0, 1):
        for step in range(length):
            for zz, there, along in come(step):

                @pl.when(there)
                def _():
                    passed_on(zz, h, along, lambda copy_: copy_.wait_send())

            copy(3, order[step], 1 - y, c, h, {"c": 1 - c}).wait_send()


GATHER_SEMAPHORES = 4


def gather_scratch(units, rows, width):
    return [
        pltpu.VMEM((units, 2 * rows, width), bf16),
        pltpu.SemaphoreType.DMA((GATHER_SEMAPHORES, 4 * units)),
        pltpu.SemaphoreType.DMA((4 * units,)),
    ]


def scatter_scratch(length, rows, width):
    return [
        pltpu.VMEM((length + 1, rows, width), f32),
        pltpu.VMEM((2 * length + 4, rows, width), bf16),
        pltpu.VMEM((2, length, rows, width), bf16),
        pltpu.VMEM((3, length, rows, width), bf16),
        pltpu.SemaphoreType.DMA((2, 2 * length)),
        pltpu.SemaphoreType.DMA((2, length, 2)),
        pltpu.SemaphoreType.DMA((3, length, 2)),
    ]


def group_scatter(length, produce, finish, own, cross, across, along, cross_sem, across_sem, along_sem, prepare=None, between=None, at_step=None):
    z, y, c = here("z", "y", "c")

    def to_core(unit, slot=0):
        source = cross.at[2 * length + slot]
        return remote(source, cross.at[unit], cross_sem.at[0, unit], cross_sem.at[1, unit], {"c": 1 - c})

    half = own.shape[1] // 2

    def part(h):
        return pl.ds(h * half, half)

    def to_y(zz, h):
        return remote(
            across.at[0, zz, part(h)], across.at[1, zz, part(h)], across_sem.at[0, zz, h],
            across_sem.at[1, zz, h], {"y": 1 - y},
        )

    def to_z(zz, slot, h, device):
        return remote(
            along.at[0, zz, part(h)], along.at[slot, zz, part(h)], along_sem.at[0, zz, h],
            along_sem.at[slot, zz, h], device,
        )

    def from_z(zz, slot, h):
        to_z(zz, slot, h, {"c": 1 - c}).wait_recv()
        return along[slot, zz, part(h)].astype(f32)

    order = [line_order(z, length, length - 1 - step) for step in range(length)]

    def give(unit, slot):
        cross[2 * length + slot] = produce(unit, 1 - c).astype(bf16)
        to_core(unit, slot).start()

    def first(step):
        zz = order[step]
        slot = 2 * (step % 2)
        if step >= 2:
            for yy in (0, 1):
                to_core(order[step - 2] * 2 + yy).wait_send()
        there, here_ = zz * 2 + 1 - y, zz * 2 + y
        if prepare is not None:
            prepare(there)
        give(there, slot)
        own[length] = produce(there, c)
        if prepare is not None:
            prepare(here_)
        to_core(there).wait_recv()
        across[0, zz] = (own[length] + cross[there].astype(f32)).astype(bf16)
        for h in (0, 1):
            to_y(zz, h).start()
        give(here_, slot + 1)
        own[zz] = produce(here_, c)

    def third(zz, h, last):
        unit = zz * 2 + y
        if h == 0:
            to_core(unit).wait_recv()
        own[zz, part(h)] += cross[unit, part(h)].astype(f32)
        to_y(zz, h).wait_recv()
        own[zz, part(h)] += across[1, zz, part(h)].astype(f32)

        @pl.when((zz >= z) & (z > 0))
        def _():
            own[zz, part(h)] += from_z(zz, 1, h)

        @pl.when((zz <= z) & (z < length - 1))
        def _():
            own[zz, part(h)] += from_z(zz, 2, h)

        if last:
            finish(h, own[zz, part(h)])
            return
        along[0, zz, part(h)] = own[zz, part(h)].astype(bf16)

        @pl.when(zz > z)
        def _():
            to_z(zz, 1, h, {"z": z + 1}).start()

        @pl.when(zz < z)
        def _():
            to_z(zz, 2, h, {"z": z - 1}).start()

    for step in range(length + 1):
        if step < length:
            first(step)
        if at_step is not None:
            at_step(step)
        if step == length - 1 and between is not None:
            between()
        if step >= 1:
            for h in (0, 1):
                third(order[step - 1], h, step == length)
    for step in range(length):
        zz = order[step]
        if step >= length - 2:
            for yy in (0, 1):
                to_core(zz * 2 + yy).wait_send()
        for h in (0, 1):
            to_y(zz, h).wait_send()
            if step < length - 1:
                to_z(zz, 1, h, {"c": 1 - c}).wait_send()


def remote_call(kernel, name, number, outs, out_specs, in_specs, scratch, *operands):
    return pl.pallas_call(
        kernel,
        name=name,
        out_shape=outs,
        in_specs=in_specs,
        out_specs=out_specs,
        scratch_shapes=scratch,
        compiler_params=pltpu.CompilerParams(
            collective_id=number, has_side_effects=True, vmem_limit_bytes=VMEM_LIMIT
        ),
    )(*operands)


IN_VMEM = pl.BlockSpec(memory_space=pltpu.VMEM)
IN_SMEM = pl.BlockSpec(memory_space=pltpu.SMEM)
ANYWHERE = pl.BlockSpec(memory_space=pl.ANY)


def like(shape, dtype):
    return jax.ShapeDtypeStruct(shape, dtype)


class LineGather:
    def __init__(self, length, own, held, send, receive, local_sem):
        self.length, self.own, self.held = length, own, held
        self.sems, self.local_sem = (send, receive), local_sem
        self.z = lax.axis_index("z")

    def copy(self, way, zz, source=None):
        send, receive = self.sems
        at = self.held.at[zz]
        device = {"z": self.z + 1} if way == 0 else {"z": self.z - 1}
        return remote(at if source is None else source, at, send.at[way, zz], receive.at[zz], device)

    def ways(self, d, act):
        z, length = self.z, self.length
        for way, zz, there, more in (
            (0, z - d, z - d >= 0, z < length - 1),
            (1, z + d, z + d < length, z > 0),
        ):
            act(way, zz, there, there & more)

    def start(self):
        pltpu.make_async_copy(self.own, self.held.at[self.z], self.local_sem).start()
        self.hand_on(0)

    def hand_on(self, d):
        def begin(way, zz, there, more):
            @pl.when(more)
            def _():
                self.copy(way, zz, self.own if d == 0 else None).start()

        self.ways(d, begin)

    def wait(self, d):
        def arrive(way, zz, there, more):
            @pl.when(there)
            def _():
                self.arrival(way, zz).wait_recv()

        self.ways(d, arrive)

    def sent(self, d):
        def leave(way, zz, there, more):
            @pl.when(more)
            def _():
                self.copy(way, zz, self.own if d == 0 else None).wait_send()

        self.ways(d, leave)
        if d == 0:
            pltpu.make_async_copy(self.own, self.held.at[self.z], self.local_sem).wait()

    def arrival(self, way, zz):
        send, receive = self.sems
        at = self.held.at[zz]
        return remote(at, at, send.at[way, zz], receive.at[zz], {"c": 1 - lax.axis_index("c")})


def line_gather_semaphores(length):
    return [
        pltpu.SemaphoreType.DMA((2, length)),
        pltpu.SemaphoreType.DMA((length,)),
        pltpu.SemaphoreType.DMA,
    ]


class LineScatter:
    def __init__(self, length, parts, rest, out, into, send_sem, receive_sem):
        self.length, self.parts, self.rest = length, parts, rest
        self.out, self.into, self.sems = out, into, (send_sem, receive_sem)
        self.z = lax.axis_index("z")

    def copy(self, way, d, source):
        send, receive = self.sems
        device = {"z": self.z + 1} if way == 0 else {"z": self.z - 1}
        return remote(source, self.into.at[way, d - 2], send.at[way, d - 2], receive.at[way, d - 2], device)

    def arrived(self, way, d):
        send, receive = self.sems
        at = self.into.at[way, d - 2]
        device = {"c": 1 - lax.axis_index("c")}
        remote(at, at, send.at[way, d - 2], receive.at[way, d - 2], device).wait_recv()

    def cases(self, d, alone, joined):
        z, length = self.z, self.length
        for way, dest, valid, behind in (
            (0, z + d, z + d < length, z > 0),
            (1, z - d, z - d >= 0, z < length - 1),
        ):
            behind = behind if d < length - 1 else z < 0
            pl.when(valid & jnp.logical_not(behind))(functools.partial(alone, way, dest))
            pl.when(valid & behind)(functools.partial(joined, way, dest))

    def joint(self, way, dest, d):
        self.arrived(way, d + 1)
        return (self.parts[dest].astype(f32) + self.into[way, d - 1].astype(f32)).astype(bf16)

    def send(self, d):
        def alone(way, dest):
            self.copy(way, d, self.parts.at[dest]).start()

        def joined(way, dest):
            self.out[way, d - 2] = self.joint(way, dest, d)
            self.copy(way, d, self.out.at[way, d - 2]).start()

        self.cases(d, alone, joined)

    def finish(self):
        def alone(way, dest):
            self.rest[way] = self.parts[dest]

        def joined(way, dest):
            self.rest[way] = self.joint(way, dest, 1)

        self.cases(1, alone, joined)
        for d in range(2, self.length):

            def left(way, dest):
                self.copy(way, d, self.parts.at[dest]).wait_send()

            self.cases(d, left, left)


def line_scatter_scratch(parts):
    length = parts.shape[0]
    hops = (2, length - 2, *parts.shape[1:])
    joint = (2, max(length - 3, 1), *parts.shape[1:])
    return [pltpu.VMEM(joint, bf16), pltpu.VMEM(hops, bf16)] + [pltpu.SemaphoreType.DMA(hops[:2])] * 2


def half_columns(unit, half):
    rows = BLOCK // 2
    return pl.ds(pl.multiple_of(unit * BLOCK + half * rows, rows), rows)


def attention_kernel(
    length, lengths, tokens, w_query, w_key, w_value, gain_row, w_out, weight,
    gathered, turned_q, turned_k, cosine, sine, qt, kt, vt, weights, branch, ot, lse,
    joint, held, send, receive, out_sem, line_send, line_receive, line_local, total, attended, *scratch,
):
    greet(group_neighbours(length))
    line = LineGather(length, weight, weights, line_send, line_receive, line_local)
    join(joint, w_query, w_key, w_value)
    gain = as_column(gain_row[...])

    def start_line(step):
        if step == length - 1:
            line.start()

    def on_unit(unit):
        pltpu.make_async_copy(held.at[unit], gathered.at[unit], out_sem.at[unit]).start()
        columns = block_columns(unit)
        projected = dot(joint[...], held[unit], 1, 1)
        cosine[:, columns], sine[:, columns] = turn_table(lengths, unit)
        for part, turned, features in ((0, turned_q, qt), (1, turned_k, kt)):
            values = turn(
                projected[part * HEAD_DIM : (part + 1) * HEAD_DIM], cosine[:, columns], sine[:, columns]
            )
            turned[:, columns] = values
            features[:, columns] = (unit_features(values)[0] * gain).astype(bf16)
        vt[:, columns] = projected[2 * HEAD_DIM :].astype(bf16)

    group_gather(length, tokens, held, send, receive, on_unit, start_line)
    line.wait(1)
    line.hand_on(1)

    def move_line(step):
        if 2 <= step < length - 1:
            line.wait(step)
            line.hand_on(step)

    def finish(h, total):
        branch[pl.ds(h * total.shape[0], total.shape[0])] = total

    group_scatter(
        length, lambda unit, half: dot(ot[:, half_columns(unit, half)], w_out[...], 0, 0), finish, *scratch,
        prepare=lambda unit: attend(lengths, unit, qt, kt, vt, ot, lse, total, attended), at_step=move_line,
    )
    line.wait(length - 1)
    for d in range(length - 1):
        line.sent(d)
    for unit in range(2 * length):
        pltpu.make_async_copy(held.at[unit], gathered.at[unit], out_sem.at[unit]).wait()


def attention(length, lengths, tokens, w_query, w_key, w_value, gain, w_out, weight):
    rows, width = tokens.shape
    units = 2 * length
    total = units * 2 * rows
    wide, narrow = like((HEAD_DIM, total), f32), like((HEAD_DIM, total), bf16)
    table = like((HEAD_DIM // 2, total), f32)
    return remote_call(
        functools.partial(attention_kernel, length), "attention", 1,
        (
            like((units, 2 * rows, width), bf16), wide, wide, table, table, narrow, narrow, narrow,
            like((length, *weight.shape), bf16), like((rows, width), f32), narrow, like((1, total), f32),
        ),
        (ANYWHERE,) + (IN_VMEM,) * 7 + (ANYWHERE,) + (IN_VMEM,) * 3, [IN_SMEM] + [IN_VMEM] * 6 + [ANYWHERE],
        [pltpu.VMEM((3 * HEAD_DIM, width), bf16)] + gather_scratch(units, rows, width) + [pltpu.SemaphoreType.DMA((units,))]
        + line_gather_semaphores(length) + [pltpu.VMEM((1, BLOCK), f32), pltpu.VMEM((HEAD_DIM, BLOCK), f32)]
        + scatter_scratch(length, rows, width),
        lengths, tokens, w_query, w_key, w_value, gain, w_out, weight,
    )


def flip(position, bit):
    return position + bit - 2 * bit * ((position // bit) % 2)


def back_kernel(
    length, lengths, grad, w_out, qt, kt, vt, ot, lse, parts, turned_q, turned_k, gain_row, cosine, sine,
    w_query, w_key, w_value, alpha_grads, scale_grads, direct, gathered,
    token_grad, weight_grads, alpha_sums, scale_sums, gain_grad, sums,
    joint, out_grad, gqt, gkt, gvt, got, rest, arrivals, rest_sem, grads, held_sem, gains, gain_sem, sent, taken,
    weight_sem, small_out, small_in, small_sem, line_out, line_into, line_send, line_receive,
    held, send, receive, *scratch,
):
    x, z, y, c = here("x", "z", "y", "c")
    to_x = {"x": 1 - x}
    bits = [1 << i for i in range(length.bit_length() - 1)]
    greet(group_neighbours(length) + [(x >= 0, to_x)] + [(x >= 0, {"z": flip(z, bit)}) for bit in bits])
    partners = [{"c": 1 - c}, {"y": 1 - y}, to_x] + [{"z": flip(z, bit)} for bit in bits]
    line = LineScatter(length, parts, rest, line_out, line_into, line_send, line_receive)
    join(joint, w_query, w_key, w_value)
    gain = as_column(gain_row[...])

    def spread_step(step):
        if step == 0:
            for array in (out_grad, gqt, gkt, gvt):
                array[...] = jnp.zeros_like(array)
        if step % 2 == 0 and step < 2 * (length - 2):
            line.send(length - 1 - step // 2)

    def on_unit(unit):
        columns = block_columns(unit)
        got[...] = dot(w_out[...], held[unit], 1, 1).astype(bf16)
        out_grad[...] += dot(ot[:, columns], held[unit], 1, 0)
        attend_back(lengths, unit, qt, kt, vt, ot, got, lse, gqt, gkt, gvt)

    group_gather(length, grad, held, send, receive, on_unit, spread_step)
    load = pltpu.make_async_copy(gathered, held, held_sem)
    load.start()
    line.finish()
    lines = [
        (remote(rest.at[way], arrivals.at[way], rest_sem.at[0, way], rest_sem.at[1, way], {"z": to}), goes, comes)
        for way, to, goes, comes in (
            (0, z + 1, z < length - 1, z > 0), (1, z - 1, z > 0, z < length - 1)
        )
    ]
    for last_hop, goes, _ in lines:
        pl.when(goes)(last_hop.start)
    gains[0] = jnp.zeros_like(gains[0])
    small_out[0] = jnp.zeros_like(small_out[0])
    small_out[0, 0:2] = alpha_grads[...]
    small_out[0, 2:4, : scale_grads.shape[1]] = scale_grads[...]

    def exchange(i):
        return remote(small_out.at[i], small_in.at[i], small_sem.at[0, i], small_sem.at[1, i], partners[i])

    def at_step(step):
        if 0 < step <= len(partners):
            exchange(step - 1).wait_recv()
            small_out[step] = small_out[step - 1]
            summed = 2 if step <= 3 else 4
            small_out[step, :summed] += small_in[step - 1, :summed]
        if step < len(partners):
            exchange(step).start()

    def prepare(unit):
        columns = block_columns(unit)
        for part, turned, outer in ((0, turned_q, gqt), (1, turned_k, gkt)):
            normal, scale = unit_features(turned[:, columns])
            grad = outer[:, columns] * (1.0 / ROOT)
            product = grad * normal
            width = gains.shape[2]
            for i in range(BLOCK // width):
                gains[0] += product[:, i * width : (i + 1) * width]
            grad = grad * gain
            grad = scale * (grad - normal * jnp.mean(grad * normal, axis=0, keepdims=True))
            grad = turn(grad, cosine[:, columns], -sine[:, columns])
            grads[part * HEAD_DIM : (part + 1) * HEAD_DIM, columns] = grad.astype(bf16)
        grads[2 * HEAD_DIM :, columns] = gvt[:, columns].astype(bf16)

    gain_copy = remote(gains.at[0], gains.at[1], gain_sem.at[0], gain_sem.at[1], to_x)
    weight_copy = remote(sent, taken, weight_sem.at[0], weight_sem.at[1], to_x)

    def between():
        gain_copy.start()
        load.wait()
        rows = grads.shape[1]
        product = dot(grads[...], held[...].reshape(rows, held.shape[2]), 1, 0)
        sent[: 3 * HEAD_DIM] = product.astype(bf16)
        sent[3 * HEAD_DIM :] = out_grad[...].astype(bf16)
        weight_copy.start()

    def finish(h, total):
        part = pl.ds(h * total.shape[0], total.shape[0])
        token_grad[part] = (direct[part] + total).astype(bf16)

    group_scatter(
        length, lambda unit, half: dot(grads[:, half_columns(unit, half)], joint[...], 0, 0), finish, *scratch,
        prepare=prepare, between=between, at_step=at_step,
    )
    for step in range(length + 1, len(partners) + 1):
        at_step(step)
    alpha_sums[...] = small_out[len(partners), 0:2]
    scale_sums[...] = small_out[len(partners), 2:4, : scale_sums.shape[1]]
    sums[...] = parts[z].astype(f32)
    for way, (last_hop, goes, comes) in enumerate(lines):

        @pl.when(comes)
        def _():
            remote(
                arrivals.at[way], arrivals.at[way], rest_sem.at[0, way], rest_sem.at[1, way], {"c": 1 - c}
            ).wait_recv()
            sums[...] += arrivals[way].astype(f32)

        pl.when(goes)(last_hop.wait_send)
    gain_copy.wait()
    gain_grad[...] = as_row(jnp.sum(gains[0] + gains[1], axis=1, keepdims=True))
    weight_copy.wait()
    weight_grads[...] = sent[...].astype(f32) + taken[...].astype(f32)
    for i in range(len(partners)):
        exchange(i).wait_send()


def back(length, lengths, grad, w_out, qt, kt, vt, ot, lse, parts, *operands):
    rows, width = grad.shape
    units = 2 * length
    total = qt.shape[1]
    alpha_grads, scale_grads, direct, gathered = operands[-4:]
    exchanges = 3 + length.bit_length() - 1
    small = (exchanges + 1, 4, width)
    weights = (4 * HEAD_DIM, width)
    wide = pltpu.VMEM((HEAD_DIM, total), f32)
    hops = pltpu.VMEM((2, *parts.shape[1:]), bf16)
    scratch = [
        pltpu.VMEM((3 * HEAD_DIM, width), bf16), pltpu.VMEM(w_out.shape, f32), wide, wide, wide, pltpu.VMEM((HEAD_DIM, BLOCK), bf16), hops, hops,
        pltpu.SemaphoreType.DMA((2, 2)),
        pltpu.VMEM((3 * HEAD_DIM, total), bf16),
        pltpu.SemaphoreType.DMA,
        pltpu.VMEM((2, HEAD_DIM, 128), f32),
        pltpu.SemaphoreType.DMA((2,)),
        pltpu.VMEM(weights, bf16),
        pltpu.VMEM(weights, bf16),
        pltpu.SemaphoreType.DMA((2,)),
        pltpu.VMEM(small, f32),
        pltpu.VMEM(small, f32),
        pltpu.SemaphoreType.DMA((2, exchanges)),
    ]
    return remote_call(
        functools.partial(back_kernel, length), "back", 4,
        (
            like((rows, width), bf16), like(weights, f32), like(alpha_grads.shape, f32),
            like(scale_grads.shape, f32), like((1, HEAD_DIM), f32), like(parts.shape[1:], f32),
        ),
        (IN_VMEM,) * 6, [IN_SMEM] + [IN_VMEM] * 19 + [ANYWHERE],
        scratch + line_scatter_scratch(parts) + gather_scratch(units, rows, width)
        + scatter_scratch(length, rows, width),
        lengths, grad, w_out, qt, kt, vt, ot, lse, parts, *operands,
    )


def plane_neighbours():
    x, y, c = here("x", "y", "c")
    return [(x >= 0, {"x": 1 - x}), (x >= 0, {"y": 1 - y}), (x >= 0, {"c": 1 - c})]


def plane_gather(held, send, receive, make_half, on_pair, before_corner):
    x, y, c = here("x", "y", "c")
    rows = held.shape[1] // 2
    half = rows // 2
    q0, qx, qy, qd = x * 2 + y, (1 - x) * 2 + y, x * 2 + 1 - y, (1 - x) * 2 + 1 - y
    to_x, to_y, to_c = (0, {"x": 1 - x}), (1, {"y": 1 - y}), (2, {"c": 1 - c})

    def copy(way, q, cc, h):
        at = held.at[q, pl.ds(pl.multiple_of(cc * rows + h * half, half), half)]
        return remote(at, at, send.at[way[0], q * 2 + h], receive.at[(q * 2 + cc) * 2 + h], way[1])

    def arrived(q, cc, h):
        copy(to_c, q, cc, h).wait_recv()

    sent = []

    def start(way, q, h):
        sent.append((way, q, h))
        copy(way, q, c, h).start()

    for h in (0, 1):
        make_half(h)
        for way in (to_x, to_y, to_c):
            start(way, q0, h)
    for h in (0, 1):
        arrived(q0, 1 - c, h)
    on_pair(q0)
    arrived(qx, c, 0)
    start(to_y, qx, 0)
    start(to_c, qx, 0)
    arrived(qy, c, 0)
    start(to_c, qy, 0)
    arrived(qy, c, 1)
    start(to_x, qy, 1)
    start(to_c, qy, 1)
    arrived(qx, c, 1)
    start(to_c, qx, 1)
    for q in (qx, qy):
        for h in (0, 1):
            arrived(q, 1 - c, h)
        on_pair(q)
    before_corner()
    for h in (0, 1):
        arrived(qd, c, h)
        start(to_c, qd, h)
    for h in (0, 1):
        arrived(qd, 1 - c, h)
    on_pair(qd)
    for way, q, h in sent:
        copy(way, q, c, h).wait_send()


class PlaneScatter:
    def __init__(self, produce, own, cross, side, cross_sem, side_sem):
        self.produce, self.own, self.cross, self.side = produce, own, cross, side
        self.cross_sem, self.side_sem = cross_sem, side_sem
        x, y, self.c = here("x", "y", "c")
        self.half = own.shape[1] // 2
        self.chips = x * 2 + y, (1 - x) * 2 + y, x * 2 + 1 - y, (1 - x) * 2 + 1 - y
        self.to_x, self.to_y = {"x": 1 - x}, {"y": 1 - y}

    def to_core(self, q):
        cross, sem = self.cross, self.cross_sem
        return remote(cross.at[0, q], cross.at[1, q], sem.at[0, q], sem.at[1, q], {"c": 1 - self.c})

    def part(self, h):
        return pl.ds(h * self.half, self.half)

    def beside(self, kind, h, device):
        side, sem, part = self.side, self.side_sem, self.part(h)
        return remote(
            side.at[0, kind, part], side.at[1, kind, part], sem.at[0, kind, h], sem.at[1, kind, h], device
        )

    def first(self, q):
        self.cross[0, q] = self.produce(q, 1 - self.c).astype(bf16)
        self.to_core(q).start()
        self.own[q] = self.produce(q, self.c)

    def joined(self, q):
        self.to_core(q).wait_recv()
        self.own[q] += self.cross[1, q].astype(f32)

    def send(self, kind, q, h, device):
        self.side[0, kind, self.part(h)] = self.own[q, self.part(h)].astype(bf16)
        self.beside(kind, h, device).start()

    def add(self, q, kind, h, device):
        self.beside(kind, h, device).wait_recv()
        self.own[q, self.part(h)] += self.side[1, kind, self.part(h)].astype(f32)

    def begin(self):
        q0, qx, qy, qd = self.chips
        self.first(qx)
        self.first(qy)
        self.joined(qx)
        self.send(1, qx, 0, self.to_x)
        self.joined(qy)
        self.send(2, qy, 1, self.to_y)

    def end(self, between=None):
        q0, qx, qy, qd = self.chips
        to_x, to_y = self.to_x, self.to_y
        self.first(qd)
        self.joined(qd)
        self.send(0, qd, 0, to_x)
        self.send(0, qd, 1, to_y)
        self.first(q0)
        self.add(qx, 0, 1, to_y)
        self.send(1, qx, 1, to_x)
        self.add(qy, 0, 0, to_x)
        self.send(2, qy, 0, to_y)
        self.joined(q0)
        if between is not None:
            between()
        self.add(q0, 1, 0, to_x)
        self.add(q0, 2, 1, to_y)
        self.add(q0, 2, 0, to_y)
        self.add(q0, 1, 1, to_x)
        for q in self.chips:
            self.to_core(q).wait_send()
        self.beside(0, 0, to_x).wait_send()
        self.beside(0, 1, to_y).wait_send()
        for h in (0, 1):
            self.beside(1, h, to_x).wait_send()
            self.beside(2, h, to_y).wait_send()


def mean_of(values):
    return jnp.mean(values, axis=-1, keepdims=True)


def scale_of(values):
    return lax.rsqrt(mean_of(values * values) + EPSILON)


def step_forward(target, start, alpha):
    target_scale = scale_of(target)
    unit = target * target_scale
    moved = start + alpha * (unit - start)
    moved_scale = scale_of(moved)
    return moved * moved_scale, unit, target_scale, moved_scale


def step_back(grad, result, unit, target_scale, moved_scale, start, alpha):
    moved_grad = moved_scale * (grad - result * mean_of(grad * result))
    unit_grad = alpha * moved_grad
    target_grad = target_scale * (unit_grad - unit * mean_of(unit_grad * unit))
    return target_grad, moved_grad - unit_grad, moved_grad * (unit - start)


CHUNK = 32
SCALE_ROWS = 16


def mlp_kernel(
    length, branch, tokens, alpha_attn, alpha_mlp, cotangent, up_gate, own_down,
    mixed, branch_low, token_grad, alpha_grads, weight_grads, scale_grads,
    hidden, hidden_grad, held, grads, ups, gates, inner, up_low, gate_low, own, cross, side,
    gather_send, gather_receive, cross_sem, side_sem, down, down_send, down_receive, down_local,
):
    x, z, y, c = here("x", "z", "y", "c")
    rows, width = branch.shape
    owners, units = length, own_down.shape[0]
    full = owners * units
    q0 = x * 2 + y
    greet(plane_neighbours() + [(z > 0, {"z": z - 1}), (z < length - 1, {"z": z + 1})])
    line = LineGather(length, own_down, down, down_send, down_receive, down_local)
    line.start()
    done = []

    def each_chunk(body, h):
        def step(i, carry):
            start = pl.multiple_of(i * CHUNK, CHUNK)
            body(pl.ds(start, CHUNK), pl.ds(pl.multiple_of(c * rows + start, CHUNK), CHUNK))
            return carry

        chunks = rows // CHUNK // 2
        lax.fori_loop(h * chunks, (h + 1) * chunks, step, 0)

    def each_half(body):
        def step(i, carry):
            body(pl.ds(pl.multiple_of(i * rows, rows), rows))
            return carry

        lax.fori_loop(0, 2, step, 0)

    def weight(i):
        return up_gate[:, i, :units].reshape(full, width)

    def scale(i):
        rows_of = [up_gate[k, i, units : units + SCALE_ROWS, :units].astype(f32)[:1] for k in range(length)]
        return jnp.concatenate(rows_of, axis=1)

    up_scale, gate_scale = scale(0), scale(1)

    def down_weight():
        return down[...].reshape(full, width)

    def half_rows(half):
        return pl.ds(pl.multiple_of(half * rows, rows), rows)

    alpha_grads[...] = jnp.zeros_like(alpha_grads)
    scale_grads[...] = jnp.zeros_like(scale_grads)

    def enter(part, place):
        result = step_forward(branch[part], tokens[part].astype(f32), alpha_attn[...])[0]
        hidden[part] = result
        held[q0, place] = result.astype(bf16)

    def forward(q):
        def half(part):
            block = held[q, part]
            up = dot(block, weight(0), 1, 1)
            gate = dot(block, weight(1), 1, 1)
            ups[q, part] = up
            gates[q, part] = gate
            gated = gate * gate_scale
            inner[q, part] = (up * up_scale * (gated * jax.nn.sigmoid(gated))).astype(bf16)

        each_half(half)
        done.append(q)
        if len(done) in (1, 3):
            line.wait(len(done) // 2 + 1)
            line.hand_on(len(done) // 2 + 1)

    def forward_end():
        for d in range(3, length):
            line.wait(d)
            line.hand_on(d)
        for d in range(length - 1):
            line.sent(d)

    out = PlaneScatter(
        lambda q, half: dot(inner[q, half_rows(half)], down_weight(), 1, 0),
        own, cross, side, cross_sem.at[0], side_sem.at[0],
    )

    def forward_corner():
        forward_end()
        out.begin()

    plane_gather(
        held, gather_send.at[0], gather_receive.at[0], lambda h: each_chunk(enter, h), forward, forward_corner
    )
    out.end()

    def turn_back(part, place):
        start, alpha = hidden[part], alpha_mlp[...]
        result, unit, target_scale, moved_scale = step_forward(own[q0, part], start, alpha)
        mixed[part] = result.astype(bf16)
        target_grad, start_grad, alpha_part = step_back(
            cotangent[part].astype(f32), result, unit, target_scale, moved_scale, start, alpha
        )
        alpha_grads[1:2] += jnp.sum(alpha_part, axis=0, keepdims=True)
        hidden_grad[part] = start_grad
        grads[q0, place] = target_grad.astype(bf16)

    def backward(q):
        def half(part):
            inner_grad = dot(grads[q, part], down_weight(), 1, 1)
            up, gate = ups[q, part], gates[q, part]
            gated = gate * gate_scale
            share = jax.nn.sigmoid(gated)
            silu = gated * share
            lifted = inner_grad * up
            gated_grad = lifted * up_scale * (share * (1.0 + gated * (1.0 - share)))
            up_low[q, part] = (inner_grad * up_scale * silu).astype(bf16)
            gate_low[q, part] = (gated_grad * gate_scale).astype(bf16)
            scale_grads[0:1] += jnp.sum(lifted * silu, axis=0, keepdims=True)
            scale_grads[1:2] += jnp.sum(gated_grad * gate, axis=0, keepdims=True)

        each_half(half)

    def weights_back():
        tall = 4 * 2 * rows
        for i, (left, right) in enumerate(((up_low, held), (gate_low, held), (inner, grads))):

            def step(n, carry):
                columns = pl.ds(pl.multiple_of(n * BLOCK, BLOCK), BLOCK)
                product = dot(
                    left[...].reshape(tall, full), right[:, :, columns].reshape(tall, BLOCK), 0, 0
                )
                weight_grads[:, i, :, columns] = product.astype(bf16).reshape(owners, units, BLOCK)
                return carry

            lax.fori_loop(0, width // BLOCK, step, 0)

    back = PlaneScatter(
        lambda q, half: dot(up_low[q, half_rows(half)], weight(0), 1, 0)
        + dot(gate_low[q, half_rows(half)], weight(1), 1, 0),
        own, cross, side, cross_sem.at[1], side_sem.at[1],
    )
    plane_gather(
        grads, gather_send.at[1], gather_receive.at[1], lambda h: each_chunk(turn_back, h), backward, back.begin
    )
    back.end(weights_back)

    def leave(part, place):
        start, alpha = tokens[part].astype(f32), alpha_attn[...]
        result, unit, target_scale, moved_scale = step_forward(branch[part], start, alpha)
        target_grad, start_grad, alpha_part = step_back(
            hidden_grad[part] + own[q0, part], result, unit, target_scale, moved_scale, start, alpha
        )
        alpha_grads[0:1] += jnp.sum(alpha_part, axis=0, keepdims=True)
        branch_low[part] = target_grad.astype(bf16)
        token_grad[part] = start_grad

    for h in (0, 1):
        each_chunk(leave, h)


def mlp(length, branch, tokens, alpha_attn, alpha_mlp, cotangent, up_gate, down):
    rows, width = branch.shape
    owners, units = length, down.shape[0]
    full = owners * units
    low, wide = like((rows, width), bf16), like((rows, width), f32)
    scratch = [
        pltpu.VMEM((rows, width), f32),
        pltpu.VMEM((rows, width), f32),
        pltpu.VMEM((4, 2 * rows, width), bf16),
        pltpu.VMEM((4, 2 * rows, width), bf16),
        pltpu.VMEM((4, 2 * rows, full), f32),
        pltpu.VMEM((4, 2 * rows, full), f32),
        pltpu.VMEM((4, 2 * rows, full), bf16),
        pltpu.VMEM((4, 2 * rows, full), bf16),
        pltpu.VMEM((4, 2 * rows, full), bf16),
        pltpu.VMEM((4, rows, width), f32),
        pltpu.VMEM((2, 4, rows, width), bf16),
        pltpu.VMEM((2, 3, rows, width), bf16),
        pltpu.SemaphoreType.DMA((2, 3, 8)),
        pltpu.SemaphoreType.DMA((2, 16)),
        pltpu.SemaphoreType.DMA((2, 2, 4)),
        pltpu.SemaphoreType.DMA((2, 2, 3, 2)),
        pltpu.VMEM((length, *down.shape), bf16),
    ] + line_gather_semaphores(length)
    return remote_call(
        functools.partial(mlp_kernel, length), "mlp", 5,
        (low, low, wide, like((2, width), f32), like((owners, 3, units, width), bf16), like((2, full), f32)),
        (IN_VMEM,) * 6, [IN_VMEM] * 7, scratch,
        branch, tokens, alpha_attn, alpha_mlp, cotangent, up_gate, down,
    )


def shards(
    tokens, lengths, w_query, w_key, w_value, s_qk, w_out, up_weight, gate_weight, down_weight,
    s_up, s_gate, alpha_attn, alpha_mlp, cotangent,
):
    outer = lax.axis_size("o")
    own_units = up_weight.shape[0]
    if outer > 1:
        up_weight, gate_weight, down_weight, s_up, s_gate = (
            gather(a, "o") for a in (up_weight, gate_weight, down_weight, s_up, s_gate)
        )
    units = up_weight.shape[0]
    scales = jnp.zeros((2, SCALE_ROWS, up_weight.shape[1]), bf16)
    scales = scales.at[:, 0, :units].set(jnp.stack([s_up, s_gate]))
    up_gate = jnp.concatenate([jnp.stack([up_weight, gate_weight]), scales], axis=1)

    length = lax.axis_size("z")
    projections = w_query.T, w_key.T, w_value.T
    group_tokens, turned_q, turned_k, cosine, sine, qt, kt, vt, up_gate, branch, ot, lse = attention(
        length, lengths, tokens, *projections, s_qk[None], w_out, up_gate
    )
    mixed, branch_low, token_grad, alpha_grads, mlp_grads, scale_grads = mlp(
        length, branch, tokens, alpha_attn[None], alpha_mlp[None], cotangent, up_gate, down_weight,
    )
    tokens_grad, attn_grads, alpha_sums, scale_sums, gain_grad, mlp_grads = back(
        length, lengths, branch_low, w_out, qt, kt, vt, ot, lse, mlp_grads, turned_q, turned_k, s_qk[None],
        cosine, sine, *projections, alpha_grads, scale_grads, token_grad, group_tokens,
    )
    if outer > 1:
        mlp_grads = lax.psum_scatter(mlp_grads, "o", scatter_dimension=1, tiled=True)
        attn_grads, alpha_sums, scale_sums, gain_grad = lax.psum(
            (attn_grads, alpha_sums, scale_sums, gain_grad), "o"
        )
    place = lax.axis_index("z") * units + lax.axis_index("o") * own_units
    scale_sums = lax.dynamic_slice_in_dim(scale_sums, place, own_units, 1)
    return (
        mixed,
        tokens_grad,
        attn_grads[:HEAD_DIM].T,
        attn_grads[HEAD_DIM : 2 * HEAD_DIM].T,
        attn_grads[2 * HEAD_DIM : 3 * HEAD_DIM].T,
        gain_grad[0],
        attn_grads[3 * HEAD_DIM :],
        mlp_grads[0],
        mlp_grads[1],
        mlp_grads[2],
        scale_sums[0],
        scale_sums[1],
        alpha_sums[0],
        alpha_sums[1],
    )


def solution(mesh):
    dp, head = mesh.shape["dp"], mesh.shape["head"]
    fine = Mesh(mesh.devices.reshape(dp // 2, 2, head // 4, 2, 2), AXES)
    group, rows, heads = P(("o", "x"), None), P(AXES, None), P(None, GROUP)
    in_specs = (
        rows, group, heads, heads, heads, P(GROUP), P(GROUP, None), rows, rows, rows,
        P(AXES), P(AXES), P(), P(), rows,
    )
    out_specs = (
        rows, rows, heads, heads, heads, P(GROUP), P(GROUP, None), rows, rows, rows,
        P(AXES), P(AXES), P(), P(),
    )
    return jax.shard_map(
        shards, mesh=fine, in_specs=in_specs, out_specs=out_specs, check_vma=False
    )
```

```python
import functools
import math

import jax
import jax.numpy as jnp
from jax import lax
from jax.experimental import pallas as pl
from jax.experimental.pallas import tpu as pltpu
from jax.sharding import Mesh
from jax.sharding import PartitionSpec as P

HEAD_DIM = 64
BLOCK = 512
REACH = 4
EPSILON = 1e-06
ROOT = math.sqrt(HEAD_DIM)
SCORE_SCALE = math.log2(math.e) / ROOT
AXES = ("o", "x", "z", "y", "c")
GROUP = ("z", "y", "c")
f32, bf16 = jnp.float32, jnp.bfloat16
VMEM_LIMIT = 60 * 2**20


def dot(left, right, left_dim, right_dim):
    return lax.dot_general(
        left, right, (((left_dim,), (right_dim,)), ((), ())), preferred_element_type=f32
    )


def unit_start(lengths, unit):
    start, end = jnp.int32(0), jnp.int32(0)
    for j in range(lengths.shape[1]):
        end = end + lengths[0, j]
        start = jnp.where(unit >= end, end, start)
    return start


def causal(weights):
    key = lax.broadcasted_iota(jnp.int32, weights.shape, 0)
    query = lax.broadcasted_iota(jnp.int32, weights.shape, 1)
    return jnp.where(key <= query, weights, 0.0)


def block_columns(index):
    return pl.ds(pl.multiple_of(index * BLOCK, BLOCK), BLOCK)


def barred(lengths, unit, back):
    return jnp.where(unit - back >= unit_start(lengths, unit), 0.0, 1e30).astype(f32)


def attend(lengths, unit, qt, kt, vt, ot, lse, total, attended):
    columns = block_columns(unit)

    def part(back):
        keys = block_columns(unit - back)
        scores = dot(kt[:, keys], qt[:, columns], 0, 0) * SCORE_SCALE
        if back == 0:
            weights = causal(jnp.exp2(scores))
        else:
            weights = jnp.exp2(scores - barred(lengths, unit, back))
        sums = jnp.sum(weights, axis=0, keepdims=True)
        values = dot(vt[:, keys], weights.astype(bf16), 1, 0)
        if back == 0:
            total[...] = sums
            attended[...] = values
        else:
            total[...] += sums
            attended[...] += values

    part(0)
    for back in range(1, REACH):
        pl.when(unit >= back)(functools.partial(part, back))
    ot[:, columns] = (attended[...] * (1.0 / total[...])).astype(bf16)
    lse[:, columns] = jnp.log2(total[...])


def attend_back(lengths, unit, qt, kt, vt, ot, got, lse, gqt, gkt, gvt):
    columns = block_columns(unit)
    query, grad = qt[:, columns], got[...]
    inner = jnp.sum(grad.astype(f32) * ot[:, columns].astype(f32), axis=0, keepdims=True)

    def part(back):
        keys = block_columns(unit - back)
        key, value = kt[:, keys], vt[:, keys]
        log_total = lse[:, columns]
        if back > 0:
            log_total = log_total + barred(lengths, unit, back)
        weights = jnp.exp2(dot(key, query, 0, 0) * SCORE_SCALE - log_total)
        if back == 0:
            weights = causal(weights)
        score_grad = (weights * (dot(value, grad, 0, 0) - inner)).astype(bf16)
        gkt[:, keys] += dot(query, score_grad, 1, 1)
        gvt[:, keys] += dot(grad, weights.astype(bf16), 1, 1)
        gqt[:, columns] += dot(key, score_grad, 1, 0)

    part(0)
    for back in range(1, REACH):
        pl.when(unit >= back)(functools.partial(part, back))


def turn_table(lengths, unit):
    shape = (HEAD_DIM // 2, BLOCK)
    first = (unit - unit_start(lengths, unit)) * BLOCK
    place = (first + lax.broadcasted_iota(jnp.int32, shape, 1)).astype(f32)
    turns = lax.broadcasted_iota(jnp.int32, shape, 0).astype(f32)
    angle = place * jnp.exp(turns * (-2.0 * math.log(10000.0) / HEAD_DIM))
    return jnp.cos(angle), jnp.sin(angle)


def as_column(row):
    n = row.shape[1]
    same = lax.broadcasted_iota(jnp.int32, (n, n), 0) == lax.broadcasted_iota(jnp.int32, (n, n), 1)
    return jnp.sum(jnp.where(same, row, 0.0), axis=1, keepdims=True)


def as_row(column):
    n = column.shape[0]
    same = lax.broadcasted_iota(jnp.int32, (n, n), 0) == lax.broadcasted_iota(jnp.int32, (n, n), 1)
    return jnp.sum(jnp.where(same, column, 0.0), axis=0, keepdims=True)


def join(joint, *parts):
    for i, part in enumerate(parts):
        joint[i * HEAD_DIM : (i + 1) * HEAD_DIM] = part[...]


def turn(values, cosine, sine):
    half = HEAD_DIM // 2
    a, b = values[:half], values[half:]
    return jnp.concatenate([a * cosine - b * sine, b * cosine + a * sine], axis=0)


def unit_features(turned):
    scale = lax.rsqrt(jnp.mean(turned * turned, axis=0, keepdims=True) + EPSILON)
    return turned * scale, scale


def gather(values, axes):
    return lax.all_gather(values, axes, axis=0, tiled=True)


MESH_ID = pl.DeviceIdType.MESH


def here(*names):
    return tuple(lax.axis_index(name) for name in names)


def greet(neighbours):
    barrier = pltpu.get_barrier_semaphore()
    count = jnp.int32(0)
    for condition, device in neighbours:

        @pl.when(condition)
        def _():
            pl.semaphore_signal(barrier, inc=1, device_id=device, device_id_type=MESH_ID)

        count = count + jnp.where(condition, 1, 0)
    pl.semaphore_wait(barrier, count)


def remote(source, target, send, receive, device):
    return pltpu.make_async_remote_copy(
        src_ref=source,
        dst_ref=target,
        send_sem=send,
        recv_sem=receive,
        device_id=device,
        device_id_type=MESH_ID,
    )


def line_order(z, length, step):
    picked = jnp.int32(0)
    for at in range(length):
        order = sorted(range(length), key=lambda p: (abs(p - at), p))
        picked = jnp.where(z == at, order[step], picked)
    return picked


def group_neighbours(length):
    z, y, c = here("z", "y", "c")
    return [
        (z > 0, {"z": z - 1}),
        (z < length - 1, {"z": z + 1}),
        (z >= 0, {"y": 1 - y}),
        (z >= 0, {"c": 1 - c}),
    ]


def group_gather(length, own, held, send, receive, on_unit, at_step=None):
    z, y, c = here("z", "y", "c")
    rows = held.shape[1] // 2
    half = rows // 2

    def copy(kind, zz, yy, cc, h, device):
        at = held.at[zz * 2 + yy, pl.ds(pl.multiple_of(cc * rows + h * half, half), half)]
        number = ((zz * 2 + yy) * 2 + cc) * 2 + h
        return remote(at, at, send.at[kind, number], receive.at[number], device)

    def arrived(zz, yy, cc, h):
        copy(3, zz, yy, cc, h, {"c": 1 - c}).wait_recv()

    def come(distance):
        if distance == 0:
            return [(z, z >= 0, [(0, z < length - 1, {"z": z + 1}), (1, z > 0, {"z": z - 1})])]
        return [
            (z - distance, z >= distance, [(0, z < length - 1, {"z": z + 1})]),
            (z + distance, z + distance < length, [(1, z > 0, {"z": z - 1})]),
        ]

    def passed_on(zz, h, along, act):
        for kind, goes, device in along:

            @pl.when(goes)
            def _():
                act(copy(kind, zz, y, c, h, device))

        act(copy(2, zz, y, c, h, {"y": 1 - y}))
        act(copy(3, zz, y, c, h, {"c": 1 - c}))

    held[z * 2 + y, pl.ds(pl.multiple_of(c * rows, rows), rows)] = own[...]
    order = [line_order(z, length, step) for step in range(length)]
    for tick in range(2 * length + 1):
        step, h = divmod(tick, 2)
        before, last_h = divmod(tick - 1, 2)
        if step < length:
            for zz, there, along in come(step):

                @pl.when(there)
                def _():
                    if step > 0:
                        arrived(zz, y, c, h)
                    passed_on(zz, h, along, lambda copy_: copy_.start())

        if before >= 0:
            arrived(order[before], 1 - y, c, last_h)
            copy(3, order[before], 1 - y, c, last_h, {"c": 1 - c}).start()
        if at_step is not None and h == 0:
            at_step(step)
        if h == 1:
            for i in (0, 1):
                arrived(order[step], y, 1 - c, i)
            on_unit(order[step] * 2 + y)
        if last_h == 1 and before >= 0:
            for i in (0, 1):
                arrived(order[before], 1 - y, 1 - c, i)
            on_unit(order[before] * 2 + 1 - y)
    for h in (0, 1):
        for step in range(length):
            for zz, there, along in come(step):

                @pl.when(there)
                def _():
                    passed_on(zz, h, along, lambda copy_: copy_.wait_send())

            copy(3, order[step], 1 - y, c, h, {"c": 1 - c}).wait_send()


GATHER_SEMAPHORES = 4


def gather_scratch(units, rows, width):
    return [
        pltpu.VMEM((units, 2 * rows, width), bf16),
        pltpu.SemaphoreType.DMA((GATHER_SEMAPHORES, 4 * units)),
        pltpu.SemaphoreType.DMA((4 * units,)),
    ]


def scatter_scratch(length, rows, width):
    return [
        pltpu.VMEM((length + 1, rows, width), f32),
        pltpu.VMEM((2 * length + 4, rows, width), bf16),
        pltpu.VMEM((2, length, rows, width), bf16),
        pltpu.VMEM((3, length, rows, width), bf16),
        pltpu.SemaphoreType.DMA((2, 2 * length)),
        pltpu.SemaphoreType.DMA((2, length, 2)),
        pltpu.SemaphoreType.DMA((3, length, 2)),
    ]


def group_scatter(length, produce, finish, own, cross, across, along, cross_sem, across_sem, along_sem, prepare=None, between=None, at_step=None):
    z, y, c = here("z", "y", "c")

    def to_core(unit, slot=0):
        source = cross.at[2 * length + slot]
        return remote(source, cross.at[unit], cross_sem.at[0, unit], cross_sem.at[1, unit], {"c": 1 - c})

    half = own.shape[1] // 2

    def part(h):
        return pl.ds(h * half, half)

    def to_y(zz, h):
        return remote(
            across.at[0, zz, part(h)], across.at[1, zz, part(h)], across_sem.at[0, zz, h],
            across_sem.at[1, zz, h], {"y": 1 - y},
        )

    def to_z(zz, slot, h, device):
        return remote(
            along.at[0, zz, part(h)], along.at[slot, zz, part(h)], along_sem.at[0, zz, h],
            along_sem.at[slot, zz, h], device,
        )

    def from_z(zz, slot, h):
        to_z(zz, slot, h, {"c": 1 - c}).wait_recv()
        return along[slot, zz, part(h)].astype(f32)

    order = [line_order(z, length, length - 1 - step) for step in range(length)]

    def give(unit, slot):
        cross[2 * length + slot] = produce(unit, 1 - c).astype(bf16)
        to_core(unit, slot).start()

    def first(step):
        zz = order[step]
        slot = 2 * (step % 2)
        if step >= 2:
            for yy in (0, 1):
                to_core(order[step - 2] * 2 + yy).wait_send()
        there, here_ = zz * 2 + 1 - y, zz * 2 + y
        if prepare is not None:
            prepare(there)
        give(there, slot)
        own[length] = produce(there, c)
        if prepare is not None:
            prepare(here_)
        to_core(there).wait_recv()
        across[0, zz] = (own[length] + cross[there].astype(f32)).astype(bf16)
        for h in (0, 1):
            to_y(zz, h).start()
        give(here_, slot + 1)
        own[zz] = produce(here_, c)

    def third(zz, h, last):
        unit = zz * 2 + y
        if h == 0:
            to_core(unit).wait_recv()
        own[zz, part(h)] += cross[unit, part(h)].astype(f32)
        to_y(zz, h).wait_recv()
        own[zz, part(h)] += across[1, zz, part(h)].astype(f32)

        @pl.when((zz >= z) & (z > 0))
        def _():
            own[zz, part(h)] += from_z(zz, 1, h)

        @pl.when((zz <= z) & (z < length - 1))
        def _():
            own[zz, part(h)] += from_z(zz, 2, h)

        if last:
            finish(h, own[zz, part(h)])
            return
        along[0, zz, part(h)] = own[zz, part(h)].astype(bf16)

        @pl.when(zz > z)
        def _():
            to_z(zz, 1, h, {"z": z + 1}).start()

        @pl.when(zz < z)
        def _():
            to_z(zz, 2, h, {"z": z - 1}).start()

    for step in range(length + 1):
        if step < length:
            first(step)
        if at_step is not None:
            at_step(step)
        if step == length - 1 and between is not None:
            between()
        if step >= 1:
            for h in (0, 1):
                third(order[step - 1], h, step == length)
    for step in range(length):
        zz = order[step]
        if step >= length - 2:
            for yy in (0, 1):
                to_core(zz * 2 + yy).wait_send()
        for h in (0, 1):
            to_y(zz, h).wait_send()
            if step < length - 1:
                to_z(zz, 1, h, {"c": 1 - c}).wait_send()


def remote_call(kernel, name, number, outs, out_specs, in_specs, scratch, *operands):
    return pl.pallas_call(
        kernel,
        name=name,
        out_shape=outs,
        in_specs=in_specs,
        out_specs=out_specs,
        scratch_shapes=scratch,
        compiler_params=pltpu.CompilerParams(
            collective_id=number, has_side_effects=True, vmem_limit_bytes=VMEM_LIMIT
        ),
    )(*operands)


IN_VMEM = pl.BlockSpec(memory_space=pltpu.VMEM)
IN_SMEM = pl.BlockSpec(memory_space=pltpu.SMEM)
ANYWHERE = pl.BlockSpec(memory_space=pl.ANY)


def like(shape, dtype):
    return jax.ShapeDtypeStruct(shape, dtype)


class LineGather:
    def __init__(self, length, own, held, send, receive, local_sem):
        self.length, self.own, self.held = length, own, held
        self.sems, self.local_sem = (send, receive), local_sem
        self.z = lax.axis_index("z")

    def copy(self, way, zz, source=None):
        send, receive = self.sems
        at = self.held.at[zz]
        device = {"z": self.z + 1} if way == 0 else {"z": self.z - 1}
        return remote(at if source is None else source, at, send.at[way, zz], receive.at[zz], device)

    def ways(self, d, act):
        z, length = self.z, self.length
        for way, zz, there, more in (
            (0, z - d, z - d >= 0, z < length - 1),
            (1, z + d, z + d < length, z > 0),
        ):
            act(way, zz, there, there & more)

    def start(self):
        pltpu.make_async_copy(self.own, self.held.at[self.z], self.local_sem).start()
        self.hand_on(0)

    def hand_on(self, d):
        def begin(way, zz, there, more):
            @pl.when(more)
            def _():
                self.copy(way, zz, self.own if d == 0 else None).start()

        self.ways(d, begin)

    def wait(self, d):
        def arrive(way, zz, there, more):
            @pl.when(there)
            def _():
                self.arrival(way, zz).wait_recv()

        self.ways(d, arrive)

    def sent(self, d):
        def leave(way, zz, there, more):
            @pl.when(more)
            def _():
                self.copy(way, zz, self.own if d == 0 else None).wait_send()

        self.ways(d, leave)
        if d == 0:
            pltpu.make_async_copy(self.own, self.held.at[self.z], self.local_sem).wait()

    def arrival(self, way, zz):
        send, receive = self.sems
        at = self.held.at[zz]
        return remote(at, at, send.at[way, zz], receive.at[zz], {"c": 1 - lax.axis_index("c")})


def line_gather_semaphores(length):
    return [
        pltpu.SemaphoreType.DMA((2, length)),
        pltpu.SemaphoreType.DMA((length,)),
        pltpu.SemaphoreType.DMA,
    ]


class LineScatter:
    def __init__(self, length, parts, rest, out, into, send_sem, receive_sem):
        self.length, self.parts, self.rest = length, parts, rest
        self.out, self.into, self.sems = out, into, (send_sem, receive_sem)
        self.z = lax.axis_index("z")

    def copy(self, way, d, source):
        send, receive = self.sems
        device = {"z": self.z + 1} if way == 0 else {"z": self.z - 1}
        return remote(source, self.into.at[way, d - 2], send.at[way, d - 2], receive.at[way, d - 2], device)

    def arrived(self, way, d):
        send, receive = self.sems
        at = self.into.at[way, d - 2]
        device = {"c": 1 - lax.axis_index("c")}
        remote(at, at, send.at[way, d - 2], receive.at[way, d - 2], device).wait_recv()

    def cases(self, d, alone, joined):
        z, length = self.z, self.length
        for way, dest, valid, behind in (
            (0, z + d, z + d < length, z > 0),
            (1, z - d, z - d >= 0, z < length - 1),
        ):
            behind = behind if d < length - 1 else z < 0
            pl.when(valid & jnp.logical_not(behind))(functools.partial(alone, way, dest))
            pl.when(valid & behind)(functools.partial(joined, way, dest))

    def joint(self, way, dest, d):
        self.arrived(way, d + 1)
        return (self.parts[dest].astype(f32) + self.into[way, d - 1].astype(f32)).astype(bf16)

    def send(self, d):
        def alone(way, dest):
            self.copy(way, d, self.parts.at[dest]).start()

        def joined(way, dest):
            self.out[way, d - 2] = self.joint(way, dest, d)
            self.copy(way, d, self.out.at[way, d - 2]).start()

        self.cases(d, alone, joined)

    def finish(self):
        def alone(way, dest):
            self.rest[way] = self.parts[dest]

        def joined(way, dest):
            self.rest[way] = self.joint(way, dest, 1)

        self.cases(1, alone, joined)
        for d in range(2, self.length):

            def left(way, dest):
                self.copy(way, d, self.parts.at[dest]).wait_send()

            self.cases(d, left, left)


def line_scatter_scratch(parts):
    length = parts.shape[0]
    hops = (2, length - 2, *parts.shape[1:])
    joint = (2, max(length - 3, 1), *parts.shape[1:])
    return [pltpu.VMEM(joint, bf16), pltpu.VMEM(hops, bf16)] + [pltpu.SemaphoreType.DMA(hops[:2])] * 2


def half_columns(unit, half):
    rows = BLOCK // 2
    return pl.ds(pl.multiple_of(unit * BLOCK + half * rows, rows), rows)


def attention_kernel(
    length, lengths, tokens, w_query, w_key, w_value, gain_row, w_out, weight,
    gathered, turned_q, turned_k, cosine, sine, qt, kt, vt, weights, branch, ot, lse,
    joint, held, send, receive, out_sem, line_send, line_receive, line_local, total, attended, *scratch,
):
    greet(group_neighbours(length))
    line = LineGather(length, weight, weights, line_send, line_receive, line_local)
    join(joint, w_query, w_key, w_value)
    gain = as_column(gain_row[...])

    def start_line(step):
        if step == length - 1:
            line.start()

    def on_unit(unit):
        pltpu.make_async_copy(held.at[unit], gathered.at[unit], out_sem.at[unit]).start()
        columns = block_columns(unit)
        projected = dot(joint[...], held[unit], 1, 1)
        cosine[:, columns], sine[:, columns] = turn_table(lengths, unit)
        for part, turned, features in ((0, turned_q, qt), (1, turned_k, kt)):
            values = turn(
                projected[part * HEAD_DIM : (part + 1) * HEAD_DIM], cosine[:, columns], sine[:, columns]
            )
            turned[:, columns] = values
            features[:, columns] = (unit_features(values)[0] * gain).astype(bf16)
        vt[:, columns] = projected[2 * HEAD_DIM :].astype(bf16)

    group_gather(length, tokens, held, send, receive, on_unit, start_line)
    line.wait(1)
    line.hand_on(1)

    def move_line(step):
        if 2 <= step < length - 1:
            line.wait(step)
            line.hand_on(step)

    def finish(h, total):
        branch[pl.ds(h * total.shape[0], total.shape[0])] = total

    group_scatter(
        length, lambda unit, half: dot(ot[:, half_columns(unit, half)], w_out[...], 0, 0), finish, *scratch,
        prepare=lambda unit: attend(lengths, unit, qt, kt, vt, ot, lse, total, attended), at_step=move_line,
    )
    line.wait(length - 1)
    for d in range(length - 1):
        line.sent(d)
    for unit in range(2 * length):
        pltpu.make_async_copy(held.at[unit], gathered.at[unit], out_sem.at[unit]).wait()


def attention(length, lengths, tokens, w_query, w_key, w_value, gain, w_out, weight):
    rows, width = tokens.shape
    units = 2 * length
    total = units * 2 * rows
    wide, narrow = like((HEAD_DIM, total), f32), like((HEAD_DIM, total), bf16)
    table = like((HEAD_DIM // 2, total), f32)
    return remote_call(
        functools.partial(attention_kernel, length), "attention", 1,
        (
            like((units, 2 * rows, width), bf16), wide, wide, table, table, narrow, narrow, narrow,
            like((length, *weight.shape), bf16), like((rows, width), f32), narrow, like((1, total), f32),
        ),
        (ANYWHERE,) + (IN_VMEM,) * 7 + (ANYWHERE,) + (IN_VMEM,) * 3, [IN_SMEM] + [IN_VMEM] * 6 + [ANYWHERE],
        [pltpu.VMEM((3 * HEAD_DIM, width), bf16)] + gather_scratch(units, rows, width) + [pltpu.SemaphoreType.DMA((units,))]
        + line_gather_semaphores(length) + [pltpu.VMEM((1, BLOCK), f32), pltpu.VMEM((HEAD_DIM, BLOCK), f32)]
        + scatter_scratch(length, rows, width),
        lengths, tokens, w_query, w_key, w_value, gain, w_out, weight,
    )


def flip(position, bit):
    return position + bit - 2 * bit * ((position // bit) % 2)


def back_kernel(
    length, lengths, grad, w_out, qt, kt, vt, ot, lse, parts, turned_q, turned_k, gain_row, cosine, sine,
    w_query, w_key, w_value, alpha_grads, scale_grads, direct, gathered,
    token_grad, weight_grads, alpha_sums, scale_sums, gain_grad, sums,
    joint, out_grad, gqt, gkt, gvt, got, rest, arrivals, rest_sem, grads, held_sem, gains, gain_sem, sent, taken,
    weight_sem, small_out, small_in, small_sem, line_out, line_into, line_send, line_receive,
    held, send, receive, *scratch,
):
    x, z, y, c = here("x", "z", "y", "c")
    to_x = {"x": 1 - x}
    bits = [1 << i for i in range(length.bit_length() - 1)]
    greet(group_neighbours(length) + [(x >= 0, to_x)] + [(x >= 0, {"z": flip(z, bit)}) for bit in bits])
    partners = [{"c": 1 - c}, {"y": 1 - y}, to_x] + [{"z": flip(z, bit)} for bit in bits]
    line = LineScatter(length, parts, rest, line_out, line_into, line_send, line_receive)
    join(joint, w_query, w_key, w_value)
    gain = as_column(gain_row[...])

    def spread_step(step):
        if step == 0:
            for array in (out_grad, gqt, gkt, gvt):
                array[...] = jnp.zeros_like(array)
        if step % 2 == 0 and step < 2 * (length - 2):
            line.send(length - 1 - step // 2)

    def on_unit(unit):
        columns = block_columns(unit)
        got[...] = dot(w_out[...], held[unit], 1, 1).astype(bf16)
        out_grad[...] += dot(ot[:, columns], held[unit], 1, 0)
        attend_back(lengths, unit, qt, kt, vt, ot, got, lse, gqt, gkt, gvt)

    group_gather(length, grad, held, send, receive, on_unit, spread_step)
    load = pltpu.make_async_copy(gathered, held, held_sem)
    load.start()
    line.finish()
    lines = [
        (remote(rest.at[way], arrivals.at[way], rest_sem.at[0, way], rest_sem.at[1, way], {"z": to}), goes, comes)
        for way, to, goes, comes in (
            (0, z + 1, z < length - 1, z > 0), (1, z - 1, z > 0, z < length - 1)
        )
    ]
    for last_hop, goes, _ in lines:
        pl.when(goes)(last_hop.start)
    gains[0] = jnp.zeros_like(gains[0])
    small_out[0] = jnp.zeros_like(small_out[0])
    small_out[0, 0:2] = alpha_grads[...]
    small_out[0, 2:4, : scale_grads.shape[1]] = scale_grads[...]

    def exchange(i):
        return remote(small_out.at[i], small_in.at[i], small_sem.at[0, i], small_sem.at[1, i], partners[i])

    def at_step(step):
        if 0 < step <= len(partners):
            exchange(step - 1).wait_recv()
            small_out[step] = small_out[step - 1]
            summed = 2 if step <= 3 else 4
            small_out[step, :summed] += small_in[step - 1, :summed]
        if step < len(partners):
            exchange(step).start()

    def prepare(unit):
        columns = block_columns(unit)
        for part, turned, outer in ((0, turned_q, gqt), (1, turned_k, gkt)):
            normal, scale = unit_features(turned[:, columns])
            grad = outer[:, columns] * (1.0 / ROOT)
            product = grad * normal
            width = gains.shape[2]
            for i in range(BLOCK // width):
                gains[0] += product[:, i * width : (i + 1) * width]
            grad = grad * gain
            grad = scale * (grad - normal * jnp.mean(grad * normal, axis=0, keepdims=True))
            grad = turn(grad, cosine[:, columns], -sine[:, columns])
            grads[part * HEAD_DIM : (part + 1) * HEAD_DIM, columns] = grad.astype(bf16)
        grads[2 * HEAD_DIM :, columns] = gvt[:, columns].astype(bf16)

    gain_copy = remote(gains.at[0], gains.at[1], gain_sem.at[0], gain_sem.at[1], to_x)
    weight_copy = remote(sent, taken, weight_sem.at[0], weight_sem.at[1], to_x)

    def between():
        gain_copy.start()
        load.wait()
        rows = grads.shape[1]
        product = dot(grads[...], held[...].reshape(rows, held.shape[2]), 1, 0)
        sent[: 3 * HEAD_DIM] = product.astype(bf16)
        sent[3 * HEAD_DIM :] = out_grad[...].astype(bf16)
        weight_copy.start()

    def finish(h, total):
        part = pl.ds(h * total.shape[0], total.shape[0])
        token_grad[part] = (direct[part] + total).astype(bf16)

    group_scatter(
        length, lambda unit, half: dot(grads[:, half_columns(unit, half)], joint[...], 0, 0), finish, *scratch,
        prepare=prepare, between=between, at_step=at_step,
    )
    for step in range(length + 1, len(partners) + 1):
        at_step(step)
    alpha_sums[...] = small_out[len(partners), 0:2]
    scale_sums[...] = small_out[len(partners), 2:4, : scale_sums.shape[1]]
    sums[...] = parts[z].astype(f32)
    for way, (last_hop, goes, comes) in enumerate(lines):

        @pl.when(comes)
        def _():
            remote(
                arrivals.at[way], arrivals.at[way], rest_sem.at[0, way], rest_sem.at[1, way], {"c": 1 - c}
            ).wait_recv()
            sums[...] += arrivals[way].astype(f32)

        pl.when(goes)(last_hop.wait_send)
    gain_copy.wait()
    gain_grad[...] = as_row(jnp.sum(gains[0] + gains[1], axis=1, keepdims=True))
    weight_copy.wait()
    weight_grads[...] = sent[...].astype(f32) + taken[...].astype(f32)
    for i in range(len(partners)):
        exchange(i).wait_send()


def back(length, lengths, grad, w_out, qt, kt, vt, ot, lse, parts, *operands):
    rows, width = grad.shape
    units = 2 * length
    total = qt.shape[1]
    alpha_grads, scale_grads, direct, gathered = operands[-4:]
    exchanges = 3 + length.bit_length() - 1
    small = (exchanges + 1, 4, width)
    weights = (4 * HEAD_DIM, width)
    wide = pltpu.VMEM((HEAD_DIM, total), f32)
    hops = pltpu.VMEM((2, *parts.shape[1:]), bf16)
    scratch = [
        pltpu.VMEM((3 * HEAD_DIM, width), bf16), pltpu.VMEM(w_out.shape, f32), wide, wide, wide, pltpu.VMEM((HEAD_DIM, BLOCK), bf16), hops, hops,
        pltpu.SemaphoreType.DMA((2, 2)),
        pltpu.VMEM((3 * HEAD_DIM, total), bf16),
        pltpu.SemaphoreType.DMA,
        pltpu.VMEM((2, HEAD_DIM, 128), f32),
        pltpu.SemaphoreType.DMA((2,)),
        pltpu.VMEM(weights, bf16),
        pltpu.VMEM(weights, bf16),
        pltpu.SemaphoreType.DMA((2,)),
        pltpu.VMEM(small, f32),
        pltpu.VMEM(small, f32),
        pltpu.SemaphoreType.DMA((2, exchanges)),
    ]
    return remote_call(
        functools.partial(back_kernel, length), "back", 4,
        (
            like((rows, width), bf16), like(weights, f32), like(alpha_grads.shape, f32),
            like(scale_grads.shape, f32), like((1, HEAD_DIM), f32), like(parts.shape[1:], f32),
        ),
        (IN_VMEM,) * 6, [IN_SMEM] + [IN_VMEM] * 19 + [ANYWHERE],
        scratch + line_scatter_scratch(parts) + gather_scratch(units, rows, width)
        + scatter_scratch(length, rows, width),
        lengths, grad, w_out, qt, kt, vt, ot, lse, parts, *operands,
    )


def plane_neighbours():
    x, y, c = here("x", "y", "c")
    return [(x >= 0, {"x": 1 - x}), (x >= 0, {"y": 1 - y}), (x >= 0, {"c": 1 - c})]


def plane_gather(held, send, receive, make_half, on_pair, before_corner):
    x, y, c = here("x", "y", "c")
    rows = held.shape[1] // 2
    half = rows // 2
    q0, qx, qy, qd = x * 2 + y, (1 - x) * 2 + y, x * 2 + 1 - y, (1 - x) * 2 + 1 - y
    to_x, to_y, to_c = (0, {"x": 1 - x}), (1, {"y": 1 - y}), (2, {"c": 1 - c})

    def copy(way, q, cc, h):
        at = held.at[q, pl.ds(pl.multiple_of(cc * rows + h * half, half), half)]
        return remote(at, at, send.at[way[0], q * 2 + h], receive.at[(q * 2 + cc) * 2 + h], way[1])

    def arrived(q, cc, h):
        copy(to_c, q, cc, h).wait_recv()

    sent = []

    def start(way, q, h):
        sent.append((way, q, h))
        copy(way, q, c, h).start()

    for h in (0, 1):
        make_half(h)
        for way in (to_x, to_y, to_c):
            start(way, q0, h)
    for h in (0, 1):
        arrived(q0, 1 - c, h)
    on_pair(q0)
    arrived(qx, c, 0)
    start(to_y, qx, 0)
    start(to_c, qx, 0)
    arrived(qy, c, 0)
    start(to_c, qy, 0)
    arrived(qy, c, 1)
    start(to_x, qy, 1)
    start(to_c, qy, 1)
    arrived(qx, c, 1)
    start(to_c, qx, 1)
    for q in (qx, qy):
        for h in (0, 1):
            arrived(q, 1 - c, h)
        on_pair(q)
    before_corner()
    for h in (0, 1):
        arrived(qd, c, h)
        start(to_c, qd, h)
    for h in (0, 1):
        arrived(qd, 1 - c, h)
    on_pair(qd)
    for way, q, h in sent:
        copy(way, q, c, h).wait_send()


class PlaneScatter:
    def __init__(self, produce, own, cross, side, cross_sem, side_sem):
        self.produce, self.own, self.cross, self.side = produce, own, cross, side
        self.cross_sem, self.side_sem = cross_sem, side_sem
        x, y, self.c = here("x", "y", "c")
        self.half = own.shape[1] // 2
        self.chips = x * 2 + y, (1 - x) * 2 + y, x * 2 + 1 - y, (1 - x) * 2 + 1 - y
        self.to_x, self.to_y = {"x": 1 - x}, {"y": 1 - y}

    def to_core(self, q):
        cross, sem = self.cross, self.cross_sem
        return remote(cross.at[0, q], cross.at[1, q], sem.at[0, q], sem.at[1, q], {"c": 1 - self.c})

    def part(self, h):
        return pl.ds(h * self.half, self.half)

    def beside(self, kind, h, device):
        side, sem, part = self.side, self.side_sem, self.part(h)
        return remote(
            side.at[0, kind, part], side.at[1, kind, part], sem.at[0, kind, h], sem.at[1, kind, h], device
        )

    def first(self, q):
        self.cross[0, q] = self.produce(q, 1 - self.c).astype(bf16)
        self.to_core(q).start()
        self.own[q] = self.produce(q, self.c)

    def joined(self, q):
        self.to_core(q).wait_recv()
        self.own[q] += self.cross[1, q].astype(f32)

    def send(self, kind, q, h, device):
        self.side[0, kind, self.part(h)] = self.own[q, self.part(h)].astype(bf16)
        self.beside(kind, h, device).start()

    def add(self, q, kind, h, device):
        self.beside(kind, h, device).wait_recv()
        self.own[q, self.part(h)] += self.side[1, kind, self.part(h)].astype(f32)

    def begin(self):
        q0, qx, qy, qd = self.chips
        self.first(qx)
        self.first(qy)
        self.joined(qx)
        self.send(1, qx, 0, self.to_x)
        self.joined(qy)
        self.send(2, qy, 1, self.to_y)

    def end(self, between=None):
        q0, qx, qy, qd = self.chips
        to_x, to_y = self.to_x, self.to_y
        self.first(qd)
        self.joined(qd)
        self.send(0, qd, 0, to_x)
        self.send(0, qd, 1, to_y)
        self.first(q0)
        self.add(qx, 0, 1, to_y)
        self.send(1, qx, 1, to_x)
        self.add(qy, 0, 0, to_x)
        self.send(2, qy, 0, to_y)
        self.joined(q0)
        if between is not None:
            between()
        self.add(q0, 1, 0, to_x)
        self.add(q0, 2, 1, to_y)
        self.add(q0, 2, 0, to_y)
        self.add(q0, 1, 1, to_x)
        for q in self.chips:
            self.to_core(q).wait_send()
        self.beside(0, 0, to_x).wait_send()
        self.beside(0, 1, to_y).wait_send()
        for h in (0, 1):
            self.beside(1, h, to_x).wait_send()
            self.beside(2, h, to_y).wait_send()


def mean_of(values):
    return jnp.mean(values, axis=-1, keepdims=True)


def scale_of(values):
    return lax.rsqrt(mean_of(values * values) + EPSILON)


def step_forward(target, start, alpha):
    target_scale = scale_of(target)
    unit = target * target_scale
    moved = start + alpha * (unit - start)
    moved_scale = scale_of(moved)
    return moved * moved_scale, unit, target_scale, moved_scale


def step_back(grad, result, unit, target_scale, moved_scale, start, alpha):
    moved_grad = moved_scale * (grad - result * mean_of(grad * result))
    unit_grad = alpha * moved_grad
    target_grad = target_scale * (unit_grad - unit * mean_of(unit_grad * unit))
    return target_grad, moved_grad - unit_grad, moved_grad * (unit - start)


CHUNK = 128
SCALE_ROWS = 16


def mlp_kernel(
    length, branch, tokens, alpha_attn, alpha_mlp, cotangent, up_gate, own_down,
    mixed, branch_low, token_grad, alpha_grads, weight_grads, scale_grads,
    hidden, hidden_grad, held, grads, ups, gates, inner, up_low, gate_low, own, cross, side,
    gather_send, gather_receive, cross_sem, side_sem, down, down_send, down_receive, down_local,
):
    x, z, y, c = here("x", "z", "y", "c")
    rows, width = branch.shape
    owners, units = length, own_down.shape[0]
    full = owners * units
    q0 = x * 2 + y
    greet(plane_neighbours() + [(z > 0, {"z": z - 1}), (z < length - 1, {"z": z + 1})])
    line = LineGather(length, own_down, down, down_send, down_receive, down_local)
    line.start()
    done = []

    def each_chunk(body, h):
        def step(i, carry):
            start = pl.multiple_of(i * CHUNK, CHUNK)
            body(pl.ds(start, CHUNK), pl.ds(pl.multiple_of(c * rows + start, CHUNK), CHUNK))
            return carry

        chunks = rows // CHUNK // 2
        lax.fori_loop(h * chunks, (h + 1) * chunks, step, 0)

    def each_half(body):
        body(pl.ds(0, 2 * rows))

    def weight(i):
        return up_gate[:, i, :units].reshape(full, width)

    def scale(i):
        rows_of = [up_gate[k, i, units : units + SCALE_ROWS, :units].astype(f32)[:1] for k in range(length)]
        return jnp.concatenate(rows_of, axis=1)

    up_scale, gate_scale = scale(0), scale(1)

    def down_weight():
        return down[...].reshape(full, width)

    def half_rows(half):
        return pl.ds(pl.multiple_of(half * rows, rows), rows)

    alpha_grads[...] = jnp.zeros_like(alpha_grads)
    scale_grads[...] = jnp.zeros_like(scale_grads)

    def enter(part, place):
        result = step_forward(branch[part], tokens[part].astype(f32), alpha_attn[...])[0]
        hidden[part] = result
        held[q0, place] = result.astype(bf16)

    def forward(q):
        def half(part):
            block = held[q, part]
            up = dot(block, weight(0), 1, 1)
            gate = dot(block, weight(1), 1, 1)
            ups[q, part] = up
            gates[q, part] = gate
            gated = gate * gate_scale
            inner[q, part] = (up * up_scale * (gated * jax.nn.sigmoid(gated))).astype(bf16)

        each_half(half)
        done.append(q)
        if len(done) in (1, 3):
            line.wait(len(done) // 2 + 1)
            line.hand_on(len(done) // 2 + 1)

    def forward_end():
        for d in range(3, length):
            line.wait(d)
            line.hand_on(d)
        for d in range(length - 1):
            line.sent(d)

    out = PlaneScatter(
        lambda q, half: dot(inner[q, half_rows(half)], down_weight(), 1, 0),
        own, cross, side, cross_sem.at[0], side_sem.at[0],
    )

    def forward_corner():
        forward_end()
        out.begin()

    plane_gather(
        held, gather_send.at[0], gather_receive.at[0], lambda h: each_chunk(enter, h), forward, forward_corner
    )
    out.end()

    def turn_back(part, place):
        start, alpha = hidden[part], alpha_mlp[...]
        result, unit, target_scale, moved_scale = step_forward(own[q0, part], start, alpha)
        mixed[part] = result.astype(bf16)
        target_grad, start_grad, alpha_part = step_back(
            cotangent[part].astype(f32), result, unit, target_scale, moved_scale, start, alpha
        )
        alpha_grads[1:2] += jnp.sum(alpha_part, axis=0, keepdims=True)
        hidden_grad[part] = start_grad
        grads[q0, place] = target_grad.astype(bf16)

    def backward(q):
        def half(part):
            inner_grad = dot(grads[q, part], down_weight(), 1, 1)
            up, gate = ups[q, part], gates[q, part]
            gated = gate * gate_scale
            share = jax.nn.sigmoid(gated)
            silu = gated * share
            lifted = inner_grad * up
            gated_grad = lifted * up_scale * (share * (1.0 + gated * (1.0 - share)))
            up_low[q, part] = (inner_grad * up_scale * silu).astype(bf16)
            gate_low[q, part] = (gated_grad * gate_scale).astype(bf16)
            scale_grads[0:1] += jnp.sum(lifted * silu, axis=0, keepdims=True)
            scale_grads[1:2] += jnp.sum(gated_grad * gate, axis=0, keepdims=True)

        each_half(half)

    def weights_back():
        tall = 4 * 2 * rows
        for i, (left, right) in enumerate(((up_low, held), (gate_low, held), (inner, grads))):

            def step(n, carry):
                columns = pl.ds(pl.multiple_of(n * BLOCK, BLOCK), BLOCK)
                product = dot(
                    left[...].reshape(tall, full), right[:, :, columns].reshape(tall, BLOCK), 0, 0
                )
                weight_grads[:, i, :, columns] = product.astype(bf16).reshape(owners, units, BLOCK)
                return carry

            lax.fori_loop(0, width // BLOCK, step, 0)

    back = PlaneScatter(
        lambda q, half: dot(up_low[q, half_rows(half)], weight(0), 1, 0)
        + dot(gate_low[q, half_rows(half)], weight(1), 1, 0),
        own, cross, side, cross_sem.at[1], side_sem.at[1],
    )
    plane_gather(
        grads, gather_send.at[1], gather_receive.at[1], lambda h: each_chunk(turn_back, h), backward, back.begin
    )
    back.end(weights_back)

    def leave(part, place):
        start, alpha = tokens[part].astype(f32), alpha_attn[...]
        result, unit, target_scale, moved_scale = step_forward(branch[part], start, alpha)
        target_grad, start_grad, alpha_part = step_back(
            hidden_grad[part] + own[q0, part], result, unit, target_scale, moved_scale, start, alpha
        )
        alpha_grads[0:1] += jnp.sum(alpha_part, axis=0, keepdims=True)
        branch_low[part] = target_grad.astype(bf16)
        token_grad[part] = start_grad

    for h in (0, 1):
        each_chunk(leave, h)


def mlp(length, branch, tokens, alpha_attn, alpha_mlp, cotangent, up_gate, down):
    rows, width = branch.shape
    owners, units = length, down.shape[0]
    full = owners * units
    low, wide = like((rows, width), bf16), like((rows, width), f32)
    scratch = [
        pltpu.VMEM((rows, width), f32),
        pltpu.VMEM((rows, width), f32),
        pltpu.VMEM((4, 2 * rows, width), bf16),
        pltpu.VMEM((4, 2 * rows, width), bf16),
        pltpu.VMEM((4, 2 * rows, full), f32),
        pltpu.VMEM((4, 2 * rows, full), f32),
        pltpu.VMEM((4, 2 * rows, full), bf16),
        pltpu.VMEM((4, 2 * rows, full), bf16),
        pltpu.VMEM((4, 2 * rows, full), bf16),
        pltpu.VMEM((4, rows, width), f32),
        pltpu.VMEM((2, 4, rows, width), bf16),
        pltpu.VMEM((2, 3, rows, width), bf16),
        pltpu.SemaphoreType.DMA((2, 3, 8)),
        pltpu.SemaphoreType.DMA((2, 16)),
        pltpu.SemaphoreType.DMA((2, 2, 4)),
        pltpu.SemaphoreType.DMA((2, 2, 3, 2)),
        pltpu.VMEM((length, *down.shape), bf16),
    ] + line_gather_semaphores(length)
    return remote_call(
        functools.partial(mlp_kernel, length), "mlp", 5,
        (low, low, wide, like((2, width), f32), like((owners, 3, units, width), bf16), like((2, full), f32)),
        (IN_VMEM,) * 6, [IN_VMEM] * 7, scratch,
        branch, tokens, alpha_attn, alpha_mlp, cotangent, up_gate, down,
    )


def shards(
    tokens, lengths, w_query, w_key, w_value, s_qk, w_out, up_weight, gate_weight, down_weight,
    s_up, s_gate, alpha_attn, alpha_mlp, cotangent,
):
    outer = lax.axis_size("o")
    own_units = up_weight.shape[0]
    if outer > 1:
        up_weight, gate_weight, down_weight, s_up, s_gate = (
            gather(a, "o") for a in (up_weight, gate_weight, down_weight, s_up, s_gate)
        )
    units = up_weight.shape[0]
    scales = jnp.zeros((2, SCALE_ROWS, up_weight.shape[1]), bf16)
    scales = scales.at[:, 0, :units].set(jnp.stack([s_up, s_gate]))
    up_gate = jnp.concatenate([jnp.stack([up_weight, gate_weight]), scales], axis=1)

    length = lax.axis_size("z")
    projections = w_query.T, w_key.T, w_value.T
    group_tokens, turned_q, turned_k, cosine, sine, qt, kt, vt, up_gate, branch, ot, lse = attention(
        length, lengths, tokens, *projections, s_qk[None], w_out, up_gate
    )
    mixed, branch_low, token_grad, alpha_grads, mlp_grads, scale_grads = mlp(
        length, branch, tokens, alpha_attn[None], alpha_mlp[None], cotangent, up_gate, down_weight,
    )
    tokens_grad, attn_grads, alpha_sums, scale_sums, gain_grad, mlp_grads = back(
        length, lengths, branch_low, w_out, qt, kt, vt, ot, lse, mlp_grads, turned_q, turned_k, s_qk[None],
        cosine, sine, *projections, alpha_grads, scale_grads, token_grad, group_tokens,
    )
    if outer > 1:
        mlp_grads = lax.psum_scatter(mlp_grads, "o", scatter_dimension=1, tiled=True)
        attn_grads, alpha_sums, scale_sums, gain_grad = lax.psum(
            (attn_grads, alpha_sums, scale_sums, gain_grad), "o"
        )
    place = lax.axis_index("z") * units + lax.axis_index("o") * own_units
    scale_sums = lax.dynamic_slice_in_dim(scale_sums, place, own_units, 1)
    return (
        mixed,
        tokens_grad,
        attn_grads[:HEAD_DIM].T,
        attn_grads[HEAD_DIM : 2 * HEAD_DIM].T,
        attn_grads[2 * HEAD_DIM : 3 * HEAD_DIM].T,
        gain_grad[0],
        attn_grads[3 * HEAD_DIM :],
        mlp_grads[0],
        mlp_grads[1],
        mlp_grads[2],
        scale_sums[0],
        scale_sums[1],
        alpha_sums[0],
        alpha_sums[1],
    )


def solution(mesh):
    dp, head = mesh.shape["dp"], mesh.shape["head"]
    fine = Mesh(mesh.devices.reshape(dp // 2, 2, head // 4, 2, 2), AXES)
    group, rows, heads = P(("o", "x"), None), P(AXES, None), P(None, GROUP)
    in_specs = (
        rows, group, heads, heads, heads, P(GROUP), P(GROUP, None), rows, rows, rows,
        P(AXES), P(AXES), P(), P(), rows,
    )
    out_specs = (
        rows, rows, heads, heads, heads, P(GROUP), P(GROUP, None), rows, rows, rows,
        P(AXES), P(AXES), P(), P(),
    )
    return jax.shard_map(
        shards, mesh=fine, in_specs=in_specs, out_specs=out_specs, check_vma=False
    )
```

```python
import functools
import math

import jax
import jax.numpy as jnp
from jax import lax
from jax.experimental import pallas as pl
from jax.experimental.pallas import tpu as pltpu
from jax.sharding import Mesh
from jax.sharding import PartitionSpec as P

HEAD_DIM = 64
BLOCK = 512
REACH = 4
EPSILON = 1e-06
ROOT = math.sqrt(HEAD_DIM)
SCORE_SCALE = math.log2(math.e) / ROOT
AXES = ("o", "x", "z", "y", "c")
GROUP = ("z", "y", "c")
f32, bf16 = jnp.float32, jnp.bfloat16
VMEM_LIMIT = 60 * 2**20


def dot(left, right, left_dim, right_dim):
    return lax.dot_general(
        left, right, (((left_dim,), (right_dim,)), ((), ())), preferred_element_type=f32
    )


def unit_start(lengths, unit):
    start, end = jnp.int32(0), jnp.int32(0)
    for j in range(lengths.shape[1]):
        end = end + lengths[0, j]
        start = jnp.where(unit >= end, end, start)
    return start


def causal(weights):
    key = lax.broadcasted_iota(jnp.int32, weights.shape, 0)
    query = lax.broadcasted_iota(jnp.int32, weights.shape, 1)
    return jnp.where(key <= query, weights, 0.0)


def block_columns(index):
    return pl.ds(pl.multiple_of(index * BLOCK, BLOCK), BLOCK)


def barred(lengths, unit, back):
    return jnp.where(unit - back >= unit_start(lengths, unit), 0.0, 1e30).astype(f32)


def attend(lengths, unit, qt, kt, vt, ot, lse, total, attended):
    columns = block_columns(unit)

    def part(back):
        keys = block_columns(unit - back)
        scores = dot(kt[:, keys], qt[:, columns], 0, 0) * SCORE_SCALE
        if back == 0:
            weights = causal(jnp.exp2(scores))
        else:
            weights = jnp.exp2(scores - barred(lengths, unit, back))
        sums = jnp.sum(weights, axis=0, keepdims=True)
        values = dot(vt[:, keys], weights.astype(bf16), 1, 0)
        if back == 0:
            total[...] = sums
            attended[...] = values
        else:
            total[...] += sums
            attended[...] += values

    part(0)
    for back in range(1, REACH):
        pl.when(unit >= back)(functools.partial(part, back))
    ot[:, columns] = (attended[...] * (1.0 / total[...])).astype(bf16)
    lse[:, columns] = jnp.log2(total[...])


def attend_back(lengths, unit, qt, kt, vt, ot, got, lse, gqt, gkt, gvt):
    columns = block_columns(unit)
    query, grad = qt[:, columns], got[...]
    inner = jnp.sum(grad.astype(f32) * ot[:, columns].astype(f32), axis=0, keepdims=True)

    def part(back):
        keys = block_columns(unit - back)
        key, value = kt[:, keys], vt[:, keys]
        log_total = lse[:, columns]
        if back > 0:
            log_total = log_total + barred(lengths, unit, back)
        weights = jnp.exp2(dot(key, query, 0, 0) * SCORE_SCALE - log_total)
        if back == 0:
            weights = causal(weights)
        score_grad = (weights * (dot(value, grad, 0, 0) - inner)).astype(bf16)
        gkt[:, keys] += dot(query, score_grad, 1, 1)
        gvt[:, keys] += dot(grad, weights.astype(bf16), 1, 1)
        gqt[:, columns] += dot(key, score_grad, 1, 0)

    part(0)
    for back in range(1, REACH):
        pl.when(unit >= back)(functools.partial(part, back))


def turn_table(lengths, unit):
    shape = (HEAD_DIM // 2, BLOCK)
    first = (unit - unit_start(lengths, unit)) * BLOCK
    place = (first + lax.broadcasted_iota(jnp.int32, shape, 1)).astype(f32)
    turns = lax.broadcasted_iota(jnp.int32, shape, 0).astype(f32)
    angle = place * jnp.exp(turns * (-2.0 * math.log(10000.0) / HEAD_DIM))
    return jnp.cos(angle), jnp.sin(angle)


def as_column(row):
    n = row.shape[1]
    same = lax.broadcasted_iota(jnp.int32, (n, n), 0) == lax.broadcasted_iota(jnp.int32, (n, n), 1)
    return jnp.sum(jnp.where(same, row, 0.0), axis=1, keepdims=True)


def as_row(column):
    n = column.shape[0]
    same = lax.broadcasted_iota(jnp.int32, (n, n), 0) == lax.broadcasted_iota(jnp.int32, (n, n), 1)
    return jnp.sum(jnp.where(same, column, 0.0), axis=0, keepdims=True)


def join(joint, *parts):
    for i, part in enumerate(parts):
        joint[i * HEAD_DIM : (i + 1) * HEAD_DIM] = part[...]


def turn(values, cosine, sine):
    half = HEAD_DIM // 2
    a, b = values[:half], values[half:]
    return jnp.concatenate([a * cosine - b * sine, b * cosine + a * sine], axis=0)


def unit_features(turned):
    scale = lax.rsqrt(jnp.mean(turned * turned, axis=0, keepdims=True) + EPSILON)
    return turned * scale, scale


def gather(values, axes):
    return lax.all_gather(values, axes, axis=0, tiled=True)


MESH_ID = pl.DeviceIdType.MESH


def here(*names):
    return tuple(lax.axis_index(name) for name in names)


def greet(neighbours):
    barrier = pltpu.get_barrier_semaphore()
    count = jnp.int32(0)
    for condition, device in neighbours:

        @pl.when(condition)
        def _():
            pl.semaphore_signal(barrier, inc=1, device_id=device, device_id_type=MESH_ID)

        count = count + jnp.where(condition, 1, 0)
    pl.semaphore_wait(barrier, count)


def remote(source, target, send, receive, device):
    return pltpu.make_async_remote_copy(
        src_ref=source,
        dst_ref=target,
        send_sem=send,
        recv_sem=receive,
        device_id=device,
        device_id_type=MESH_ID,
    )


def line_order(z, length, step):
    picked = jnp.int32(0)
    for at in range(length):
        order = sorted(range(length), key=lambda p: (abs(p - at), p))
        picked = jnp.where(z == at, order[step], picked)
    return picked


def group_neighbours(length):
    z, y, c = here("z", "y", "c")
    return [
        (z > 0, {"z": z - 1}),
        (z < length - 1, {"z": z + 1}),
        (z >= 0, {"y": 1 - y}),
        (z >= 0, {"c": 1 - c}),
    ]


def group_gather(length, own, held, send, receive, on_unit, at_step=None):
    z, y, c = here("z", "y", "c")
    rows = held.shape[1] // 2
    half = rows // 2

    def copy(kind, zz, yy, cc, h, device):
        at = held.at[zz * 2 + yy, pl.ds(pl.multiple_of(cc * rows + h * half, half), half)]
        number = ((zz * 2 + yy) * 2 + cc) * 2 + h
        return remote(at, at, send.at[kind, number], receive.at[number], device)

    def arrived(zz, yy, cc, h):
        copy(3, zz, yy, cc, h, {"c": 1 - c}).wait_recv()

    def come(distance):
        if distance == 0:
            return [(z, z >= 0, [(0, z < length - 1, {"z": z + 1}), (1, z > 0, {"z": z - 1})])]
        return [
            (z - distance, z >= distance, [(0, z < length - 1, {"z": z + 1})]),
            (z + distance, z + distance < length, [(1, z > 0, {"z": z - 1})]),
        ]

    def passed_on(zz, h, along, act):
        for kind, goes, device in along:

            @pl.when(goes)
            def _():
                act(copy(kind, zz, y, c, h, device))

        act(copy(2, zz, y, c, h, {"y": 1 - y}))
        act(copy(3, zz, y, c, h, {"c": 1 - c}))

    held[z * 2 + y, pl.ds(pl.multiple_of(c * rows, rows), rows)] = own[...]
    order = [line_order(z, length, step) for step in range(length)]
    for tick in range(2 * length + 1):
        step, h = divmod(tick, 2)
        before, last_h = divmod(tick - 1, 2)
        if step < length:
            for zz, there, along in come(step):

                @pl.when(there)
                def _():
                    if step > 0:
                        arrived(zz, y, c, h)
                    passed_on(zz, h, along, lambda copy_: copy_.start())

        if before >= 0:
            arrived(order[before], 1 - y, c, last_h)
            copy(3, order[before], 1 - y, c, last_h, {"c": 1 - c}).start()
        if at_step is not None and h == 0:
            at_step(step)
        if h == 1:
            for i in (0, 1):
                arrived(order[step], y, 1 - c, i)
            on_unit(order[step] * 2 + y)
        if last_h == 1 and before >= 0:
            for i in (0, 1):
                arrived(order[before], 1 - y, 1 - c, i)
            on_unit(order[before] * 2 + 1 - y)
    for h in (0, 1):
        for step in range(length):
            for zz, there, along in come(step):

                @pl.when(there)
                def _():
                    passed_on(zz, h, along, lambda copy_: copy_.wait_send())

            copy(3, order[step], 1 - y, c, h, {"c": 1 - c}).wait_send()


GATHER_SEMAPHORES = 4


def gather_scratch(units, rows, width):
    return [
        pltpu.VMEM((units, 2 * rows, width), bf16),
        pltpu.SemaphoreType.DMA((GATHER_SEMAPHORES, 4 * units)),
        pltpu.SemaphoreType.DMA((4 * units,)),
    ]


def scatter_scratch(length, rows, width):
    return [
        pltpu.VMEM((length + 1, rows, width), f32),
        pltpu.VMEM((2 * length + 4, rows, width), bf16),
        pltpu.VMEM((2, length, rows, width), bf16),
        pltpu.VMEM((3, length, rows, width), bf16),
        pltpu.SemaphoreType.DMA((2, 2 * length)),
        pltpu.SemaphoreType.DMA((2, length, 2)),
        pltpu.SemaphoreType.DMA((3, length, 2)),
    ]


def group_scatter(length, produce, finish, own, cross, across, along, cross_sem, across_sem, along_sem, prepare=None, between=None, at_step=None):
    z, y, c = here("z", "y", "c")

    def to_core(unit, slot=0):
        source = cross.at[2 * length + slot]
        return remote(source, cross.at[unit], cross_sem.at[0, unit], cross_sem.at[1, unit], {"c": 1 - c})

    half = own.shape[1] // 2

    def part(h):
        return pl.ds(h * half, half)

    def to_y(zz, h):
        return remote(
            across.at[0, zz, part(h)], across.at[1, zz, part(h)], across_sem.at[0, zz, h],
            across_sem.at[1, zz, h], {"y": 1 - y},
        )

    def to_z(zz, slot, h, device):
        return remote(
            along.at[0, zz, part(h)], along.at[slot, zz, part(h)], along_sem.at[0, zz, h],
            along_sem.at[slot, zz, h], device,
        )

    def from_z(zz, slot, h):
        to_z(zz, slot, h, {"c": 1 - c}).wait_recv()
        return along[slot, zz, part(h)].astype(f32)

    order = [line_order(z, length, length - 1 - step) for step in range(length)]

    def give(unit, slot):
        cross[2 * length + slot] = produce(unit, 1 - c).astype(bf16)
        to_core(unit, slot).start()

    def first(step):
        zz = order[step]
        slot = 2 * (step % 2)
        if step >= 2:
            for yy in (0, 1):
                to_core(order[step - 2] * 2 + yy).wait_send()
        there, here_ = zz * 2 + 1 - y, zz * 2 + y
        if prepare is not None:
            prepare(there)
        give(there, slot)
        own[length] = produce(there, c)
        if prepare is not None:
            prepare(here_)
        to_core(there).wait_recv()
        across[0, zz] = (own[length] + cross[there].astype(f32)).astype(bf16)
        for h in (0, 1):
            to_y(zz, h).start()
        give(here_, slot + 1)
        own[zz] = produce(here_, c)

    def third(zz, h, last):
        unit = zz * 2 + y
        if h == 0:
            to_core(unit).wait_recv()
        own[zz, part(h)] += cross[unit, part(h)].astype(f32)
        to_y(zz, h).wait_recv()
        own[zz, part(h)] += across[1, zz, part(h)].astype(f32)

        @pl.when((zz >= z) & (z > 0))
        def _():
            own[zz, part(h)] += from_z(zz, 1, h)

        @pl.when((zz <= z) & (z < length - 1))
        def _():
            own[zz, part(h)] += from_z(zz, 2, h)

        if last:
            finish(h, own[zz, part(h)])
            return
        along[0, zz, part(h)] = own[zz, part(h)].astype(bf16)

        @pl.when(zz > z)
        def _():
            to_z(zz, 1, h, {"z": z + 1}).start()

        @pl.when(zz < z)
        def _():
            to_z(zz, 2, h, {"z": z - 1}).start()

    for step in range(length + 1):
        if step < length:
            first(step)
        if at_step is not None:
            at_step(step)
        if step == length - 1 and between is not None:
            between()
        if step >= 1:
            for h in (0, 1):
                third(order[step - 1], h, step == length)
    for step in range(length):
        zz = order[step]
        if step >= length - 2:
            for yy in (0, 1):
                to_core(zz * 2 + yy).wait_send()
        for h in (0, 1):
            to_y(zz, h).wait_send()
            if step < length - 1:
                to_z(zz, 1, h, {"c": 1 - c}).wait_send()


def remote_call(kernel, name, number, outs, out_specs, in_specs, scratch, *operands):
    return pl.pallas_call(
        kernel,
        name=name,
        out_shape=outs,
        in_specs=in_specs,
        out_specs=out_specs,
        scratch_shapes=scratch,
        compiler_params=pltpu.CompilerParams(
            collective_id=number, has_side_effects=True, vmem_limit_bytes=VMEM_LIMIT
        ),
    )(*operands)


IN_VMEM = pl.BlockSpec(memory_space=pltpu.VMEM)
IN_SMEM = pl.BlockSpec(memory_space=pltpu.SMEM)
ANYWHERE = pl.BlockSpec(memory_space=pl.ANY)


def like(shape, dtype):
    return jax.ShapeDtypeStruct(shape, dtype)


class LineGather:
    def __init__(self, length, own, held, send, receive, local_sem):
        self.length, self.own, self.held = length, own, held
        self.sems, self.local_sem = (send, receive), local_sem
        self.z = lax.axis_index("z")

    def copy(self, way, zz, source=None):
        send, receive = self.sems
        at = self.held.at[zz]
        device = {"z": self.z + 1} if way == 0 else {"z": self.z - 1}
        return remote(at if source is None else source, at, send.at[way, zz], receive.at[zz], device)

    def ways(self, d, act):
        z, length = self.z, self.length
        for way, zz, there, more in (
            (0, z - d, z - d >= 0, z < length - 1),
            (1, z + d, z + d < length, z > 0),
        ):
            act(way, zz, there, there & more)

    def start(self):
        pltpu.make_async_copy(self.own, self.held.at[self.z], self.local_sem).start()
        self.hand_on(0)

    def hand_on(self, d):
        def begin(way, zz, there, more):
            @pl.when(more)
            def _():
                self.copy(way, zz, self.own if d == 0 else None).start()

        self.ways(d, begin)

    def wait(self, d):
        def arrive(way, zz, there, more):
            @pl.when(there)
            def _():
                self.arrival(way, zz).wait_recv()

        self.ways(d, arrive)

    def sent(self, d):
        def leave(way, zz, there, more):
            @pl.when(more)
            def _():
                self.copy(way, zz, self.own if d == 0 else None).wait_send()

        self.ways(d, leave)
        if d == 0:
            pltpu.make_async_copy(self.own, self.held.at[self.z], self.local_sem).wait()

    def arrival(self, way, zz):
        send, receive = self.sems
        at = self.held.at[zz]
        return remote(at, at, send.at[way, zz], receive.at[zz], {"c": 1 - lax.axis_index("c")})


def line_gather_semaphores(length):
    return [
        pltpu.SemaphoreType.DMA((2, length)),
        pltpu.SemaphoreType.DMA((length,)),
        pltpu.SemaphoreType.DMA,
    ]


class LineScatter:
    def __init__(self, length, parts, rest, out, into, send_sem, receive_sem):
        self.length, self.parts, self.rest = length, parts, rest
        self.out, self.into, self.sems = out, into, (send_sem, receive_sem)
        self.z = lax.axis_index("z")

    def copy(self, way, d, source):
        send, receive = self.sems
        device = {"z": self.z + 1} if way == 0 else {"z": self.z - 1}
        return remote(source, self.into.at[way, d - 2], send.at[way, d - 2], receive.at[way, d - 2], device)

    def arrived(self, way, d):
        send, receive = self.sems
        at = self.into.at[way, d - 2]
        device = {"c": 1 - lax.axis_index("c")}
        remote(at, at, send.at[way, d - 2], receive.at[way, d - 2], device).wait_recv()

    def cases(self, d, alone, joined):
        z, length = self.z, self.length
        for way, dest, valid, behind in (
            (0, z + d, z + d < length, z > 0),
            (1, z - d, z - d >= 0, z < length - 1),
        ):
            behind = behind if d < length - 1 else z < 0
            pl.when(valid & jnp.logical_not(behind))(functools.partial(alone, way, dest))
            pl.when(valid & behind)(functools.partial(joined, way, dest))

    def joint(self, way, dest, d):
        self.arrived(way, d + 1)
        return (self.parts[dest].astype(f32) + self.into[way, d - 1].astype(f32)).astype(bf16)

    def send(self, d):
        def alone(way, dest):
            self.copy(way, d, self.parts.at[dest]).start()

        def joined(way, dest):
            self.out[way, d - 2] = self.joint(way, dest, d)
            self.copy(way, d, self.out.at[way, d - 2]).start()

        self.cases(d, alone, joined)

    def finish(self):
        def alone(way, dest):
            self.rest[way] = self.parts[dest]

        def joined(way, dest):
            self.rest[way] = self.joint(way, dest, 1)

        self.cases(1, alone, joined)
        for d in range(2, self.length):

            def left(way, dest):
                self.copy(way, d, self.parts.at[dest]).wait_send()

            self.cases(d, left, left)


def line_scatter_scratch(parts):
    length = parts.shape[0]
    hops = (2, length - 2, *parts.shape[1:])
    joint = (2, max(length - 3, 1), *parts.shape[1:])
    return [pltpu.VMEM(joint, bf16), pltpu.VMEM(hops, bf16)] + [pltpu.SemaphoreType.DMA(hops[:2])] * 2


def half_columns(unit, half):
    rows = BLOCK // 2
    return pl.ds(pl.multiple_of(unit * BLOCK + half * rows, rows), rows)


def attention_kernel(
    length, lengths, tokens, w_query, w_key, w_value, gain_row, w_out, weight,
    gathered, turned_q, turned_k, cosine, sine, qt, kt, vt, weights, branch, ot, lse,
    joint, held, send, receive, out_sem, line_send, line_receive, line_local, total, attended, *scratch,
):
    greet(group_neighbours(length))
    line = LineGather(length, weight, weights, line_send, line_receive, line_local)
    join(joint, w_query, w_key, w_value)
    gain = as_column(gain_row[...])

    def start_line(step):
        if step == length - 1:
            line.start()

    def on_unit(unit):
        pltpu.make_async_copy(held.at[unit], gathered.at[unit], out_sem.at[unit]).start()
        columns = block_columns(unit)
        projected = dot(joint[...], held[unit], 1, 1)
        cosine[:, columns], sine[:, columns] = turn_table(lengths, unit)
        for part, turned, features in ((0, turned_q, qt), (1, turned_k, kt)):
            values = turn(
                projected[part * HEAD_DIM : (part + 1) * HEAD_DIM], cosine[:, columns], sine[:, columns]
            )
            turned[:, columns] = values
            features[:, columns] = (unit_features(values)[0] * gain).astype(bf16)
        vt[:, columns] = projected[2 * HEAD_DIM :].astype(bf16)

    group_gather(length, tokens, held, send, receive, on_unit, start_line)
    line.wait(1)
    line.hand_on(1)

    def move_line(step):
        if 2 <= step < length - 1:
            line.wait(step)
            line.hand_on(step)

    def finish(h, total):
        branch[pl.ds(h * total.shape[0], total.shape[0])] = total

    group_scatter(
        length, lambda unit, half: dot(ot[:, half_columns(unit, half)], w_out[...], 0, 0), finish, *scratch,
        prepare=lambda unit: attend(lengths, unit, qt, kt, vt, ot, lse, total, attended), at_step=move_line,
    )
    line.wait(length - 1)
    for d in range(length - 1):
        line.sent(d)
    for unit in range(2 * length):
        pltpu.make_async_copy(held.at[unit], gathered.at[unit], out_sem.at[unit]).wait()


def attention(length, lengths, tokens, w_query, w_key, w_value, gain, w_out, weight):
    rows, width = tokens.shape
    units = 2 * length
    total = units * 2 * rows
    wide, narrow = like((HEAD_DIM, total), f32), like((HEAD_DIM, total), bf16)
    table = like((HEAD_DIM // 2, total), f32)
    return remote_call(
        functools.partial(attention_kernel, length), "attention", 1,
        (
            like((units, 2 * rows, width), bf16), wide, wide, table, table, narrow, narrow, narrow,
            like((length, *weight.shape), bf16), like((rows, width), f32), narrow, like((1, total), f32),
        ),
        (ANYWHERE,) + (IN_VMEM,) * 7 + (ANYWHERE,) + (IN_VMEM,) * 3, [IN_SMEM] + [IN_VMEM] * 6 + [ANYWHERE],
        [pltpu.VMEM((3 * HEAD_DIM, width), bf16)] + gather_scratch(units, rows, width) + [pltpu.SemaphoreType.DMA((units,))]
        + line_gather_semaphores(length) + [pltpu.VMEM((1, BLOCK), f32), pltpu.VMEM((HEAD_DIM, BLOCK), f32)]
        + scatter_scratch(length, rows, width),
        lengths, tokens, w_query, w_key, w_value, gain, w_out, weight,
    )


def flip(position, bit):
    return position + bit - 2 * bit * ((position // bit) % 2)


def back_kernel(
    length, lengths, grad, w_out, qt, kt, vt, ot, lse, far_parts, far_q, far_k, gain_row, far_cosine, far_sine,
    w_query, w_key, w_value, alpha_grads, scale_grads, far_direct, gathered,
    token_grad, weight_grads, alpha_sums, scale_sums, gain_grad, sums,
    parts, turned_q, turned_k, cosine, sine, load_sem,
    joint, out_grad, gqt, gkt, gvt, got, rest, arrivals, rest_sem, grads, held_sem, gains, gain_sem, sent, taken,
    weight_sem, small_out, small_in, small_sem, line_out, line_into, line_send, line_receive,
    held, send, receive, *scratch,
):
    x, z, y, c = here("x", "z", "y", "c")
    to_x = {"x": 1 - x}
    bits = [1 << i for i in range(length.bit_length() - 1)]
    loads = [
        pltpu.make_async_copy(source, target, load_sem.at[i])
        for i, (source, target) in enumerate(
            (
                (far_parts, parts), (far_q, turned_q), (far_k, turned_k), (far_cosine, cosine),
                (far_sine, sine), (far_direct, scratch[0].at[length]),
            )
        )
    ]
    for copy in loads[:5]:
        copy.start()
    greet(group_neighbours(length) + [(x >= 0, to_x)] + [(x >= 0, {"z": flip(z, bit)}) for bit in bits])
    partners = [{"c": 1 - c}, {"y": 1 - y}, to_x] + [{"z": flip(z, bit)} for bit in bits]
    line = LineScatter(length, parts, rest, line_out, line_into, line_send, line_receive)
    join(joint, w_query, w_key, w_value)
    gain = as_column(gain_row[...])

    def spread_step(step):
        if step == 0:
            for array in (out_grad, gqt, gkt, gvt):
                array[...] = jnp.zeros_like(array)
            loads[0].wait()
        if step % 2 == 0 and step < 2 * (length - 2):
            line.send(length - 1 - step // 2)

    def on_unit(unit):
        columns = block_columns(unit)
        got[...] = dot(w_out[...], held[unit], 1, 1).astype(bf16)
        out_grad[...] += dot(ot[:, columns], held[unit], 1, 0)
        attend_back(lengths, unit, qt, kt, vt, ot, got, lse, gqt, gkt, gvt)

    group_gather(length, grad, held, send, receive, on_unit, spread_step)
    load = pltpu.make_async_copy(gathered, held, held_sem)
    load.start()
    for copy in loads[1:5]:
        copy.wait()
    line.finish()
    lines = [
        (remote(rest.at[way], arrivals.at[way], rest_sem.at[0, way], rest_sem.at[1, way], {"z": to}), goes, comes)
        for way, to, goes, comes in (
            (0, z + 1, z < length - 1, z > 0), (1, z - 1, z > 0, z < length - 1)
        )
    ]
    for last_hop, goes, _ in lines:
        pl.when(goes)(last_hop.start)
    gains[0] = jnp.zeros_like(gains[0])
    small_out[0] = jnp.zeros_like(small_out[0])
    small_out[0, 0:2] = alpha_grads[...]
    small_out[0, 2:4, : scale_grads.shape[1]] = scale_grads[...]

    def exchange(i):
        return remote(small_out.at[i], small_in.at[i], small_sem.at[0, i], small_sem.at[1, i], partners[i])

    def at_step(step):
        if 0 < step <= len(partners):
            exchange(step - 1).wait_recv()
            small_out[step] = small_out[step - 1]
            summed = 2 if step <= 3 else 4
            small_out[step, :summed] += small_in[step - 1, :summed]
        if step < len(partners):
            exchange(step).start()
        if step == length - 1:
            loads[5].start()

    def prepare(unit):
        columns = block_columns(unit)
        for part, turned, outer in ((0, turned_q, gqt), (1, turned_k, gkt)):
            normal, scale = unit_features(turned[:, columns])
            grad = outer[:, columns] * (1.0 / ROOT)
            product = grad * normal
            width = gains.shape[2]
            for i in range(BLOCK // width):
                gains[0] += product[:, i * width : (i + 1) * width]
            grad = grad * gain
            grad = scale * (grad - normal * jnp.mean(grad * normal, axis=0, keepdims=True))
            grad = turn(grad, cosine[:, columns], -sine[:, columns])
            grads[part * HEAD_DIM : (part + 1) * HEAD_DIM, columns] = grad.astype(bf16)
        grads[2 * HEAD_DIM :, columns] = gvt[:, columns].astype(bf16)

    gain_copy = remote(gains.at[0], gains.at[1], gain_sem.at[0], gain_sem.at[1], to_x)
    weight_copy = remote(sent, taken, weight_sem.at[0], weight_sem.at[1], to_x)

    def between():
        gain_copy.start()
        load.wait()
        rows = grads.shape[1]
        product = dot(grads[...], held[...].reshape(rows, held.shape[2]), 1, 0)
        sent[: 3 * HEAD_DIM] = product.astype(bf16)
        sent[3 * HEAD_DIM :] = out_grad[...].astype(bf16)
        weight_copy.start()

    def finish(h, total):
        part = pl.ds(h * total.shape[0], total.shape[0])
        if h == 0:
            loads[5].wait()
        token_grad[part] = (scratch[0][length, part] + total).astype(bf16)

    group_scatter(
        length, lambda unit, half: dot(grads[:, half_columns(unit, half)], joint[...], 0, 0), finish, *scratch,
        prepare=prepare, between=between, at_step=at_step,
    )
    for step in range(length + 1, len(partners) + 1):
        at_step(step)
    alpha_sums[...] = small_out[len(partners), 0:2]
    scale_sums[...] = small_out[len(partners), 2:4, : scale_sums.shape[1]]
    sums[...] = parts[z].astype(f32)
    for way, (last_hop, goes, comes) in enumerate(lines):

        @pl.when(comes)
        def _():
            remote(
                arrivals.at[way], arrivals.at[way], rest_sem.at[0, way], rest_sem.at[1, way], {"c": 1 - c}
            ).wait_recv()
            sums[...] += arrivals[way].astype(f32)

        pl.when(goes)(last_hop.wait_send)
    gain_copy.wait()
    gain_grad[...] = as_row(jnp.sum(gains[0] + gains[1], axis=1, keepdims=True))
    weight_copy.wait()
    weight_grads[...] = sent[...].astype(f32) + taken[...].astype(f32)
    for i in range(len(partners)):
        exchange(i).wait_send()


def back(length, lengths, grad, w_out, qt, kt, vt, ot, lse, parts, *operands):
    rows, width = grad.shape
    units = 2 * length
    total = qt.shape[1]
    alpha_grads, scale_grads, direct, gathered = operands[-4:]
    exchanges = 3 + length.bit_length() - 1
    small = (exchanges + 1, 4, width)
    weights = (4 * HEAD_DIM, width)
    wide = pltpu.VMEM((HEAD_DIM, total), f32)
    hops = pltpu.VMEM((2, *parts.shape[1:]), bf16)
    table = pltpu.VMEM((HEAD_DIM // 2, total), f32)
    scratch = [
        pltpu.VMEM(parts.shape, bf16), wide, wide, table, table,
        pltpu.SemaphoreType.DMA((6,)),
        pltpu.VMEM((3 * HEAD_DIM, width), bf16), pltpu.VMEM(w_out.shape, f32), wide, wide, wide, pltpu.VMEM((HEAD_DIM, BLOCK), bf16), hops, hops,
        pltpu.SemaphoreType.DMA((2, 2)),
        pltpu.VMEM((3 * HEAD_DIM, total), bf16),
        pltpu.SemaphoreType.DMA,
        pltpu.VMEM((2, HEAD_DIM, 128), f32),
        pltpu.SemaphoreType.DMA((2,)),
        pltpu.VMEM(weights, bf16),
        pltpu.VMEM(weights, bf16),
        pltpu.SemaphoreType.DMA((2,)),
        pltpu.VMEM(small, f32),
        pltpu.VMEM(small, f32),
        pltpu.SemaphoreType.DMA((2, exchanges)),
    ]
    return remote_call(
        functools.partial(back_kernel, length), "back", 4,
        (
            like((rows, width), bf16), like(weights, f32), like(alpha_grads.shape, f32),
            like(scale_grads.shape, f32), like((1, HEAD_DIM), f32), like(parts.shape[1:], f32),
        ),
        (IN_VMEM,) * 6, [IN_SMEM] + [IN_VMEM] * 7 + [ANYWHERE] * 3 + [IN_VMEM] + [ANYWHERE] * 2 + [IN_VMEM] * 5 + [ANYWHERE] * 2,
        scratch + line_scatter_scratch(parts) + gather_scratch(units, rows, width)
        + scatter_scratch(length, rows, width),
        lengths, grad, w_out, qt, kt, vt, ot, lse, parts, *operands,
    )


def plane_neighbours():
    x, y, c = here("x", "y", "c")
    return [(x >= 0, {"x": 1 - x}), (x >= 0, {"y": 1 - y}), (x >= 0, {"c": 1 - c})]


def plane_gather(held, send, receive, make_half, on_pair, before_corner):
    x, y, c = here("x", "y", "c")
    rows = held.shape[1] // 2
    half = rows // 2
    q0, qx, qy, qd = x * 2 + y, (1 - x) * 2 + y, x * 2 + 1 - y, (1 - x) * 2 + 1 - y
    to_x, to_y, to_c = (0, {"x": 1 - x}), (1, {"y": 1 - y}), (2, {"c": 1 - c})

    def copy(way, q, cc, h):
        at = held.at[q, pl.ds(pl.multiple_of(cc * rows + h * half, half), half)]
        return remote(at, at, send.at[way[0], q * 2 + h], receive.at[(q * 2 + cc) * 2 + h], way[1])

    def arrived(q, cc, h):
        copy(to_c, q, cc, h).wait_recv()

    sent = []

    def start(way, q, h):
        sent.append((way, q, h))
        copy(way, q, c, h).start()

    for h in (0, 1):
        make_half(h)
        for way in (to_x, to_y, to_c):
            start(way, q0, h)
    for h in (0, 1):
        arrived(q0, 1 - c, h)
    on_pair(q0)
    arrived(qx, c, 0)
    start(to_y, qx, 0)
    start(to_c, qx, 0)
    arrived(qy, c, 0)
    start(to_c, qy, 0)
    arrived(qy, c, 1)
    start(to_x, qy, 1)
    start(to_c, qy, 1)
    arrived(qx, c, 1)
    start(to_c, qx, 1)
    for q in (qx, qy):
        for h in (0, 1):
            arrived(q, 1 - c, h)
        on_pair(q)
    before_corner()
    for h in (0, 1):
        arrived(qd, c, h)
        start(to_c, qd, h)
    for h in (0, 1):
        arrived(qd, 1 - c, h)
    on_pair(qd)
    for way, q, h in sent:
        copy(way, q, c, h).wait_send()


class PlaneScatter:
    def __init__(self, produce, own, cross, side, cross_sem, side_sem):
        self.produce, self.own, self.cross, self.side = produce, own, cross, side
        self.cross_sem, self.side_sem = cross_sem, side_sem
        x, y, self.c = here("x", "y", "c")
        self.half = own.shape[1] // 2
        self.chips = x * 2 + y, (1 - x) * 2 + y, x * 2 + 1 - y, (1 - x) * 2 + 1 - y
        self.to_x, self.to_y = {"x": 1 - x}, {"y": 1 - y}

    def to_core(self, q):
        cross, sem = self.cross, self.cross_sem
        return remote(cross.at[0, q], cross.at[1, q], sem.at[0, q], sem.at[1, q], {"c": 1 - self.c})

    def part(self, h):
        return pl.ds(h * self.half, self.half)

    def beside(self, kind, h, device):
        side, sem, part = self.side, self.side_sem, self.part(h)
        return remote(
            side.at[0, kind, part], side.at[1, kind, part], sem.at[0, kind, h], sem.at[1, kind, h], device
        )

    def first(self, q):
        self.cross[0, q] = self.produce(q, 1 - self.c).astype(bf16)
        self.to_core(q).start()
        self.own[q] = self.produce(q, self.c)

    def joined(self, q):
        self.to_core(q).wait_recv()
        self.own[q] += self.cross[1, q].astype(f32)

    def send(self, kind, q, h, device):
        self.side[0, kind, self.part(h)] = self.own[q, self.part(h)].astype(bf16)
        self.beside(kind, h, device).start()

    def add(self, q, kind, h, device):
        self.beside(kind, h, device).wait_recv()
        self.own[q, self.part(h)] += self.side[1, kind, self.part(h)].astype(f32)

    def begin(self):
        q0, qx, qy, qd = self.chips
        self.first(qx)
        self.first(qy)
        self.joined(qx)
        self.send(1, qx, 0, self.to_x)
        self.joined(qy)
        self.send(2, qy, 1, self.to_y)

    def end(self, between=None):
        q0, qx, qy, qd = self.chips
        to_x, to_y = self.to_x, self.to_y
        self.first(qd)
        self.joined(qd)
        self.send(0, qd, 0, to_x)
        self.send(0, qd, 1, to_y)
        self.first(q0)
        self.add(qx, 0, 1, to_y)
        self.send(1, qx, 1, to_x)
        self.add(qy, 0, 0, to_x)
        self.send(2, qy, 0, to_y)
        self.joined(q0)
        if between is not None:
            between()
        self.add(q0, 1, 0, to_x)
        self.add(q0, 2, 1, to_y)
        self.add(q0, 2, 0, to_y)
        self.add(q0, 1, 1, to_x)
        for q in self.chips:
            self.to_core(q).wait_send()
        self.beside(0, 0, to_x).wait_send()
        self.beside(0, 1, to_y).wait_send()
        for h in (0, 1):
            self.beside(1, h, to_x).wait_send()
            self.beside(2, h, to_y).wait_send()


def mean_of(values):
    return jnp.mean(values, axis=-1, keepdims=True)


def scale_of(values):
    return lax.rsqrt(mean_of(values * values) + EPSILON)


def step_forward(target, start, alpha):
    target_scale = scale_of(target)
    unit = target * target_scale
    moved = start + alpha * (unit - start)
    moved_scale = scale_of(moved)
    return moved * moved_scale, unit, target_scale, moved_scale


def step_back(grad, result, unit, target_scale, moved_scale, start, alpha):
    moved_grad = moved_scale * (grad - result * mean_of(grad * result))
    unit_grad = alpha * moved_grad
    target_grad = target_scale * (unit_grad - unit * mean_of(unit_grad * unit))
    return target_grad, moved_grad - unit_grad, moved_grad * (unit - start)


CHUNK = 128
SCALE_ROWS = 16


def mlp_kernel(
    length, branch, tokens, alpha_attn, alpha_mlp, cotangent, far_weights, own_down,
    mixed, branch_low, token_grad, alpha_grads, weight_grads, scale_grads,
    hidden, hidden_grad, held, grads, ups, gates, inner, up_low, gate_low, own, cross, side,
    gather_send, gather_receive, cross_sem, side_sem, down, up_gate, load_sem,
    down_send, down_receive, down_local,
):
    x, z, y, c = here("x", "z", "y", "c")
    rows, width = branch.shape
    owners, units = length, own_down.shape[0]
    full = owners * units
    q0 = x * 2 + y
    load = pltpu.make_async_copy(far_weights, up_gate, load_sem)
    load.start()
    greet(plane_neighbours() + [(z > 0, {"z": z - 1}), (z < length - 1, {"z": z + 1})])
    line = LineGather(length, own_down, down, down_send, down_receive, down_local)
    line.start()
    done = []

    def each_chunk(body, h):
        def step(i, carry):
            start = pl.multiple_of(i * CHUNK, CHUNK)
            body(pl.ds(start, CHUNK), pl.ds(pl.multiple_of(c * rows + start, CHUNK), CHUNK))
            return carry

        chunks = rows // CHUNK // 2
        lax.fori_loop(h * chunks, (h + 1) * chunks, step, 0)

    def each_half(body):
        body(pl.ds(0, 2 * rows))

    def weight(i):
        return up_gate[:, i, :units].reshape(full, width)

    def scale(i):
        rows_of = [up_gate[k, i, units : units + SCALE_ROWS, :units].astype(f32)[:1] for k in range(length)]
        return jnp.concatenate(rows_of, axis=1)

    def down_weight():
        return down[...].reshape(full, width)

    def half_rows(half):
        return pl.ds(pl.multiple_of(half * rows, rows), rows)

    alpha_grads[...] = jnp.zeros_like(alpha_grads)
    scale_grads[...] = jnp.zeros_like(scale_grads)

    def enter(part, place):
        result = step_forward(branch[part], tokens[part].astype(f32), alpha_attn[...])[0]
        hidden[part] = result
        held[q0, place] = result.astype(bf16)

    scales = []

    def forward(q):
        if not scales:
            load.wait()
            scales.extend((scale(0), scale(1)))
        up_scale, gate_scale = scales

        def half(part):
            block = held[q, part]
            up = dot(block, weight(0), 1, 1)
            gate = dot(block, weight(1), 1, 1)
            ups[q, part] = up
            gates[q, part] = gate
            gated = gate * gate_scale
            inner[q, part] = (up * up_scale * (gated * jax.nn.sigmoid(gated))).astype(bf16)

        each_half(half)
        done.append(q)
        if len(done) in (1, 3):
            line.wait(len(done) // 2 + 1)
            line.hand_on(len(done) // 2 + 1)

    def forward_end():
        for d in range(3, length):
            line.wait(d)
            line.hand_on(d)
        for d in range(length - 1):
            line.sent(d)

    out = PlaneScatter(
        lambda q, half: dot(inner[q, half_rows(half)], down_weight(), 1, 0),
        own, cross, side, cross_sem.at[0], side_sem.at[0],
    )

    def forward_corner():
        forward_end()
        out.begin()

    plane_gather(
        held, gather_send.at[0], gather_receive.at[0], lambda h: each_chunk(enter, h), forward, forward_corner
    )
    out.end()

    def turn_back(part, place):
        start, alpha = hidden[part], alpha_mlp[...]
        result, unit, target_scale, moved_scale = step_forward(own[q0, part], start, alpha)
        mixed[part] = result.astype(bf16)
        target_grad, start_grad, alpha_part = step_back(
            cotangent[part].astype(f32), result, unit, target_scale, moved_scale, start, alpha
        )
        alpha_grads[1:2] += jnp.sum(alpha_part, axis=0, keepdims=True)
        hidden_grad[part] = start_grad
        grads[q0, place] = target_grad.astype(bf16)

    def backward(q):
        up_scale, gate_scale = scales

        def half(part):
            inner_grad = dot(grads[q, part], down_weight(), 1, 1)
            up, gate = ups[q, part], gates[q, part]
            gated = gate * gate_scale
            share = jax.nn.sigmoid(gated)
            silu = gated * share
            lifted = inner_grad * up
            gated_grad = lifted * up_scale * (share * (1.0 + gated * (1.0 - share)))
            up_low[q, part] = (inner_grad * up_scale * silu).astype(bf16)
            gate_low[q, part] = (gated_grad * gate_scale).astype(bf16)
            scale_grads[0:1] += jnp.sum(lifted * silu, axis=0, keepdims=True)
            scale_grads[1:2] += jnp.sum(gated_grad * gate, axis=0, keepdims=True)

        each_half(half)

    def weights_back():
        tall = 4 * 2 * rows
        for i, (left, right) in enumerate(((up_low, held), (gate_low, held), (inner, grads))):

            def step(n, carry):
                columns = pl.ds(pl.multiple_of(n * BLOCK, BLOCK), BLOCK)
                product = dot(
                    left[...].reshape(tall, full), right[:, :, columns].reshape(tall, BLOCK), 0, 0
                )
                weight_grads[:, i, :, columns] = product.astype(bf16).reshape(owners, units, BLOCK)
                return carry

            lax.fori_loop(0, width // BLOCK, step, 0)

    back = PlaneScatter(
        lambda q, half: dot(up_low[q, half_rows(half)], weight(0), 1, 0)
        + dot(gate_low[q, half_rows(half)], weight(1), 1, 0),
        own, cross, side, cross_sem.at[1], side_sem.at[1],
    )
    plane_gather(
        grads, gather_send.at[1], gather_receive.at[1], lambda h: each_chunk(turn_back, h), backward, back.begin
    )
    back.end(weights_back)

    def leave(part, place):
        start, alpha = tokens[part].astype(f32), alpha_attn[...]
        result, unit, target_scale, moved_scale = step_forward(branch[part], start, alpha)
        target_grad, start_grad, alpha_part = step_back(
            hidden_grad[part] + own[q0, part], result, unit, target_scale, moved_scale, start, alpha
        )
        alpha_grads[0:1] += jnp.sum(alpha_part, axis=0, keepdims=True)
        branch_low[part] = target_grad.astype(bf16)
        token_grad[part] = start_grad

    for h in (0, 1):
        each_chunk(leave, h)


def mlp(length, branch, tokens, alpha_attn, alpha_mlp, cotangent, up_gate, down):
    rows, width = branch.shape
    owners, units = length, down.shape[0]
    full = owners * units
    low, wide = like((rows, width), bf16), like((rows, width), f32)
    scratch = [
        pltpu.VMEM((rows, width), f32),
        pltpu.VMEM((rows, width), f32),
        pltpu.VMEM((4, 2 * rows, width), bf16),
        pltpu.VMEM((4, 2 * rows, width), bf16),
        pltpu.VMEM((4, 2 * rows, full), f32),
        pltpu.VMEM((4, 2 * rows, full), f32),
        pltpu.VMEM((4, 2 * rows, full), bf16),
        pltpu.VMEM((4, 2 * rows, full), bf16),
        pltpu.VMEM((4, 2 * rows, full), bf16),
        pltpu.VMEM((4, rows, width), f32),
        pltpu.VMEM((2, 4, rows, width), bf16),
        pltpu.VMEM((2, 3, rows, width), bf16),
        pltpu.SemaphoreType.DMA((2, 3, 8)),
        pltpu.SemaphoreType.DMA((2, 16)),
        pltpu.SemaphoreType.DMA((2, 2, 4)),
        pltpu.SemaphoreType.DMA((2, 2, 3, 2)),
        pltpu.VMEM((length, *down.shape), bf16),
        pltpu.VMEM(up_gate.shape, bf16),
        pltpu.SemaphoreType.DMA,
    ] + line_gather_semaphores(length)
    return remote_call(
        functools.partial(mlp_kernel, length), "mlp", 5,
        (low, low, wide, like((2, width), f32), like((owners, 3, units, width), bf16), like((2, full), f32)),
        (IN_VMEM,) * 6, [IN_VMEM] * 5 + [ANYWHERE, IN_VMEM], scratch,
        branch, tokens, alpha_attn, alpha_mlp, cotangent, up_gate, down,
    )


def shards(
    tokens, lengths, w_query, w_key, w_value, s_qk, w_out, up_weight, gate_weight, down_weight,
    s_up, s_gate, alpha_attn, alpha_mlp, cotangent,
):
    outer = lax.axis_size("o")
    own_units = up_weight.shape[0]
    if outer > 1:
        up_weight, gate_weight, down_weight, s_up, s_gate = (
            gather(a, "o") for a in (up_weight, gate_weight, down_weight, s_up, s_gate)
        )
    units = up_weight.shape[0]
    scales = jnp.zeros((2, SCALE_ROWS, up_weight.shape[1]), bf16)
    scales = scales.at[:, 0, :units].set(jnp.stack([s_up, s_gate]))
    up_gate = jnp.concatenate([jnp.stack([up_weight, gate_weight]), scales], axis=1)

    length = lax.axis_size("z")
    projections = w_query.T, w_key.T, w_value.T
    group_tokens, turned_q, turned_k, cosine, sine, qt, kt, vt, up_gate, branch, ot, lse = attention(
        length, lengths, tokens, *projections, s_qk[None], w_out, up_gate
    )
    mixed, branch_low, token_grad, alpha_grads, mlp_grads, scale_grads = mlp(
        length, branch, tokens, alpha_attn[None], alpha_mlp[None], cotangent, up_gate, down_weight,
    )
    tokens_grad, attn_grads, alpha_sums, scale_sums, gain_grad, mlp_grads = back(
        length, lengths, branch_low, w_out, qt, kt, vt, ot, lse, mlp_grads, turned_q, turned_k, s_qk[None],
        cosine, sine, *projections, alpha_grads, scale_grads, token_grad, group_tokens,
    )
    if outer > 1:
        mlp_grads = lax.psum_scatter(mlp_grads, "o", scatter_dimension=1, tiled=True)
        attn_grads, alpha_sums, scale_sums, gain_grad = lax.psum(
            (attn_grads, alpha_sums, scale_sums, gain_grad), "o"
        )
    place = lax.axis_index("z") * units + lax.axis_index("o") * own_units
    scale_sums = lax.dynamic_slice_in_dim(scale_sums, place, own_units, 1)
    return (
        mixed,
        tokens_grad,
        attn_grads[:HEAD_DIM].T,
        attn_grads[HEAD_DIM : 2 * HEAD_DIM].T,
        attn_grads[2 * HEAD_DIM : 3 * HEAD_DIM].T,
        gain_grad[0],
        attn_grads[3 * HEAD_DIM :],
        mlp_grads[0],
        mlp_grads[1],
        mlp_grads[2],
        scale_sums[0],
        scale_sums[1],
        alpha_sums[0],
        alpha_sums[1],
    )


def solution(mesh):
    dp, head = mesh.shape["dp"], mesh.shape["head"]
    fine = Mesh(mesh.devices.reshape(dp // 2, 2, head // 4, 2, 2), AXES)
    group, rows, heads = P(("o", "x"), None), P(AXES, None), P(None, GROUP)
    in_specs = (
        rows, group, heads, heads, heads, P(GROUP), P(GROUP, None), rows, rows, rows,
        P(AXES), P(AXES), P(), P(), rows,
    )
    out_specs = (
        rows, rows, heads, heads, heads, P(GROUP), P(GROUP, None), rows, rows, rows,
        P(AXES), P(AXES), P(), P(),
    )
    return jax.shard_map(
        shards, mesh=fine, in_specs=in_specs, out_specs=out_specs, check_vma=False
    )
```
